256 devices in a mesh: ctx: 32 (over x, z), head: 2 (over y_hi), dp: 4 (over y_lo, core).
Axes of the slice: x: 4, y: 4 (y_hi: 2, y_lo: 2; y = y_hi * 2 + y_lo), z: 8, core: 2. Of those that a mesh axis runs over, the one named last changes fastest.
Arguments:
- tokens: bfloat16 [4, 4096, 8192], P('dp', 'ctx', 'head'), may hold values from -6 to 6
- queries: bfloat16 [4, 4096, 4096], P('dp', 'ctx', 'head'), may hold values from -120 to 120
- out_grad: bfloat16 [4, 4096, 4096], P('dp', 'ctx', 'head'), may hold values from -6 to 6
- key_weight: bfloat16 [8192, 512], P(None, 'head'), may hold values from -0.0625 to 0.0625
- value_weight: bfloat16 [8192, 512], P(None, 'head'), may hold values from -0.0625 to 0.0625
- noise_codes: int32 [2, 4, 4096, 512], P(None, 'dp', 'ctx', 'head'), may hold values from 0 to 15
- clip_masks: int32 [2, 4, 4096, 512], P(None, 'dp', 'ctx', 'head'), may hold values 0 or 1
- block_order: int32 [32], replicated, may hold values from 0 to 31, each once
Outputs:
- query_grad: bfloat16 [4, 4096, 4096], P('dp', 'ctx', 'head')
- key_weight_grad: float32 [8192, 512], P('ctx', 'head')
- value_weight_grad: float32 [8192, 512], P('ctx', 'head')
The draws below stay inside these ranges and needn't reach their ends.
Inputs may be any that keep to these rules, and one draw needn't show every extreme that they name: `block_order`: each block place appears once.
All inputs are finite; a program needn't handle non-finite values. No bound on the sum of `clip_masks` on one device may be relied on, other than what follows from the above.
Results may differ from the reference program's by a relative error of at most 0.029.
The reference program's roundings to bfloat16 on the way (of `keys`, `values`, `score_grad`, `probs_low`, `key_pre` and `value_pre`) count: a program that leaves them out, or rounds other values in their place, can miss the bound.
Values may be sent and summed in bfloat16 or wider, within the bound.
A program may use at most 128 MiB of HBM per device.

```python
import math
import jax
import jax.numpy as jnp
from jax import lax

D = 8192
HD = 128
QH = 32
KVH = 4
TOK_DEV = 128
GROUP = 8
TOKENS = 4096
SEQS = 4
BLOCKS = 32
N_DP = 4


def draw_queries(key, part):
    key = jax.random.fold_in(key, 11)
    first, second = jax.random.split(key, 2)
    full_shape = (SEQS, TOKENS, QH, HD)
    scale_shape = (SEQS, TOKENS, QH, 1)
    base = jax.random.truncated_normal(first, -4.0, 4.0, full_shape, jnp.float32)
    scales = jnp.exp(jax.random.uniform(second, scale_shape, jnp.float32, math.log(0.5), math.log(5.0)))
    return (base * scales).reshape(SEQS, TOKENS, QH * HD).astype(jnp.bfloat16)


def set_ends(array, key, smallest, high):
    spot = [jax.random.randint(jax.random.fold_in(key, axis), (), 0, length) for axis, length in enumerate(array.shape)]
    widest = array.shape.index(max(array.shape))
    beside = spot[:widest] + [(spot[widest] + 1) % array.shape[widest]] + spot[widest + 1:]
    return array.at[tuple(spot)].set(smallest).at[tuple(beside)].set(high)


def raised(result, stream_key, source, target, shards_of, factor):
    def block_of(position):
        return (jnp.arange(result.shape[position]) // (result.shape[position] // shards_of)).reshape((-1,) + (1,) * (result.ndim - 1 - position))

    first = jax.random.permutation(stream_key, shards_of)[block_of(target)]
    other_side = (block_of(target) + shards_of // 2) % shards_of
    return jnp.where((block_of(source) == first) | (block_of(source) == other_side), factor * result, result)


def shard_levels(stream_key, extent, cuts, least, largest):
    def one(axis_at, shards_of):
        heights = jax.random.uniform(jax.random.fold_in(jax.random.fold_in(stream_key, 6), axis_at), (shards_of,), jnp.float32, least / len(cuts), largest / len(cuts))
        return jnp.repeat(jnp.exp(heights), extent[axis_at] // shards_of).reshape((-1,) + (1,) * (len(extent) - axis_at - 1))

    factor_of = one(*cuts[0])
    for cut in cuts[1:]:
        factor_of = factor_of * one(*cut)
    return factor_of


def noise(rng, extent, width, bound, cuts=(), kind=jnp.bfloat16):
    gain = shard_levels(rng, extent, cuts, -0.22, 0.18) if cuts else 1.0
    drawn = jax.random.normal(rng, extent, jnp.float32) * width * gain
    return jnp.minimum(jnp.maximum(drawn, -bound), bound).astype(kind)


def noise_with(key, extent, spread, most, cuts, heavy, kind=jnp.bfloat16):
    drawn = spread * jax.random.normal(key, extent, jnp.float32)
    if cuts:
        drawn = drawn * shard_levels(key, extent, cuts, -0.22, 0.18)
    return jnp.clip(raised(drawn, jax.random.fold_in(key, 3), *heavy), -most, most).astype(kind)


def setup_inputs(seed: int = 0) -> dict:
    key_list = jax.random.split(jax.random.key(seed), 9)
    return {
        "tokens": noise_with(key_list[0], (SEQS, TOKENS, D), 1.0, 6.0, ((0, 4), (1, 32), (2, 2)), (1, 2, 32, 2.75)),
        "queries": draw_queries(jax.random.fold_in(key_list[8], 71), 0),
        "out_grad": noise(key_list[2], (SEQS, TOKENS, QH * HD), 1.0, 6.0, ((0, 4), (1, 32), (2, 2))),
        "key_weight": noise(key_list[3], (D, KVH * HD), D ** -0.5, 0.0625, ((1, 2),)),
        "value_weight": noise(key_list[4], (D, KVH * HD), D ** -0.5, 0.0625, ((1, 2),)),
        "noise_codes": set_ends(jax.random.randint(key_list[5], (2, SEQS, TOKENS, KVH * HD), 0, 16), jax.random.fold_in(key_list[5], 1), 0, 15).astype(jnp.int32),
        "clip_masks": set_ends((jax.random.randint(key_list[6], (2, SEQS, TOKENS, KVH * HD), 0, 8) < 7).astype(jnp.int32), jax.random.fold_in(key_list[6], 1), 0, 1),
        "block_order": jax.random.permutation(key_list[7], BLOCKS).astype(jnp.int32),
    }


NOISE_STEP = 0.05
NOISE_MIDDLE = 7.5

def project(features, weight, codes):
    before = jnp.dot(features, weight, preferred_element_type=jnp.float32)
    return (before + NOISE_STEP * (codes.astype(jnp.float32) - NOISE_MIDDLE)).astype(jnp.bfloat16)

def reference(tokens, queries, out_grad, key_weight, value_weight, noise_codes, clip_masks, block_order):
    score_scale = 1.0 / math.sqrt(HD)
    token_rows = jnp.arange(TOKENS, dtype=jnp.int32)
    places = block_order[token_rows // TOK_DEV] * TOK_DEV + token_rows % TOK_DEV
    visible = places[:, None] >= places[None, :]
    contract = (((0,), (0,)), ((), ()))

    def head_grads(query_part, grad_part, key_part, value_part):
        scores = jnp.dot(query_part, key_part.T, preferred_element_type=jnp.float32) * score_scale
        scores = jnp.where(visible, scores, -jnp.inf)
        row_max = lax.optimization_barrier(jnp.max(scores, axis=1, keepdims=True))
        log_total = row_max + jnp.log(lax.optimization_barrier(jnp.sum(jnp.exp(scores - row_max), axis=1, keepdims=True)))
        probs = jnp.exp(scores - log_total)
        prob_grad = jnp.dot(grad_part, value_part.T, preferred_element_type=jnp.float32)
        deltas = lax.optimization_barrier(jnp.sum(probs * prob_grad, axis=1, keepdims=True))
        score_grad = (probs * (prob_grad - deltas)).astype(jnp.bfloat16)
        probs_low = probs.astype(jnp.bfloat16)
        query_grad = jnp.dot(score_grad, key_part, preferred_element_type=jnp.float32) * score_scale
        key_grad = jnp.dot(score_grad.T, query_part, preferred_element_type=jnp.float32) * score_scale
        value_grad = jnp.dot(probs_low.T, grad_part, preferred_element_type=jnp.float32)
        return (query_grad.astype(jnp.bfloat16), key_grad, value_grad)

    def one_sequence(sequence):
        features = tokens[sequence]
        keys = project(features, key_weight, noise_codes[0, sequence])
        values = project(features, value_weight, noise_codes[1, sequence])
        query_heads = queries[sequence].reshape(TOKENS, QH, HD).transpose(1, 0, 2)
        grad_heads = out_grad[sequence].reshape(TOKENS, QH, HD).transpose(1, 0, 2)
        key_heads = keys.reshape(TOKENS, KVH, HD).transpose(1, 0, 2)
        value_heads = values.reshape(TOKENS, KVH, HD).transpose(1, 0, 2)

        def one_head(head_index):
            kv_index = head_index // GROUP
            return head_grads(query_heads[head_index], grad_heads[head_index], key_heads[kv_index], value_heads[kv_index])
        query_grad, key_grad, value_grad = lax.map(one_head, jnp.arange(QH, dtype=jnp.int32))
        query_out = query_grad.transpose(1, 0, 2).reshape(TOKENS, QH * HD)
        key_sum = key_grad.reshape(KVH, GROUP, TOKENS, HD).sum(axis=1).transpose(1, 0, 2).reshape(TOKENS, KVH * HD)
        value_sum = value_grad.reshape(KVH, GROUP, TOKENS, HD).sum(axis=1).transpose(1, 0, 2).reshape(TOKENS, KVH * HD)
        key_pre = (key_sum * clip_masks[0, sequence].astype(jnp.float32)).astype(jnp.bfloat16)
        value_pre = (value_sum * clip_masks[1, sequence].astype(jnp.float32)).astype(jnp.bfloat16)
        key_part = lax.dot_general(features, key_pre, contract, preferred_element_type=jnp.float32)
        value_part = lax.dot_general(features, value_pre, contract, preferred_element_type=jnp.float32)
        return (query_out, key_part, value_part)
    query_all, key_parts, value_parts = lax.map(one_sequence, jnp.arange(SEQS, dtype=jnp.int32))
    return (query_all, lax.optimization_barrier(jnp.sum(key_parts, axis=0)) / N_DP, lax.optimization_barrier(jnp.sum(value_parts, axis=0)) / N_DP)
```

```python
import functools
import math

import jax
import jax.numpy as jnp
from jax import lax
from jax.experimental import pallas as pl
from jax.experimental.pallas import tpu as pltpu
from jax.sharding import PartitionSpec as P

HD = 128
BLK = 128
NX, NY, NZ, NC = 4, 4, 8, 2
GROUP_COLS = 512
HALF_D = 4096
QUARTER = 1024
KV_W = 256
BLOCKS = 32
NOISE_STEP = 0.05
NOISE_MIDDLE = 7.5
SCALE = 1.0 / math.sqrt(HD)
SCALE_LOG2 = SCALE * math.log2(math.e)
FLOOR_SCORE = -1e30
BF = jnp.bfloat16
F32 = jnp.float32
MESH = pl.DeviceIdType.MESH
NT = (((1,), (1,)), ((), ()))
NN = (((1,), (0,)), ((), ()))
TN = (((0,), (0,)), ((), ()))


def here():
    ctx, head, dp = lax.axis_index("ctx"), lax.axis_index("head"), lax.axis_index("dp")
    return ctx // NZ, head * 2 + dp // 2, lax.rem(ctx, NZ), lax.rem(dp, 2)


def device(x, y, z, core):
    return {"ctx": x * NZ + z, "head": y // 2, "dp": lax.rem(y, 2) * 2 + core}


def around(value, count):
    return lax.rem(value + count, count)


def signal(target):
    pl.semaphore_signal(pltpu.get_barrier_semaphore(), inc=1, device_id=target, device_id_type=MESH)


def remote(src, dst, send_sem, recv_sem, target):
    return pltpu.make_async_remote_copy(
        src_ref=src, dst_ref=dst, send_sem=send_sem, recv_sem=recv_sem, device_id=target, device_id_type=MESH
    )


def wait_bytes(ref, sem):
    pltpu.make_async_copy(ref, ref, sem).wait()


def send_or_copy(is_self, src, dst, send_sem, recv_sem, target):
    @pl.when(is_self)
    def _():
        pltpu.make_async_copy(src, dst, recv_sem).start()

    @pl.when(jnp.logical_not(is_self))
    def _():
        remote(src, dst, send_sem, recv_sem, target).start()


def wait_sent(is_self, ref, send_sem):
    @pl.when(jnp.logical_not(is_self))
    def _():
        wait_bytes(ref, send_sem)


ROW_CHUNKS = 4
CHUNK = BLK // ROW_CHUNKS


def front_kernel(
    tok, q, do, kw, vw, codes, qx, dox, kv,
    xbuf, wbuf, acc, kvst,
    w_sem, own_sem, tok_send, tok_recv, q_send, q_recv, kv_send, kv_send0, kv_recv, fw_send, fw_recv,
):
    X, Y, Z, C = here()
    head = Y // 2
    unit_core = X // 2
    same = unit_core == C
    peer = device(X, around(Y + 2, NY), Z, C)
    partner = device(X, Y, Z, 1 - C)

    loads = []
    for half in range(2):
        rows = pl.ds(half * HALF_D, HALF_D)
        loads.append(pltpu.make_async_copy(kw.at[rows, :], wbuf.at[half, :, pl.ds(0, KV_W)], w_sem.at[half, 0]))
        loads.append(pltpu.make_async_copy(vw.at[rows, :], wbuf.at[half, :, pl.ds(KV_W, KV_W)], w_sem.at[half, 1]))
    own_x = pltpu.make_async_copy(tok.at[0], xbuf.at[head], own_sem)
    own_x.start()
    for load in loads:
        load.start()

    signal(peer)
    signal(partner)
    for xs in range(NX):
        @pl.when(jnp.logical_not(jnp.logical_and(same, X == xs)))
        def _(xs=xs):
            signal(device(xs, Y, Z, unit_core))
    for part in range(2):
        signal_x = 2 * C + part

        @pl.when(jnp.logical_not(jnp.logical_and(same, X == signal_x)))
        def _(signal_x=signal_x):
            signal(device(signal_x, Y, Z, unit_core))

        def far(step, carry, signal_x=signal_x):
            signal(device(signal_x, Y, around(Z + step, NZ), unit_core))
            return carry

        lax.fori_loop(1, NZ, far, 0)
    pl.semaphore_wait(pltpu.get_barrier_semaphore(), 22 - 2 * same.astype(jnp.int32))

    for r in range(ROW_CHUNKS):
        rows = pl.ds(r * CHUNK, CHUNK)
        remote(tok.at[0, rows, :], xbuf.at[head, rows, :], tok_send.at[r], tok_recv.at[r], peer).start()
    for j in range(2):
        for c2 in range(NC):
            cols = pl.ds((j * 8 + c2 * 4) * HD, GROUP_COLS)
            target = device(2 * C + j, Y, Z, c2)
            is_self = jnp.logical_and(2 * C + j == X, C == c2)
            send_or_copy(is_self, q.at[0, :, cols], qx.at[X], q_send.at[0, j, c2], q_recv.at[0], target)
            send_or_copy(is_self, do.at[0, :, cols], dox.at[X], q_send.at[1, j, c2], q_recv.at[1], target)

    own_x.wait()
    for load in loads:
        load.wait()
    acc[...] = jnp.dot(xbuf[head], wbuf[head], preferred_element_type=F32)

    mine = X * NZ + Z

    def forward(r):
        rows = pl.ds(r * CHUNK, CHUNK)
        blocks = kv.at[pl.ds(C * 16, 16), rows, :]
        wait_bytes(blocks, kv_recv.at[r])
        copy = remote(blocks, blocks, fw_send.at[r], fw_recv.at[r], partner)
        copy.start()

    for r in range(ROW_CHUNKS):
        rows = pl.ds(r * CHUNK, CHUNK)
        wait_bytes(xbuf.at[1 - head, rows, :], tok_recv.at[r])
        both = acc[rows, :] + jnp.dot(xbuf[1 - head, rows, :], wbuf[1 - head], preferred_element_type=F32)
        for what in range(2):
            shift = NOISE_STEP * (codes[what, 0, rows, :].astype(F32) - NOISE_MIDDLE)
            value = (both[:, what * KV_W : (what + 1) * KV_W] + shift).astype(BF)
            for j in range(2):
                kvst[j, rows, what * HD : (what + 1) * HD] = value[:, j * HD : (j + 1) * HD]
        for j in range(2):
            src = kvst.at[j, rows, :]
            dst = kv.at[mine, rows, :]
            is_self = jnp.logical_and(same, 2 * C + j == X)
            send_or_copy(is_self, src, dst, kv_send0.at[r, j], kv_recv.at[r], device(2 * C + j, Y, Z, unit_core))

            def far(step, carry, j=j, r=r, src=src, dst=dst):
                target = device(2 * C + j, Y, around(Z + step, NZ), unit_core)
                remote(src, dst, kv_send.at[r, j], kv_recv.at[r], target).start()
                return carry

            lax.fori_loop(1, NZ, far, 0)
        if r:
            forward(r - 1)
    forward(ROW_CHUNKS - 1)

    for r in range(ROW_CHUNKS):
        rows = pl.ds(r * CHUNK, CHUNK)
        wait_bytes(kv.at[pl.ds((1 - C) * 16, 16), rows, :], fw_recv.at[r])
        wait_bytes(kv.at[pl.ds(C * 16, 16), rows, :], fw_send.at[r])
        wait_bytes(xbuf.at[head, rows, :], tok_send.at[r])
        for j in range(2):
            is_self = jnp.logical_and(same, 2 * C + j == X)
            wait_sent(is_self, kvst.at[j, rows, :], kv_send0.at[r, j])
            wait_bytes(kv.at[pl.ds(0, NZ - 1), rows, :], kv_send.at[r, j])
    wait_bytes(qx, q_recv.at[0])
    wait_bytes(dox, q_recv.at[1])
    for j in range(2):
        for c2 in range(NC):
            is_self = jnp.logical_and(2 * C + j == X, C == c2)
            wait_sent(is_self, qx.at[0], q_send.at[0, j, c2])
            wait_sent(is_self, dox.at[0], q_send.at[1, j, c2])


ANY_SPEC = pl.BlockSpec(memory_space=pl.ANY)
VMEM_SPEC = pl.BlockSpec(memory_space=pltpu.VMEM)
DMA = pltpu.SemaphoreType.DMA


def front(tokens, queries, out_grad, key_weight, value_weight, noise_codes):
    return pl.pallas_call(
        front_kernel,
        name="front",
        out_shape=(
            jax.ShapeDtypeStruct((NX, BLK, GROUP_COLS), BF),
            jax.ShapeDtypeStruct((NX, BLK, GROUP_COLS), BF),
            jax.ShapeDtypeStruct((BLOCKS, BLK, KV_W), BF),
        ),
        in_specs=[ANY_SPEC] * 5 + [VMEM_SPEC],
        out_specs=(ANY_SPEC,) * 3,
        scratch_shapes=[
            pltpu.VMEM((2, BLK, HALF_D), BF),
            pltpu.VMEM((2, HALF_D, 2 * KV_W), BF),
            pltpu.VMEM((BLK, 2 * KV_W), F32),
            pltpu.VMEM((2, BLK, KV_W), BF),
            DMA((2, 2)),
            DMA,
            DMA((ROW_CHUNKS,)),
            DMA((ROW_CHUNKS,)),
            DMA((2, 2, 2)),
            DMA((2,)),
            DMA((ROW_CHUNKS, 2)),
            DMA((ROW_CHUNKS, 2)),
            DMA((ROW_CHUNKS,)),
            DMA((ROW_CHUNKS,)),
            DMA((ROW_CHUNKS,)),
        ],
        compiler_params=pltpu.CompilerParams(
            collective_id=0, has_side_effects=True, vmem_limit_bytes=40 * 2**20
        ),
        cost_estimate=pl.CostEstimate(flops=10**9, bytes_accessed=16 * 2**20, transcendentals=0),
    )(tokens, queries, out_grad, key_weight, value_weight, noise_codes)


KEYS = 256
LEVELS = (4, 2, 1)
ROWS = 4 * BLK


def attention_kernel(
    order, q, do, kv, dq_out, dkv_out,
    kvb, qs, dos, stb, dpb, dk, dv, dqt, dkvb, kv_sem, q_sem, do_sem, out_sem,
):
    Z = lax.rem(lax.axis_index("ctx"), NZ)

    def at_place(block):
        return pl.ds(pl.multiple_of(order[block] * BLK, BLK), BLK)

    def load(block, carry):
        pltpu.make_async_copy(kv.at[block], kvb.at[at_place(block), :], kv_sem).start()
        return carry

    for x in range(NX):
        for h in range(4):
            cols, rows = pl.ds(h * HD, HD), pl.ds(h * BLK, BLK)
            pltpu.make_async_copy(q.at[x, :, cols], qs.at[x, rows, :], q_sem).start()
            pltpu.make_async_copy(do.at[x, :, cols], dos.at[x, rows, :], do_sem).start()
    lax.fori_loop(0, BLOCKS, load, 0)

    def clear(i, carry):
        rows = pl.ds(pl.multiple_of(i * 256, 256), 256)
        dk[rows, :] = jnp.zeros((256, HD), F32)
        dv[rows, :] = jnp.zeros((256, HD), F32)
        return carry

    lax.fori_loop(0, 16, clear, 0)
    wait_bytes(qs, q_sem)
    wait_bytes(dos, do_sem)
    wait_bytes(kvb, kv_sem)

    def run(count, body, carry):
        done = 0
        for units in LEVELS:
            times = (count - done) // units
            base = done

            def step(i, state, units=units, base=base):
                start = pl.multiple_of((base + i * units) * KEYS, KEYS)
                return body(pl.ds(start, units * KEYS), units * KEYS, state)

            carry = lax.fori_loop(0, times, step, carry)
            done = base + times * units
        return carry

    def fold(array, size, how):
        return how(array.reshape(size // 8, 8, ROWS), axis=0)

    def tile(x, carry):
        place = order[x * NZ + Z]
        last = place // 2
        qx = qs[x]
        dx = dos[x]

        def score_step(rows, size, top):
            st = lax.dot_general(kvb[rows, :HD], qx, NT, preferred_element_type=F32)
            stb[rows, :] = st
            return jnp.maximum(top, fold(st, size, jnp.max))

        top = run(last, score_step, jnp.full((8, ROWS), FLOOR_SCORE, F32))
        rows = pl.ds(pl.multiple_of(last * KEYS, KEYS), KEYS)
        st = lax.dot_general(kvb[rows, :HD], qx, NT, preferred_element_type=F32)
        key_places = last * KEYS + lax.broadcasted_iota(jnp.int32, (KEYS, ROWS), 0)
        query_places = place * BLK + lax.rem(lax.broadcasted_iota(jnp.int32, (KEYS, ROWS), 1), BLK)
        st = jnp.where(key_places <= query_places, st, FLOOR_SCORE)
        stb[rows, :] = st
        top = jnp.maximum(top, fold(st, KEYS, jnp.max))
        top = jnp.max(top, axis=0, keepdims=True) * SCALE_LOG2

        def weigh_step(rows, size, state):
            total, weighted = state
            weights = jnp.exp2(stb[rows, :] * SCALE_LOG2 - top)
            dpt = lax.dot_general(kvb[rows, HD:], dx, NT, preferred_element_type=F32)
            dpb[rows, :] = dpt
            stb[rows, :] = weights
            return total + fold(weights, size, jnp.sum), weighted + fold(weights * dpt, size, jnp.sum)

        zero = jnp.zeros((8, ROWS), F32)
        total, weighted = run(last + 1, weigh_step, (zero, zero))
        inverse = 1.0 / jnp.sum(total, axis=0, keepdims=True)
        delta = jnp.sum(weighted, axis=0, keepdims=True) * inverse
        dqt[...] = jnp.zeros((HD, ROWS), F32)

        def grad_step(rows, size, state):
            probs = stb[rows, :] * inverse
            low = probs.astype(BF)
            grads = (probs * (dpb[rows, :] - delta)).astype(BF)
            dv[rows, :] += lax.dot_general(low, dx, NN, preferred_element_type=F32)
            dk[rows, :] += lax.dot_general(grads, qx, NN, preferred_element_type=F32)
            dqt[...] += lax.dot_general(kvb[rows, :HD], grads, TN, preferred_element_type=F32)
            return state

        run(last + 1, grad_step, 0)
        dq = dqt[...].T
        for h in range(4):
            dq_out[x, :, h * HD : (h + 1) * HD] = (dq[h * BLK : (h + 1) * BLK, :] * SCALE).astype(BF)
        return carry

    lax.fori_loop(0, NX, tile, 0)

    def finish(i, carry):
        rows = pl.ds(pl.multiple_of(i * 256, 256), 256)
        dkvb[rows, :HD] = (dk[rows, :] * SCALE).astype(BF)
        dkvb[rows, HD:] = dv[rows, :].astype(BF)
        return carry

    lax.fori_loop(0, 16, finish, 0)

    def store(block, carry):
        pltpu.make_async_copy(dkvb.at[at_place(block), :], dkv_out.at[block], out_sem).start()
        return carry

    lax.fori_loop(0, BLOCKS, store, 0)
    wait_bytes(dkvb, out_sem)


def attention(block_order, qx, dox, kv):
    tokens = BLOCKS * BLK
    return pl.pallas_call(
        attention_kernel,
        name="attention",
        out_shape=(
            jax.ShapeDtypeStruct((NX, BLK, GROUP_COLS), BF),
            jax.ShapeDtypeStruct((BLOCKS, BLK, KV_W), BF),
        ),
        in_specs=[pl.BlockSpec(memory_space=pltpu.SMEM)] + [ANY_SPEC] * 3,
        out_specs=(VMEM_SPEC, ANY_SPEC),
        scratch_shapes=[
            pltpu.VMEM((tokens, KV_W), BF),
            pltpu.VMEM((NX, ROWS, HD), BF),
            pltpu.VMEM((NX, ROWS, HD), BF),
            pltpu.VMEM((tokens, ROWS), F32),
            pltpu.VMEM((tokens, ROWS), F32),
            pltpu.VMEM((tokens, HD), F32),
            pltpu.VMEM((tokens, HD), F32),
            pltpu.VMEM((HD, ROWS), F32),
            pltpu.VMEM((tokens, KV_W), BF),
            DMA,
            DMA,
            DMA,
            DMA,
        ],
        compiler_params=pltpu.CompilerParams(vmem_limit_bytes=56 * 2**20),
        cost_estimate=pl.CostEstimate(flops=10**10, bytes_accessed=8 * 2**20, transcendentals=10**7),
    )(block_order, qx, dox, kv)


class Ring:
    def __init__(self, count, position, neighbour, own, slots, send_sems, recv_sems):
        self.count, self.position, self.neighbour, self.own = count, position, neighbour, own
        self.slots, self.send_sems, self.recv_sems = slots, send_sems, recv_sems
        self.steps = count // 2
        self.sent = []

    def chains(self, step):
        for way in range(2):
            for part in range(2):
                length = self.steps if way == part else self.steps - 1
                if step >= self.steps - length:
                    yield way, part, step == self.steps - length

    def step(self, step):
        for way, part, first in self.chains(step):
            sign = 1 if way == 0 else -1
            target = around(self.position + sign * (self.steps - step), self.count)
            mine = self.own(part, target)
            if first:
                src = mine
            else:
                src = self.slots.at[way, part, step - 1]
                wait_bytes(src, self.recv_sems.at[way, part, step - 1])
                src[...] = (src[...].astype(F32) + mine[...].astype(F32)).astype(BF)
            copy = remote(
                src,
                self.slots.at[way, part, step],
                self.send_sems.at[way, part, step],
                self.recv_sems.at[way, part, step],
                self.neighbour(sign),
            )
            copy.start()
            self.sent.append(copy)

    def result(self, part):
        total = self.own(part, self.position)[...].astype(F32)
        for way in range(2):
            slot = self.slots.at[way, part, self.steps - 1]
            wait_bytes(slot, self.recv_sems.at[way, part, self.steps - 1])
            total += slot[...].astype(F32)
        return total.astype(BF)

    def finish(self):
        for copy in self.sent:
            copy.wait_send()


def rows_at(ref, start, size):
    return ref.at[pl.ds(pl.multiple_of(start, 16), size), :]


def back_kernel(
    dq, dkv, tok, masks, query_grad, key_out, value_out,
    own, other, z1, home_src, raw, tokq, tokt, preall, wa, wb, az, ra, ax, fa, bx, rb, bz, fb, final,
    own_sem, ex_sem, z1_send, z1_recv, home_send, home_recv, tok_send, tok_recv, dq_send, dq_recv,
    pre_send, pre_recv, pfw_send, pfw_recv, core_sem,
    az_send, az_recv, ax_send, ax_recv, bx_send, bx_recv, bz_send, bz_recv, fin_send, fin_recv,
):
    X, Y, Z, C = here()
    head, low = Y // 2, lax.rem(Y, 2)
    unit_core = X // 2
    slot = lax.rem(X, 2)
    same = unit_core == C
    partner = device(X, Y, Z, 1 - C)
    seq = low * 2 + C

    load_own = pltpu.make_async_copy(dkv.at[pl.ds(C * 16, 16)], own, own_sem)
    load_own.start()

    def z_next(sign):
        return device(X, Y, around(Z + sign, NZ), C)

    def x_next(sign):
        return device(around(X + sign, NX), Y, Z, C)

    def y_next(by):
        return device(X, around(Y + by, NY), Z, C)

    ways = (1, 3, 2)
    own_final = jnp.logical_and(
        2 * head + low == X, jnp.where(head == 0, 4 * C + Z // 2 == Z, 4 * C + X == Z)
    )

    signal(partner)
    for xs in range(2):
        for cs in range(NC):
            @pl.when(jnp.logical_not(jnp.logical_and(2 * C + xs == X, C == cs)))
            def _(xs=xs, cs=cs):
                signal(device(2 * C + xs, Y, Z, cs))
    for sign in (1, -1):
        signal(z_next(sign))
        signal(x_next(sign))
    for cs in range(NC):
        signal(device(X, 2 * head + 1 - low, Z, cs))
    for by in ways:
        signal(y_next(by))
    for i in range(8):
        xs = (1 - head) * (i % 4) + head * lax.rem(Z, 4)
        zs = (1 - head) * (2 * lax.rem(Z, 4) + i // 4) + head * i
        ys, cs = X, Z // 4
        is_self = jnp.logical_and(jnp.logical_and(xs == X, zs == Z), jnp.logical_and(ys == Y, cs == C))

        @pl.when(jnp.logical_not(is_self))
        def _(xs=xs, ys=ys, zs=zs, cs=cs):
            signal(device(xs, ys, zs, cs))
    pl.semaphore_wait(
        pltpu.get_barrier_semaphore(), 22 - same.astype(jnp.int32) - own_final.astype(jnp.int32)
    )

    exchange = remote(dkv.at[pl.ds((1 - C) * 16, 16)], other, ex_sem.at[0], ex_sem.at[1], partner)
    exchange.start()
    for xs in range(NX):
        cols = pl.ds(pl.multiple_of((slot * 8 + C * 4) * HD, GROUP_COLS), GROUP_COLS)
        is_self = jnp.logical_and(same, X == xs)
        send_or_copy(
            is_self, dq.at[xs], query_grad.at[0, :, cols], dq_send.at[xs], dq_recv, device(xs, Y, Z, unit_core)
        )
    for quarter in range(4):
        is_self = seq == quarter
        send_or_copy(
            is_self,
            tok.at[0, :, pl.ds(quarter * QUARTER, QUARTER)],
            tokq.at[seq],
            tok_send.at[quarter],
            tok_recv,
            device(X, 2 * head + quarter // 2, Z, quarter % 2),
        )

    load_own.wait()
    exchange.wait_recv()

    def add(i, carry):
        own[i] = (own[i].astype(F32) + other[i].astype(F32)).astype(BF)
        return carry

    lax.fori_loop(0, 16, add, 0)
    ring = Ring(NZ, Z, z_next, lambda part, t: own.at[part * NZ + t], z1, z1_send, z1_recv)
    for step in range(ring.steps):
        ring.step(step)
    for part in range(2):
        home_src[part] = ring.result(part)
        xs = 2 * C + part
        is_self = jnp.logical_and(same, X == xs)
        send_or_copy(
            is_self,
            home_src.at[part],
            raw.at[slot],
            home_send.at[part],
            home_recv,
            device(xs, Y, Z, unit_core),
        )
    wait_bytes(tokq, tok_recv)
    for s in range(4):
        tokt[:, s * BLK : (s + 1) * BLK] = tokq[s].T

    wait_bytes(raw, home_recv)
    my_rows = pl.ds(pl.multiple_of(seq * BLK, BLK), BLK)
    for j in range(2):
        for what in range(2):
            mask = masks[what, 0, :, j * HD : (j + 1) * HD] != 0
            piece = raw[j, :, what * HD : (what + 1) * HD]
            first = (2 * j + what) * HD
            preall[head, my_rows, first : first + HD] = jnp.where(mask, piece, jnp.zeros_like(piece))
    mine = preall.at[head, my_rows, :]
    sends = [
        remote(mine, mine, pre_send.at[i], pre_recv.at[i], y_next(by)) for i, by in enumerate(ways)
    ] + [remote(mine, mine, core_sem.at[0], core_sem.at[1], partner)]
    for copy in sends:
        copy.start()

    def piece_of(by, core):
        ys = around(Y + NY - by, NY)
        start = (lax.rem(ys, 2) * 2 + core) * BLK
        return preall.at[ys // 2, pl.ds(pl.multiple_of(start, BLK), BLK), :]

    forwards = []
    for i, by in enumerate(ways):
        piece = piece_of(by, C)
        wait_bytes(piece, pre_recv.at[i])
        copy = remote(piece, piece, pfw_send.at[i], pfw_recv.at[i], partner)
        copy.start()
        forwards.append(copy)
    sends[3].wait_recv()
    for copy in forwards:
        copy.wait_recv()

    for which, out in ((0, wa), (1, wb)):
        def multiply(i, carry, which=which, out=out):
            rows = pl.ds(pl.multiple_of(i * 256, 256), 256)
            out[rows, :] = jnp.dot(tokt[rows, :], preall[which], preferred_element_type=F32).astype(BF)
            return carry

        lax.fori_loop(0, 4, multiply, 0)

    a_first = Ring(NZ, Z, z_next, lambda part, t: rows_at(wa, t * 128 + part * 64, 64), az, az_send, az_recv)
    b_first = Ring(NX, X, x_next, lambda part, t: rows_at(wb, t * 256 + part * 128, 128), bx, bx_send, bx_recv)
    a_next = Ring(NX, X, x_next, lambda part, t: rows_at(ra, t * 32 + part * 16, 16), ax, ax_send, ax_recv)
    b_next = Ring(NZ, Z, z_next, lambda part, t: rows_at(rb, t * 32 + part * 16, 16), bz, bz_send, bz_recv)
    a_first.step(0)
    b_first.step(0)
    a_first.step(1)
    b_first.step(1)
    a_first.step(2)
    for part in range(2):
        rb[part * 128 : (part + 1) * 128, :] = b_first.result(part)
    b_next.step(0)
    a_first.step(3)
    b_next.step(1)
    for part in range(2):
        ra[part * 64 : (part + 1) * 64, :] = a_first.result(part)
    a_next.step(0)
    b_next.step(2)
    a_next.step(1)
    b_next.step(3)
    for part in range(2):
        fa[part * 16 : (part + 1) * 16, :] = a_next.result(part)
    for part in range(2):
        fb[part * 16 : (part + 1) * 16, :] = b_next.result(part)

    a_rows = rows_at(final, lax.rem(Z, 2) * 128 + X * 32, 32)
    b_rows = rows_at(final, Z * 32, 32)
    final_sends = []
    for which, src, dst, zs in ((0, fa, a_rows, 4 * C + Z // 2), (1, fb, b_rows, 4 * C + X)):
        for low2 in range(2):
            for c2 in range(NC):
                target = device(2 * head + low, 2 * which + low2, zs, c2)
                is_self = jnp.logical_and(
                    own_final, jnp.logical_and(head == which, jnp.logical_and(low == low2, C == c2))
                )
                sem = fin_send.at[which, low2, c2]
                send_or_copy(is_self, src, dst, sem, fin_recv, target)
                final_sends.append((is_self, src, sem))
    wait_bytes(final, fin_recv)
    for j in range(2):
        for what, out in ((0, key_out), (1, value_out)):
            first = (2 * j + what) * HD
            out[:, j * HD : (j + 1) * HD] = final[:, first : first + HD].astype(F32) * 0.25

    wait_bytes(query_grad, dq_recv)
    exchange.wait_send()
    for xs in range(NX):
        wait_sent(jnp.logical_and(same, X == xs), dq.at[xs], dq_send.at[xs])
    for quarter in range(4):
        wait_sent(seq == quarter, tokq.at[0], tok_send.at[quarter])
    for part in range(2):
        wait_sent(jnp.logical_and(same, X == 2 * C + part), raw.at[part], home_send.at[part])
    for copy in sends + forwards:
        copy.wait_send()
    for each in (ring, a_first, b_first, a_next, b_next):
        each.finish()
    for is_self, src, sem in final_sends:
        wait_sent(is_self, src, sem)


def back(dq, dkv, tokens, clip_masks):
    def slots(steps, rows, cols):
        return pltpu.VMEM((2, 2, steps, rows, cols), BF)

    wide = 2 * KV_W
    return pl.pallas_call(
        back_kernel,
        name="back",
        out_shape=(
            jax.ShapeDtypeStruct((1, BLK, 2048), BF),
            jax.ShapeDtypeStruct((256, KV_W), F32),
            jax.ShapeDtypeStruct((256, KV_W), F32),
        ),
        in_specs=[ANY_SPEC] * 3 + [VMEM_SPEC],
        out_specs=(ANY_SPEC, VMEM_SPEC, VMEM_SPEC),
        scratch_shapes=[
            pltpu.VMEM((16, BLK, KV_W), BF),
            pltpu.VMEM((16, BLK, KV_W), BF),
            slots(4, BLK, KV_W),
            pltpu.VMEM((2, BLK, KV_W), BF),
            pltpu.VMEM((2, BLK, KV_W), BF),
            pltpu.VMEM((4, BLK, QUARTER), BF),
            pltpu.VMEM((QUARTER, 4 * BLK), BF),
            pltpu.VMEM((2, 4 * BLK, wide), BF),
            pltpu.VMEM((QUARTER, wide), BF),
            pltpu.VMEM((QUARTER, wide), BF),
            slots(4, 64, wide),
            pltpu.VMEM((128, wide), BF),
            slots(2, 16, wide),
            pltpu.VMEM((32, wide), BF),
            slots(2, 128, wide),
            pltpu.VMEM((256, wide), BF),
            slots(4, 16, wide),
            pltpu.VMEM((32, wide), BF),
            pltpu.VMEM((256, wide), BF),
            DMA,
            DMA((2,)),
            DMA((2, 2, 4)),
            DMA((2, 2, 4)),
            DMA((2,)),
            DMA,
            DMA((4,)),
            DMA,
            DMA((4,)),
            DMA,
            DMA((3,)),
            DMA((3,)),
            DMA((3,)),
            DMA((3,)),
            DMA((2,)),
            DMA((2, 2, 4)),
            DMA((2, 2, 4)),
            DMA((2, 2, 2)),
            DMA((2, 2, 2)),
            DMA((2, 2, 2)),
            DMA((2, 2, 2)),
            DMA((2, 2, 4)),
            DMA((2, 2, 4)),
            DMA((2, 2, 2)),
            DMA,
        ],
        compiler_params=pltpu.CompilerParams(
            collective_id=1, has_side_effects=True, vmem_limit_bytes=40 * 2**20
        ),
        cost_estimate=pl.CostEstimate(flops=10**9, bytes_accessed=16 * 2**20, transcendentals=0),
    )(dq, dkv, tokens, clip_masks)


def on_device(
    tokens, queries, out_grad, key_weight, value_weight, noise_codes, clip_masks, block_order
):
    qx, dox, kv = front(tokens, queries, out_grad, key_weight, value_weight, noise_codes)
    dq, dkv = attention(block_order, qx, dox, kv)
    return back(dq, dkv, tokens, clip_masks)


def solution(mesh):
    placed = (
        P("dp", "ctx", "head"),
        P("dp", "ctx", "head"),
        P("dp", "ctx", "head"),
        P(None, "head"),
        P(None, "head"),
        P(None, "dp", "ctx", "head"),
        P(None, "dp", "ctx", "head"),
        P(),
    )
    return jax.shard_map(
        on_device,
        mesh=mesh,
        in_specs=placed,
        out_specs=(P("dp", "ctx", "head"), P("ctx", "head"), P("ctx", "head")),
        check_vma=False,
    )
```

```python
import functools
import math

import jax
import jax.numpy as jnp
from jax import lax
from jax.experimental import pallas as pl
from jax.experimental.pallas import tpu as pltpu
from jax.sharding import PartitionSpec as P

HD = 128
BLK = 128
NX, NY, NZ, NC = 4, 4, 8, 2
GROUP_COLS = 512
HALF_D = 4096
QUARTER = 1024
KV_W = 256
BLOCKS = 32
NOISE_STEP = 0.05
NOISE_MIDDLE = 7.5
SCALE = 1.0 / math.sqrt(HD)
SCALE_LOG2 = SCALE * math.log2(math.e)
FLOOR_SCORE = -1e30
BF = jnp.bfloat16
F32 = jnp.float32
MESH = pl.DeviceIdType.MESH
VMEM_GRANT = 62 * 2**20
NT = (((1,), (1,)), ((), ()))
NN = (((1,), (0,)), ((), ()))
TN = (((0,), (0,)), ((), ()))


def here():
    ctx, head, dp = lax.axis_index("ctx"), lax.axis_index("head"), lax.axis_index("dp")
    return ctx // NZ, head * 2 + dp // 2, lax.rem(ctx, NZ), lax.rem(dp, 2)


def device(x, y, z, core):
    return {"ctx": x * NZ + z, "head": y // 2, "dp": lax.rem(y, 2) * 2 + core}


def around(value, count):
    return lax.rem(value + count, count)


def signal(target):
    pl.semaphore_signal(pltpu.get_barrier_semaphore(), inc=1, device_id=target, device_id_type=MESH)


def remote(src, dst, send_sem, recv_sem, target):
    return pltpu.make_async_remote_copy(
        src_ref=src, dst_ref=dst, send_sem=send_sem, recv_sem=recv_sem, device_id=target, device_id_type=MESH
    )


def wait_bytes(ref, sem):
    pltpu.make_async_copy(ref, ref, sem).wait()


def send_or_copy(is_self, src, dst, send_sem, recv_sem, target):
    @pl.when(is_self)
    def _():
        pltpu.make_async_copy(src, dst, recv_sem).start()

    @pl.when(jnp.logical_not(is_self))
    def _():
        remote(src, dst, send_sem, recv_sem, target).start()


def wait_sent(is_self, ref, send_sem):
    @pl.when(jnp.logical_not(is_self))
    def _():
        wait_bytes(ref, send_sem)


ROW_CHUNKS = 4
CHUNK = BLK // ROW_CHUNKS


def front_kernel(
    tok, q, do, kw, vw, codes_in, qx, dox, kv,
    codes, xbuf, wbuf, acc, kvst,
    codes_sem, w_sem, own_sem, tok_send, tok_recv, q_send, q_recv, kv_send, kv_send0, kv_recv, fw_send, fw_recv,
):
    X, Y, Z, C = here()
    head = Y // 2
    unit_core = X // 2
    same = unit_core == C
    peer = device(X, around(Y + 2, NY), Z, C)
    partner = device(X, Y, Z, 1 - C)

    loads = [pltpu.make_async_copy(codes_in, codes, codes_sem)]
    for half in range(2):
        rows = pl.ds(half * HALF_D, HALF_D)
        loads.append(pltpu.make_async_copy(kw.at[rows, :], wbuf.at[half, :, pl.ds(0, KV_W)], w_sem.at[half, 0]))
        loads.append(pltpu.make_async_copy(vw.at[rows, :], wbuf.at[half, :, pl.ds(KV_W, KV_W)], w_sem.at[half, 1]))
    own_x = pltpu.make_async_copy(tok.at[0], xbuf.at[head], own_sem)
    own_x.start()
    for load in loads:
        load.start()

    signal(peer)
    signal(partner)
    for xs in range(NX):
        @pl.when(jnp.logical_not(jnp.logical_and(same, X == xs)))
        def _(xs=xs):
            signal(device(xs, Y, Z, unit_core))
    for part in range(2):
        signal_x = 2 * C + part

        @pl.when(jnp.logical_not(jnp.logical_and(same, X == signal_x)))
        def _(signal_x=signal_x):
            signal(device(signal_x, Y, Z, unit_core))

        def far(step, carry, signal_x=signal_x):
            signal(device(signal_x, Y, around(Z + step, NZ), unit_core))
            return carry

        lax.fori_loop(1, NZ, far, 0)
    pl.semaphore_wait(pltpu.get_barrier_semaphore(), 22 - 2 * same.astype(jnp.int32))

    for r in range(ROW_CHUNKS):
        rows = pl.ds(r * CHUNK, CHUNK)
        remote(tok.at[0, rows, :], xbuf.at[head, rows, :], tok_send.at[r], tok_recv.at[r], peer).start()
    for j in range(2):
        for c2 in range(NC):
            cols = pl.ds((j * 8 + c2 * 4) * HD, GROUP_COLS)
            target = device(2 * C + j, Y, Z, c2)
            is_self = jnp.logical_and(2 * C + j == X, C == c2)
            send_or_copy(is_self, q.at[0, :, cols], qx.at[X], q_send.at[0, j, c2], q_recv.at[0], target)
            send_or_copy(is_self, do.at[0, :, cols], dox.at[X], q_send.at[1, j, c2], q_recv.at[1], target)

    own_x.wait()
    for load in loads:
        load.wait()
    acc[...] = jnp.dot(xbuf[head], wbuf[head], preferred_element_type=F32)

    mine = X * NZ + Z

    def forward(r):
        rows = pl.ds(r * CHUNK, CHUNK)
        blocks = kv.at[pl.ds(C * 16, 16), rows, :]
        wait_bytes(blocks, kv_recv.at[r])
        copy = remote(blocks, blocks, fw_send.at[r], fw_recv.at[r], partner)
        copy.start()

    for r in range(ROW_CHUNKS):
        rows = pl.ds(r * CHUNK, CHUNK)
        wait_bytes(xbuf.at[1 - head, rows, :], tok_recv.at[r])
        both = acc[rows, :] + jnp.dot(xbuf[1 - head, rows, :], wbuf[1 - head], preferred_element_type=F32)
        for what in range(2):
            shift = NOISE_STEP * (codes[what, 0, rows, :].astype(F32) - NOISE_MIDDLE)
            value = (both[:, what * KV_W : (what + 1) * KV_W] + shift).astype(BF)
            for j in range(2):
                kvst[j, rows, what * HD : (what + 1) * HD] = value[:, j * HD : (j + 1) * HD]
        for j in range(2):
            src = kvst.at[j, rows, :]
            dst = kv.at[mine, rows, :]
            is_self = jnp.logical_and(same, 2 * C + j == X)
            send_or_copy(is_self, src, dst, kv_send0.at[r, j], kv_recv.at[r], device(2 * C + j, Y, Z, unit_core))

            def far(step, carry, j=j, r=r, src=src, dst=dst):
                target = device(2 * C + j, Y, around(Z + step, NZ), unit_core)
                remote(src, dst, kv_send.at[r, j], kv_recv.at[r], target).start()
                return carry

            lax.fori_loop(1, NZ, far, 0)
        if r:
            forward(r - 1)
    forward(ROW_CHUNKS - 1)

    for r in range(ROW_CHUNKS):
        rows = pl.ds(r * CHUNK, CHUNK)
        wait_bytes(kv.at[pl.ds((1 - C) * 16, 16), rows, :], fw_recv.at[r])
        wait_bytes(kv.at[pl.ds(C * 16, 16), rows, :], fw_send.at[r])
        wait_bytes(xbuf.at[head, rows, :], tok_send.at[r])
        for j in range(2):
            is_self = jnp.logical_and(same, 2 * C + j == X)
            wait_sent(is_self, kvst.at[j, rows, :], kv_send0.at[r, j])
            wait_bytes(kv.at[pl.ds(0, NZ - 1), rows, :], kv_send.at[r, j])
    wait_bytes(qx, q_recv.at[0])
    wait_bytes(dox, q_recv.at[1])
    for j in range(2):
        for c2 in range(NC):
            is_self = jnp.logical_and(2 * C + j == X, C == c2)
            wait_sent(is_self, qx.at[0], q_send.at[0, j, c2])
            wait_sent(is_self, dox.at[0], q_send.at[1, j, c2])


ANY_SPEC = pl.BlockSpec(memory_space=pl.ANY)
VMEM_SPEC = pl.BlockSpec(memory_space=pltpu.VMEM)
DMA = pltpu.SemaphoreType.DMA


def front(tokens, queries, out_grad, key_weight, value_weight, noise_codes):
    return pl.pallas_call(
        front_kernel,
        name="front",
        out_shape=(
            jax.ShapeDtypeStruct((NX, BLK, GROUP_COLS), BF),
            jax.ShapeDtypeStruct((NX, BLK, GROUP_COLS), BF),
            jax.ShapeDtypeStruct((BLOCKS, BLK, KV_W), BF),
        ),
        in_specs=[ANY_SPEC] * 6,
        out_specs=(ANY_SPEC,) * 3,
        scratch_shapes=[
            pltpu.VMEM((2, 1, BLK, KV_W), jnp.int32),
            pltpu.VMEM((2, BLK, HALF_D), BF),
            pltpu.VMEM((2, HALF_D, 2 * KV_W), BF),
            pltpu.VMEM((BLK, 2 * KV_W), F32),
            pltpu.VMEM((2, BLK, KV_W), BF),
            DMA,
            DMA((2, 2)),
            DMA,
            DMA((ROW_CHUNKS,)),
            DMA((ROW_CHUNKS,)),
            DMA((2, 2, 2)),
            DMA((2,)),
            DMA((ROW_CHUNKS, 2)),
            DMA((ROW_CHUNKS, 2)),
            DMA((ROW_CHUNKS,)),
            DMA((ROW_CHUNKS,)),
            DMA((ROW_CHUNKS,)),
        ],
        compiler_params=pltpu.CompilerParams(
            collective_id=0, has_side_effects=True, vmem_limit_bytes=VMEM_GRANT
        ),
        cost_estimate=pl.CostEstimate(flops=10**9, bytes_accessed=16 * 2**20, transcendentals=0),
    )(tokens, queries, out_grad, key_weight, value_weight, noise_codes)


KEYS = 256
LEVELS = (4, 2, 1)
ROWS = 4 * BLK


def attention_kernel(
    order, q, do, kv, dq_out, dkv_out,
    kvb, qs, dos, stb, dpb, dk, dv, dqt, dkvb, kv_sem, q_sem, do_sem, out_sem,
):
    Z = lax.rem(lax.axis_index("ctx"), NZ)

    def at_place(block):
        return pl.ds(pl.multiple_of(order[block] * BLK, BLK), BLK)

    def load(block, carry):
        pltpu.make_async_copy(kv.at[block], kvb.at[at_place(block), :], kv_sem).start()
        return carry

    for x in range(NX):
        for h in range(4):
            cols, rows = pl.ds(h * HD, HD), pl.ds(h * BLK, BLK)
            pltpu.make_async_copy(q.at[x, :, cols], qs.at[x, rows, :], q_sem).start()
            pltpu.make_async_copy(do.at[x, :, cols], dos.at[x, rows, :], do_sem).start()
    lax.fori_loop(0, BLOCKS, load, 0)

    def clear(i, carry):
        rows = pl.ds(pl.multiple_of(i * 256, 256), 256)
        dk[rows, :] = jnp.zeros((256, HD), F32)
        dv[rows, :] = jnp.zeros((256, HD), F32)
        return carry

    lax.fori_loop(0, 16, clear, 0)
    wait_bytes(qs, q_sem)
    wait_bytes(dos, do_sem)
    wait_bytes(kvb, kv_sem)

    def run(count, body, carry):
        done = 0
        for units in LEVELS:
            times = (count - done) // units
            base = done

            def step(i, state, units=units, base=base):
                start = pl.multiple_of((base + i * units) * KEYS, KEYS)
                return body(pl.ds(start, units * KEYS), units * KEYS, state)

            carry = lax.fori_loop(0, times, step, carry)
            done = base + times * units
        return carry

    def fold(array, size, how):
        return how(array.reshape(size // 8, 8, ROWS), axis=0)

    def tile(x, carry):
        place = order[x * NZ + Z]
        last = place // 2
        qx = qs[x]
        dx = dos[x]

        def score_step(rows, size, top):
            st = lax.dot_general(kvb[rows, :HD], qx, NT, preferred_element_type=F32)
            stb[rows, :] = st
            return jnp.maximum(top, fold(st, size, jnp.max))

        top = run(last, score_step, jnp.full((8, ROWS), FLOOR_SCORE, F32))
        rows = pl.ds(pl.multiple_of(last * KEYS, KEYS), KEYS)
        st = lax.dot_general(kvb[rows, :HD], qx, NT, preferred_element_type=F32)
        key_places = last * KEYS + lax.broadcasted_iota(jnp.int32, (KEYS, ROWS), 0)
        query_places = place * BLK + lax.rem(lax.broadcasted_iota(jnp.int32, (KEYS, ROWS), 1), BLK)
        st = jnp.where(key_places <= query_places, st, FLOOR_SCORE)
        stb[rows, :] = st
        top = jnp.maximum(top, fold(st, KEYS, jnp.max))
        top = jnp.max(top, axis=0, keepdims=True) * SCALE_LOG2

        def weigh_step(rows, size, state):
            total, weighted = state
            weights = jnp.exp2(stb[rows, :] * SCALE_LOG2 - top)
            dpt = lax.dot_general(kvb[rows, HD:], dx, NT, preferred_element_type=F32)
            dpb[rows, :] = dpt
            stb[rows, :] = weights
            return total + fold(weights, size, jnp.sum), weighted + fold(weights * dpt, size, jnp.sum)

        zero = jnp.zeros((8, ROWS), F32)
        total, weighted = run(last + 1, weigh_step, (zero, zero))
        inverse = 1.0 / jnp.sum(total, axis=0, keepdims=True)
        delta = jnp.sum(weighted, axis=0, keepdims=True) * inverse
        dqt[...] = jnp.zeros((HD, ROWS), F32)

        def grad_step(rows, size, state):
            probs = stb[rows, :] * inverse
            low = probs.astype(BF)
            grads = (probs * (dpb[rows, :] - delta)).astype(BF)
            dv[rows, :] += lax.dot_general(low, dx, NN, preferred_element_type=F32)
            dk[rows, :] += lax.dot_general(grads, qx, NN, preferred_element_type=F32)
            dqt[...] += lax.dot_general(kvb[rows, :HD], grads, TN, preferred_element_type=F32)
            return state

        run(last + 1, grad_step, 0)
        dq = dqt[...].T
        for h in range(4):
            dq_out[x, :, h * HD : (h + 1) * HD] = (dq[h * BLK : (h + 1) * BLK, :] * SCALE).astype(BF)
        return carry

    lax.fori_loop(0, NX, tile, 0)

    def finish(i, carry):
        rows = pl.ds(pl.multiple_of(i * 256, 256), 256)
        dkvb[rows, :HD] = (dk[rows, :] * SCALE).astype(BF)
        dkvb[rows, HD:] = dv[rows, :].astype(BF)
        return carry

    lax.fori_loop(0, 16, finish, 0)

    def store(block, carry):
        dst = dkv_out.at[block // NZ, lax.rem(block, NZ)]
        pltpu.make_async_copy(dkvb.at[at_place(block), :], dst, out_sem).start()
        return carry

    lax.fori_loop(0, BLOCKS, store, 0)
    wait_bytes(dkvb, out_sem)


def attention(block_order, qx, dox, kv):
    tokens = BLOCKS * BLK
    return pl.pallas_call(
        attention_kernel,
        name="attention",
        out_shape=(
            jax.ShapeDtypeStruct((NX, BLK, GROUP_COLS), BF),
            jax.ShapeDtypeStruct((NX, NZ, BLK, KV_W), BF),
        ),
        in_specs=[pl.BlockSpec(memory_space=pltpu.SMEM)] + [ANY_SPEC] * 3,
        out_specs=(VMEM_SPEC, ANY_SPEC),
        scratch_shapes=[
            pltpu.VMEM((tokens, KV_W), BF),
            pltpu.VMEM((NX, ROWS, HD), BF),
            pltpu.VMEM((NX, ROWS, HD), BF),
            pltpu.VMEM((tokens, ROWS), F32),
            pltpu.VMEM((tokens, ROWS), F32),
            pltpu.VMEM((tokens, HD), F32),
            pltpu.VMEM((tokens, HD), F32),
            pltpu.VMEM((HD, ROWS), F32),
            pltpu.VMEM((tokens, KV_W), BF),
            DMA,
            DMA,
            DMA,
            DMA,
        ],
        compiler_params=pltpu.CompilerParams(vmem_limit_bytes=VMEM_GRANT),
        cost_estimate=pl.CostEstimate(flops=10**10, bytes_accessed=8 * 2**20, transcendentals=10**7),
    )(block_order, qx, dox, kv)


class Ring:
    def __init__(self, count, position, neighbour, own, slots, send_sems, recv_sems):
        self.count, self.position, self.neighbour, self.own = count, position, neighbour, own
        self.slots, self.send_sems, self.recv_sems = slots, send_sems, recv_sems
        self.steps = count // 2
        self.sent = []

    def chains(self, step):
        for way in range(2):
            for part in range(2):
                length = self.steps if way == part else self.steps - 1
                if step >= self.steps - length:
                    yield way, part, step == self.steps - length

    def step(self, step):
        for way, part, first in self.chains(step):
            sign = 1 if way == 0 else -1
            mine = self.own(part, sign * (self.steps - step))
            if first:
                src = mine
            else:
                src = self.slots.at[way, part, step - 1]
                wait_bytes(src, self.recv_sems.at[way, part, step - 1])
                src[...] = (src[...].astype(F32) + mine[...].astype(F32)).astype(BF)
            copy = remote(
                src,
                self.slots.at[way, part, step],
                self.send_sems.at[way, part, step],
                self.recv_sems.at[way, part, step],
                self.neighbour(sign),
            )
            copy.start()
            self.sent.append(copy)

    def result(self, part):
        total = self.own(part, 0)[...].astype(F32)
        for way in range(2):
            slot = self.slots.at[way, part, self.steps - 1]
            wait_bytes(slot, self.recv_sems.at[way, part, self.steps - 1])
            total += slot[...].astype(F32)
        return total.astype(BF)

    def finish(self):
        for copy in self.sent:
            copy.wait_send()


def span(start, size):
    return pl.ds(pl.multiple_of(start, 16), size)


HALF_ROWS = BLK // 2
DELTAS = (4, 3, -3, 2, -2, 1, -1, 0)


def back_kernel(
    dq, dkv, tok, masks, query_grad, key_out, value_out,
    own, other, z1, home_src, raw, mbuf, tokq, tokt, preall, wa, wb, az, ra, ax, fa, bx, rb, bz, fb, final,
    own_sem, mask_sem, ex_send, ex_recv, z1_send, z1_recv, home_send, home_recv, tok_send, tok_recv, dq_send, dq_recv,
    pre_send, pre_recv, pfw_send, pfw_recv, core_sem,
    az_send, az_recv, ax_send, ax_recv, bx_send, bx_recv, bz_send, bz_recv,
    fin_send, fin_recv, f2_send, f2_recv,
):
    X, Y, Z, C = here()
    head, low = Y // 2, lax.rem(Y, 2)
    unit_core = X // 2
    slot = lax.rem(X, 2)
    same = unit_core == C
    partner = device(X, Y, Z, 1 - C)
    beside = device(X, 2 * head + 1 - low, Z, C)
    seq = low * 2 + C

    load_own = pltpu.make_async_copy(dkv.at[pl.ds(C * 2, 2)], own, own_sem)
    load_own.start()
    load_mask = pltpu.make_async_copy(masks, mbuf, mask_sem)
    load_mask.start()

    def z_next(sign):
        return device(X, Y, around(Z + sign, NZ), C)

    def x_next(sign):
        return device(around(X + sign, NX), Y, Z, C)

    def y_next(by):
        return device(X, around(Y + by, NY), Z, C)

    ways = (1, 3, 2)
    i_mine = X + 4 * lax.rem(Z, 2)
    member = i_mine // 2
    target_a = (Y, member // 2, 4 * C + Z // 2, lax.rem(member, 2))
    target_b = (Y, 2 + member // 2, 4 * C + Z // 2, lax.rem(member, 2))

    def is_me(place):
        x, y, z, core = place
        return jnp.logical_and(jnp.logical_and(x == X, y == Y), jnp.logical_and(z == Z, core == C))

    self_a, self_b = is_me(target_a), is_me(target_b)

    signal(partner)
    for xs in range(2):
        for cs in range(NC):
            @pl.when(jnp.logical_not(jnp.logical_and(2 * C + xs == X, C == cs)))
            def _(xs=xs, cs=cs):
                signal(device(2 * C + xs, Y, Z, cs))
    for sign in (1, -1):
        signal(z_next(sign))
        signal(x_next(sign))
    for cs in range(NC):
        signal(device(X, 2 * head + 1 - low, Z, cs))
    for by in ways:
        signal(y_next(by))
    signal(device(around(X + 2, NX), Y, Z, C))
    pl.semaphore_wait(pltpu.get_barrier_semaphore(), 15 - same.astype(jnp.int32))

    exchanges = {}
    for i, delta in enumerate(DELTAS):
        t = around(Z + delta, NZ)
        copy = remote(dkv.at[pl.ds((1 - C) * 2, 2), t], other.at[:, t], ex_send.at[i], ex_recv.at[i], partner)
        copy.start()
        exchanges[delta] = copy
    for xs in range(NX):
        cols = pl.ds(pl.multiple_of((slot * 8 + C * 4) * HD, GROUP_COLS), GROUP_COLS)
        is_self = jnp.logical_and(same, X == xs)
        send_or_copy(
            is_self, dq.at[xs], query_grad.at[0, :, cols], dq_send.at[xs], dq_recv, device(xs, Y, Z, unit_core)
        )
    for quarter in range(4):
        is_self = seq == quarter
        send_or_copy(
            is_self,
            tok.at[0, :, pl.ds(quarter * QUARTER, QUARTER)],
            tokq.at[seq],
            tok_send.at[quarter],
            tok_recv,
            device(X, 2 * head + quarter // 2, Z, quarter % 2),
        )

    load_own.wait()
    ready = set()

    def prepare(delta):
        if delta in ready:
            return
        ready.add(delta)
        t = around(Z + delta, NZ)
        exchanges[delta].wait_recv()
        for part in range(2):
            own[part, t] = (own[part, t].astype(F32) + other[part, t].astype(F32)).astype(BF)

    def own_part(half):
        def get(part, delta):
            prepare(4 if delta == -4 else delta)
            return own.at[part, around(Z + delta, NZ), pl.ds(half * HALF_ROWS, HALF_ROWS), :]

        return get

    rings = [
        Ring(NZ, Z, z_next, own_part(half), z1.at[half], z1_send.at[half], z1_recv.at[half]) for half in range(2)
    ]
    for step in range(NZ // 2):
        for ring in rings:
            ring.step(step)
    for half, ring in enumerate(rings):
        rows = pl.ds(half * HALF_ROWS, HALF_ROWS)
        for part in range(2):
            home_src[part, rows, :] = ring.result(part)
            xs = 2 * C + part
            is_self = jnp.logical_and(same, X == xs)
            send_or_copy(
                is_self,
                home_src.at[part, rows, :],
                raw.at[slot, rows, :],
                home_send.at[half, part],
                home_recv.at[half],
                device(xs, Y, Z, unit_core),
            )

    load_mask.wait()
    sends = []

    def my_rows(half):
        return span(seq * BLK + half * HALF_ROWS, HALF_ROWS)

    for half in range(2):
        rows = pl.ds(half * HALF_ROWS, HALF_ROWS)
        wait_bytes(raw.at[:, rows, :], home_recv.at[half])
        for j in range(2):
            for what in range(2):
                mask = mbuf[what, 0, rows, j * HD : (j + 1) * HD] != 0
                piece = raw[j, rows, what * HD : (what + 1) * HD]
                first = (2 * j + what) * HD
                preall[head, my_rows(half), first : first + HD] = jnp.where(mask, piece, jnp.zeros_like(piece))
        mine = preall.at[head, my_rows(half), :]
        for i, by in enumerate(ways):
            sends.append(remote(mine, mine, pre_send.at[half, i], pre_recv.at[half, i], y_next(by)))
            sends[-1].start()
        sends.append(remote(mine, mine, core_sem.at[half, 0], core_sem.at[half, 1], partner))
        sends[-1].start()

    wait_bytes(tokq, tok_recv)
    for s in range(4):
        tokt[:, :, :, s * BLK : (s + 1) * BLK] = tokq[s].T.reshape(NZ, NX, 32, BLK)

    forwards = []
    for half in range(2):
        for i, by in enumerate(ways):
            ys = around(Y + NY - by, NY)
            start = (lax.rem(ys, 2) * 2 + C) * BLK + half * HALF_ROWS
            piece = preall.at[ys // 2, span(start, HALF_ROWS), :]
            wait_bytes(piece, pre_recv.at[half, i])
            copy = remote(piece, piece, pfw_send.at[half, i], pfw_recv.at[half, i], partner)
            copy.start()
            forwards.append(copy)
    for half in range(2):
        sends[half * 4 + 3].wait_recv()
    for copy in forwards:
        copy.wait_recv()

    made = set()

    def product(which, delta):
        if (which, delta) in made:
            return
        made.add((which, delta))
        if which == 0:
            t = around(Z + delta, NZ)
            rows = tokt[t].reshape(128, 4 * BLK)
        else:
            t = around(X + delta, NX)
            rows = tokt[:, t].reshape(256, 4 * BLK)
        value = jnp.dot(rows, preall[which], preferred_element_type=F32).astype(BF)
        for side in range(2):
            half = value[:, side * KV_W : (side + 1) * KV_W]
            if which == 0:
                wa[side, t] = half.reshape(NX, 32, KV_W)
            else:
                wb[side, :, t] = half.reshape(NZ, 32, KV_W)

    def a_own(side):
        def get(part, delta):
            delta = 4 if delta == -4 else delta
            product(0, delta)
            return wa.at[side, around(Z + delta, NZ), pl.ds(part * 2, 2)]

        return get

    def b_own(side):
        def get(part, delta):
            delta = 2 if delta == -2 else delta
            product(1, delta)
            return wb.at[side, pl.ds(part * 4, 4), around(X + delta, NX)]

        return get

    a1 = [Ring(NZ, Z, z_next, a_own(s), az.at[s], az_send.at[s], az_recv.at[s]) for s in range(2)]
    b1 = [Ring(NX, X, x_next, b_own(s), bx.at[s], bx_send.at[s], bx_recv.at[s]) for s in range(2)]

    def go(rings, step):
        for ring in rings:
            ring.step(step)

    directs = []

    def direct(source, slots, send_sems, recv_sems, count, position, neighbour):
        deltas = sorted([d for d in range(1 - count // 2, count // 2 + 1) if d], key=lambda d: -abs(d))
        for delta in deltas:
            i = delta % count - 1
            src = source.at[around(position + delta, count)]
            copy = remote(src, slots.at[i], send_sems.at[i], recv_sems.at[i], neighbour(delta))
            copy.start()
            directs.append(copy)

    def collect(source, slots, recv_sems, count, position):
        total = source[position].astype(F32)
        for i in range(count - 1):
            wait_bytes(slots.at[i], recv_sems.at[i])
            total += slots[i].astype(F32)
        return total.astype(BF)

    go(a1, 0)
    go(b1, 0)
    go(a1, 1)
    go(b1, 1)
    go(a1, 2)
    for side in range(2):
        for part in range(2):
            rb[side, part * 4 : (part + 1) * 4] = b1[side].result(part)
        direct(rb.at[side], bz.at[side], bz_send.at[side], bz_recv.at[side], NZ, Z, z_next)
        a1[side].step(3)
    for side in range(2):
        for part in range(2):
            ra[side, part * 2 : (part + 1) * 2] = a1[side].result(part)
        direct(ra.at[side], ax.at[side], ax_send.at[side], ax_recv.at[side], NX, X, x_next)
    my_piece = span(i_mine * 32, 32)
    for side in range(2):
        cols = slice(side * KV_W, (side + 1) * KV_W)
        fb[:, cols] = collect(rb.at[side], bz.at[side], bz_recv.at[side], NZ, Z)
    send_or_copy(self_b, fb, final.at[my_piece, :], fin_send.at[1], fin_recv, device(*target_b))
    for side in range(2):
        cols = slice(side * KV_W, (side + 1) * KV_W)
        fa[:, cols] = collect(ra.at[side], ax.at[side], ax_recv.at[side], NX, X)
    send_or_copy(self_a, fa, final.at[my_piece, :], fin_send.at[0], fin_recv, device(*target_a))

    def sixty_four(member):
        return final.at[span(member * 64, 64), :]

    mine = sixty_four(seq)
    wait_bytes(mine, fin_recv)
    to_beside = remote(mine, mine, f2_send.at[0], f2_recv.at[0], beside)
    to_partner = remote(mine, mine, f2_send.at[1], f2_recv.at[1], partner)
    to_beside.start()
    to_partner.start()
    got = sixty_four((1 - low) * 2 + C)
    wait_bytes(got, f2_recv.at[0])
    passed = remote(got, got, f2_send.at[2], f2_recv.at[2], partner)
    passed.start()
    to_partner.wait_recv()
    passed.wait_recv()
    for j in range(2):
        for what, out in ((0, key_out), (1, value_out)):
            first = (2 * j + what) * HD
            out[:, j * HD : (j + 1) * HD] = final[:, first : first + HD].astype(F32) * 0.25

    wait_bytes(query_grad, dq_recv)
    for copy in exchanges.values():
        copy.wait_send()
    for xs in range(NX):
        wait_sent(jnp.logical_and(same, X == xs), dq.at[xs], dq_send.at[xs])
    for quarter in range(4):
        wait_sent(seq == quarter, tokq.at[0], tok_send.at[quarter])
    for half in range(2):
        for part in range(2):
            wait_sent(
                jnp.logical_and(same, X == 2 * C + part),
                raw.at[part, pl.ds(half * HALF_ROWS, HALF_ROWS), :],
                home_send.at[half, part],
            )
    for copy in sends + forwards + [to_beside, to_partner, passed]:
        copy.wait_send()
    for ring in rings + a1 + b1:
        ring.finish()
    for copy in directs:
        copy.wait_send()
    wait_sent(self_a, fa, fin_send.at[0])
    wait_sent(self_b, fb, fin_send.at[1])


def back(dq, dkv, tokens, clip_masks):
    wide = 2 * KV_W
    return pl.pallas_call(
        back_kernel,
        name="back",
        out_shape=(
            jax.ShapeDtypeStruct((1, BLK, 2048), BF),
            jax.ShapeDtypeStruct((256, KV_W), F32),
            jax.ShapeDtypeStruct((256, KV_W), F32),
        ),
        in_specs=[ANY_SPEC] * 4,
        out_specs=(ANY_SPEC, VMEM_SPEC, VMEM_SPEC),
        scratch_shapes=[
            pltpu.VMEM((2, NZ, BLK, KV_W), BF),
            pltpu.VMEM((2, NZ, BLK, KV_W), BF),
            pltpu.VMEM((2, 2, 2, 4, HALF_ROWS, KV_W), BF),
            pltpu.VMEM((2, BLK, KV_W), BF),
            pltpu.VMEM((2, BLK, KV_W), BF),
            pltpu.VMEM((2, 1, BLK, KV_W), jnp.int32),
            pltpu.VMEM((4, BLK, QUARTER), BF),
            pltpu.VMEM((NZ, NX, 32, 4 * BLK), BF),
            pltpu.VMEM((2, 4 * BLK, wide), BF),
            pltpu.VMEM((2, NZ, NX, 32, KV_W), BF),
            pltpu.VMEM((2, NZ, NX, 32, KV_W), BF),
            pltpu.VMEM((2, 2, 2, 4, 2, 32, KV_W), BF),
            pltpu.VMEM((2, NX, 32, KV_W), BF),
            pltpu.VMEM((2, NX - 1, 32, KV_W), BF),
            pltpu.VMEM((32, wide), BF),
            pltpu.VMEM((2, 2, 2, 2, 4, 32, KV_W), BF),
            pltpu.VMEM((2, NZ, 32, KV_W), BF),
            pltpu.VMEM((2, NZ - 1, 32, KV_W), BF),
            pltpu.VMEM((32, wide), BF),
            pltpu.VMEM((256, wide), BF),
            DMA,
            DMA,
            DMA((8,)),
            DMA((8,)),
            DMA((2, 2, 2, 4)),
            DMA((2, 2, 2, 4)),
            DMA((2, 2)),
            DMA((2,)),
            DMA((4,)),
            DMA,
            DMA((4,)),
            DMA,
            DMA((2, 3)),
            DMA((2, 3)),
            DMA((2, 3)),
            DMA((2, 3)),
            DMA((2, 2)),
            DMA((2, 2, 2, 4)),
            DMA((2, 2, 2, 4)),
            DMA((2, NX - 1)),
            DMA((2, NX - 1)),
            DMA((2, 2, 2, 2)),
            DMA((2, 2, 2, 2)),
            DMA((2, NZ - 1)),
            DMA((2, NZ - 1)),
            DMA((2,)),
            DMA,
            DMA((3,)),
            DMA((3,)),
        ],
        compiler_params=pltpu.CompilerParams(
            collective_id=1, has_side_effects=True, vmem_limit_bytes=VMEM_GRANT
        ),
        cost_estimate=pl.CostEstimate(flops=10**9, bytes_accessed=16 * 2**20, transcendentals=0),
    )(dq, dkv, tokens, clip_masks)


def on_device(
    tokens, queries, out_grad, key_weight, value_weight, noise_codes, clip_masks, block_order
):
    qx, dox, kv = front(tokens, queries, out_grad, key_weight, value_weight, noise_codes)
    dq, dkv = attention(block_order, qx, dox, kv)
    return back(dq, dkv, tokens, clip_masks)


def solution(mesh):
    placed = (
        P("dp", "ctx", "head"),
        P("dp", "ctx", "head"),
        P("dp", "ctx", "head"),
        P(None, "head"),
        P(None, "head"),
        P(None, "dp", "ctx", "head"),
        P(None, "dp", "ctx", "head"),
        P(),
    )
    return jax.shard_map(
        on_device,
        mesh=mesh,
        in_specs=placed,
        out_specs=(P("dp", "ctx", "head"), P("ctx", "head"), P("ctx", "head")),
        check_vma=False,
    )
```

```python
import functools
import math

import jax
import jax.numpy as jnp
from jax import lax
from jax.experimental import pallas as pl
from jax.experimental.pallas import tpu as pltpu
from jax.sharding import PartitionSpec as P

HD = 128
BLK = 128
NX, NY, NZ, NC = 4, 4, 8, 2
GROUP_COLS = 512
HALF_D = 4096
QUARTER = 1024
KV_W = 256
BLOCKS = 32
NOISE_STEP = 0.05
NOISE_MIDDLE = 7.5
SCALE = 1.0 / math.sqrt(HD)
SCALE_LOG2 = SCALE * math.log2(math.e)
FLOOR_SCORE = -1e30
BF = jnp.bfloat16
F32 = jnp.float32
MESH = pl.DeviceIdType.MESH
VMEM_GRANT = 62 * 2**20
BACK_GRANT = 52 * 2**20
NT = (((1,), (1,)), ((), ()))
NN = (((1,), (0,)), ((), ()))
TN = (((0,), (0,)), ((), ()))


def here():
    ctx, head, dp = lax.axis_index("ctx"), lax.axis_index("head"), lax.axis_index("dp")
    return ctx // NZ, head * 2 + dp // 2, lax.rem(ctx, NZ), lax.rem(dp, 2)


def device(x, y, z, core):
    return {"ctx": x * NZ + z, "head": y // 2, "dp": lax.rem(y, 2) * 2 + core}


def around(value, count):
    return lax.rem(value + count, count)


def signal(target):
    pl.semaphore_signal(pltpu.get_barrier_semaphore(), inc=1, device_id=target, device_id_type=MESH)


def remote(src, dst, send_sem, recv_sem, target):
    return pltpu.make_async_remote_copy(
        src_ref=src, dst_ref=dst, send_sem=send_sem, recv_sem=recv_sem, device_id=target, device_id_type=MESH
    )


def wait_bytes(ref, sem):
    pltpu.make_async_copy(ref, ref, sem).wait()


def send_or_copy(is_self, src, dst, send_sem, recv_sem, target):
    @pl.when(is_self)
    def _():
        pltpu.make_async_copy(src, dst, recv_sem).start()

    @pl.when(jnp.logical_not(is_self))
    def _():
        remote(src, dst, send_sem, recv_sem, target).start()


def wait_sent(is_self, ref, send_sem):
    @pl.when(jnp.logical_not(is_self))
    def _():
        wait_bytes(ref, send_sem)


CHUNKS = ((0, 16, True), (16, 32, True), (48, 32, True), (80, 32, True), (112, 16, False))
IN_FLIGHT = 2
ROW_CHUNKS = len(CHUNKS)


def front_kernel(
    tok, q, do, kw, vw, codes_in, qx, dox, kv,
    codes, xbuf, wbuf, acc, kvst,
    codes_sem, w_sem, own_sem, tok_send, tok_recv, q_send, q_recv, kv_send, kv_send0, kv_recv, hop_send, fw_send, fw_recv,
):
    X, Y, Z, C = here()
    head = Y // 2
    unit_core = X // 2
    same = unit_core == C
    peer = device(X, around(Y + 2, NY), Z, C)
    partner = device(X, Y, Z, 1 - C)

    loads = [pltpu.make_async_copy(codes_in, codes, codes_sem)]
    for half in range(2):
        rows = pl.ds(half * HALF_D, HALF_D)
        loads.append(pltpu.make_async_copy(kw.at[rows, :], wbuf.at[half, :, pl.ds(0, KV_W)], w_sem.at[half, 0]))
        loads.append(pltpu.make_async_copy(vw.at[rows, :], wbuf.at[half, :, pl.ds(KV_W, KV_W)], w_sem.at[half, 1]))
    own_x = pltpu.make_async_copy(tok.at[0], xbuf.at[head], own_sem)
    own_x.start()
    for load in loads:
        load.start()

    signal(peer)
    signal(partner)
    for xs in range(NX):
        @pl.when(jnp.logical_not(jnp.logical_and(same, X == xs)))
        def _(xs=xs):
            signal(device(xs, Y, Z, unit_core))
    for delta in (1, -1, 2, -2):
        zs = around(Z + delta, NZ)
        signal(device(X, Y, zs, C))
        for part in range(2):
            signal(device(2 * C + part, Y, zs, unit_core))
    pl.semaphore_wait(pltpu.get_barrier_semaphore(), 18 - same.astype(jnp.int32))

    def token_copy(r):
        rows = pl.ds(CHUNKS[r][0], CHUNKS[r][1])
        return remote(tok.at[0, rows, :], xbuf.at[head, rows, :], tok_send.at[r], tok_recv.at[r], peer)

    for r in range(IN_FLIGHT):
        token_copy(r).start()
    for j in range(2):
        for c2 in range(NC):
            cols = pl.ds((j * 8 + c2 * 4) * HD, GROUP_COLS)
            target = device(2 * C + j, Y, Z, c2)
            is_self = jnp.logical_and(2 * C + j == X, C == c2)
            send_or_copy(is_self, q.at[0, :, cols], qx.at[X], q_send.at[0, j, c2], q_recv.at[0], target)
            send_or_copy(is_self, do.at[0, :, cols], dox.at[X], q_send.at[1, j, c2], q_recv.at[1], target)

    own_x.wait()
    for load in loads:
        load.wait()
    acc[...] = jnp.dot(xbuf[head], wbuf[head], preferred_element_type=F32)

    mine = X * NZ + Z

    def rows_of(r):
        return pl.ds(CHUNKS[r][0], CHUNKS[r][1])

    def blocks(r, count):
        return kv.at[pl.ds(C * 16, count), rows_of(r), :]

    def spread(r):
        rows = rows_of(r)
        deltas = (2, -2, 1, -1) if CHUNKS[r][2] else (4, 3, -3, 2, -2, 1, -1)
        for j in range(2):
            src = kvst.at[j, rows, :]
            dst = kv.at[mine, rows, :]
            for delta in deltas:
                kind = {2: 0, -2: 1}.get(delta, 2) if CHUNKS[r][2] else 2
                target = device(2 * C + j, Y, around(Z + delta, NZ), unit_core)
                remote(src, dst, kv_send.at[r, j], kv_recv.at[r, kind], target).start()
            is_self = jnp.logical_and(same, 2 * C + j == X)
            send_or_copy(is_self, src, dst, kv_send0.at[r, j], kv_recv.at[r, 2], device(2 * C + j, Y, Z, unit_core))

    def relay(r):
        rows = rows_of(r)
        for kind, sign in ((0, 1), (1, -1)):
            wait_bytes(blocks(r, 2), kv_recv.at[r, kind])
            source = around(Z - 2 * sign, NZ)
            for part in range(2):
                piece = kv.at[(2 * C + part) * NZ + source, rows, :]
                for far in (2, 1) if part == kind else (1,):
                    target = device(X, Y, around(Z + sign * far, NZ), C)
                    remote(piece, piece, hop_send.at[r, kind], kv_recv.at[r, 2], target).start()

    def forward(r):
        wait_bytes(blocks(r, 12 if CHUNKS[r][2] else 16), kv_recv.at[r, 2])
        whole = blocks(r, 16)
        remote(whole, whole, fw_send.at[r], fw_recv.at[r], partner).start()

    for r in range(ROW_CHUNKS):
        rows = rows_of(r)
        wait_bytes(xbuf.at[1 - head, rows, :], tok_recv.at[r])
        token_copy(r).wait_send()
        if r + IN_FLIGHT < ROW_CHUNKS:
            token_copy(r + IN_FLIGHT).start()
        both = acc[rows, :] + jnp.dot(xbuf[1 - head, rows, :], wbuf[1 - head], preferred_element_type=F32)
        for what in range(2):
            shift = NOISE_STEP * (codes[what, 0, rows, :].astype(F32) - NOISE_MIDDLE)
            value = (both[:, what * KV_W : (what + 1) * KV_W] + shift).astype(BF)
            for j in range(2):
                kvst[j, rows, what * HD : (what + 1) * HD] = value[:, j * HD : (j + 1) * HD]
        spread(r)
        if r >= 1 and CHUNKS[r - 1][2]:
            relay(r - 1)
        if r >= 2:
            forward(r - 2)
    forward(ROW_CHUNKS - 2)
    forward(ROW_CHUNKS - 1)

    for r in range(ROW_CHUNKS):
        rows = rows_of(r)
        wait_bytes(kv.at[pl.ds((1 - C) * 16, 16), rows, :], fw_recv.at[r])
        wait_bytes(blocks(r, 16), fw_send.at[r])
        for j in range(2):
            is_self = jnp.logical_and(same, 2 * C + j == X)
            wait_sent(is_self, kvst.at[j, rows, :], kv_send0.at[r, j])
            wait_bytes(blocks(r, 4 if CHUNKS[r][2] else 7), kv_send.at[r, j])
        if CHUNKS[r][2]:
            for kind in range(2):
                wait_bytes(blocks(r, 3), hop_send.at[r, kind])
    wait_bytes(qx, q_recv.at[0])
    wait_bytes(dox, q_recv.at[1])
    for j in range(2):
        for c2 in range(NC):
            is_self = jnp.logical_and(2 * C + j == X, C == c2)
            wait_sent(is_self, qx.at[0], q_send.at[0, j, c2])
            wait_sent(is_self, dox.at[0], q_send.at[1, j, c2])


ANY_SPEC = pl.BlockSpec(memory_space=pl.ANY)
VMEM_SPEC = pl.BlockSpec(memory_space=pltpu.VMEM)
DMA = pltpu.SemaphoreType.DMA


def front(tokens, queries, out_grad, key_weight, value_weight, noise_codes):
    return pl.pallas_call(
        front_kernel,
        name="front",
        out_shape=(
            jax.ShapeDtypeStruct((NX, BLK, GROUP_COLS), BF),
            jax.ShapeDtypeStruct((NX, BLK, GROUP_COLS), BF),
            jax.ShapeDtypeStruct((BLOCKS, BLK, KV_W), BF),
        ),
        in_specs=[ANY_SPEC] * 6,
        out_specs=(ANY_SPEC,) * 3,
        scratch_shapes=[
            pltpu.VMEM((2, 1, BLK, KV_W), jnp.int32),
            pltpu.VMEM((2, BLK, HALF_D), BF),
            pltpu.VMEM((2, HALF_D, 2 * KV_W), BF),
            pltpu.VMEM((BLK, 2 * KV_W), F32),
            pltpu.VMEM((2, BLK, KV_W), BF),
            DMA,
            DMA((2, 2)),
            DMA,
            DMA((ROW_CHUNKS,)),
            DMA((ROW_CHUNKS,)),
            DMA((2, 2, 2)),
            DMA((2,)),
            DMA((ROW_CHUNKS, 2)),
            DMA((ROW_CHUNKS, 2)),
            DMA((ROW_CHUNKS, 3)),
            DMA((ROW_CHUNKS, 2)),
            DMA((ROW_CHUNKS,)),
            DMA((ROW_CHUNKS,)),
        ],
        compiler_params=pltpu.CompilerParams(
            collective_id=0, has_side_effects=True, vmem_limit_bytes=VMEM_GRANT
        ),
        cost_estimate=pl.CostEstimate(flops=10**9, bytes_accessed=16 * 2**20, transcendentals=0),
    )(tokens, queries, out_grad, key_weight, value_weight, noise_codes)


KEYS = 256
LEVELS = (4, 2, 1)
ROWS = 4 * BLK


def attention_kernel(
    order, q, do, kv, dq_out, dkv_out,
    kvb, qs, dos, stb, dpb, dk, dv, dqt, dkvb, block_at, kv_sem, q_sem, do_sem, out_sem,
):
    Z = lax.rem(lax.axis_index("ctx"), NZ)

    def at_place(block):
        return pl.ds(pl.multiple_of(order[block] * BLK, BLK), BLK)

    def load(block, carry):
        pltpu.make_async_copy(kv.at[block], kvb.at[at_place(block), :], kv_sem).start()
        block_at[order[block]] = block
        return carry

    for x in range(NX):
        for h in range(4):
            cols, rows = pl.ds(h * HD, HD), pl.ds(h * BLK, BLK)
            pltpu.make_async_copy(q.at[x, :, cols], qs.at[x, rows, :], q_sem).start()
            pltpu.make_async_copy(do.at[x, :, cols], dos.at[x, rows, :], do_sem).start()
    lax.fori_loop(0, BLOCKS, load, 0)

    def clear(i, carry):
        rows = pl.ds(pl.multiple_of(i * 256, 256), 256)
        dk[rows, :] = jnp.zeros((256, HD), F32)
        dv[rows, :] = jnp.zeros((256, HD), F32)
        return carry

    lax.fori_loop(0, 16, clear, 0)
    wait_bytes(qs, q_sem)
    wait_bytes(dos, do_sem)
    wait_bytes(kvb, kv_sem)

    def run(count, body, carry):
        done = 0
        for units in LEVELS:
            times = (count - done) // units
            base = done

            def step(i, state, units=units, base=base):
                start = pl.multiple_of((base + i * units) * KEYS, KEYS)
                return body(pl.ds(start, units * KEYS), units * KEYS, state)

            carry = lax.fori_loop(0, times, step, carry)
            done = base + times * units
        return carry

    def fold(array, size, how):
        return how(array.reshape(size // 8, 8, ROWS), axis=0)

    def tile(x, carry):
        place = order[x * NZ + Z]
        last = place // 2
        qx = qs[x]
        dx = dos[x]

        def score_step(rows, size, top):
            st = lax.dot_general(kvb[rows, :HD], qx, NT, preferred_element_type=F32)
            stb[rows, :] = st
            return jnp.maximum(top, fold(st, size, jnp.max))

        top = run(last, score_step, jnp.full((8, ROWS), FLOOR_SCORE, F32))
        rows = pl.ds(pl.multiple_of(last * KEYS, KEYS), KEYS)
        st = lax.dot_general(kvb[rows, :HD], qx, NT, preferred_element_type=F32)
        key_places = last * KEYS + lax.broadcasted_iota(jnp.int32, (KEYS, ROWS), 0)
        query_places = place * BLK + lax.rem(lax.broadcasted_iota(jnp.int32, (KEYS, ROWS), 1), BLK)
        st = jnp.where(key_places <= query_places, st, FLOOR_SCORE)
        stb[rows, :] = st
        top = jnp.maximum(top, fold(st, KEYS, jnp.max))
        top = jnp.max(top, axis=0, keepdims=True) * SCALE_LOG2

        def weigh_step(rows, size, state):
            total, weighted = state
            weights = jnp.exp2(stb[rows, :] * SCALE_LOG2 - top)
            dpt = lax.dot_general(kvb[rows, HD:], dx, NT, preferred_element_type=F32)
            dpb[rows, :] = dpt
            stb[rows, :] = weights
            return total + fold(weights, size, jnp.sum), weighted + fold(weights * dpt, size, jnp.sum)

        zero = jnp.zeros((8, ROWS), F32)
        total, weighted = run(last + 1, weigh_step, (zero, zero))
        inverse = 1.0 / jnp.sum(total, axis=0, keepdims=True)
        delta = jnp.sum(weighted, axis=0, keepdims=True) * inverse
        dqt[...] = jnp.zeros((HD, ROWS), F32)

        def grad_step(rows, size, state):
            probs = stb[rows, :] * inverse
            low = probs.astype(BF)
            grads = (probs * (dpb[rows, :] - delta)).astype(BF)
            dv[rows, :] += lax.dot_general(low, dx, NN, preferred_element_type=F32)
            dk[rows, :] += lax.dot_general(grads, qx, NN, preferred_element_type=F32)
            dqt[...] += lax.dot_general(kvb[rows, :HD], grads, TN, preferred_element_type=F32)
            return state

        run(last + 1, grad_step, 0)
        dq = dqt[...].T
        for h in range(4):
            dq_out[x, :, h * HD : (h + 1) * HD] = (dq[h * BLK : (h + 1) * BLK, :] * SCALE).astype(BF)
        return carry

    lax.fori_loop(0, NX, tile, 0)

    def finish(i, carry):
        rows = pl.ds(pl.multiple_of(i * 256, 256), 256)
        dkvb[rows, :HD] = (dk[rows, :] * SCALE).astype(BF)
        dkvb[rows, HD:] = dv[rows, :].astype(BF)
        for j in range(2):
            block = block_at[2 * i + j]
            src = dkvb.at[pl.ds(pl.multiple_of(i * 256 + j * BLK, BLK), BLK), :]
            pltpu.make_async_copy(src, dkv_out.at[block // NZ, lax.rem(block, NZ)], out_sem).start()
        return carry

    lax.fori_loop(0, 16, finish, 0)
    wait_bytes(dkvb, out_sem)


def attention(block_order, qx, dox, kv):
    tokens = BLOCKS * BLK
    return pl.pallas_call(
        attention_kernel,
        name="attention",
        out_shape=(
            jax.ShapeDtypeStruct((NX, BLK, GROUP_COLS), BF),
            jax.ShapeDtypeStruct((NX, NZ, BLK, KV_W), BF),
        ),
        in_specs=[pl.BlockSpec(memory_space=pltpu.SMEM)] + [ANY_SPEC] * 3,
        out_specs=(VMEM_SPEC, ANY_SPEC),
        scratch_shapes=[
            pltpu.VMEM((tokens, KV_W), BF),
            pltpu.VMEM((NX, ROWS, HD), BF),
            pltpu.VMEM((NX, ROWS, HD), BF),
            pltpu.VMEM((tokens, ROWS), F32),
            pltpu.VMEM((tokens, ROWS), F32),
            pltpu.VMEM((tokens, HD), F32),
            pltpu.VMEM((tokens, HD), F32),
            pltpu.VMEM((HD, ROWS), F32),
            pltpu.VMEM((tokens, KV_W), BF),
            pltpu.SMEM((BLOCKS,), jnp.int32),
            DMA,
            DMA,
            DMA,
            DMA,
        ],
        compiler_params=pltpu.CompilerParams(vmem_limit_bytes=VMEM_GRANT),
        cost_estimate=pl.CostEstimate(flops=10**10, bytes_accessed=8 * 2**20, transcendentals=10**7),
    )(block_order, qx, dox, kv)


class Ring:
    def __init__(self, count, position, neighbour, own, slots, send_sems, recv_sems):
        self.count, self.position, self.neighbour, self.own = count, position, neighbour, own
        self.slots, self.send_sems, self.recv_sems = slots, send_sems, recv_sems
        self.steps = count // 2
        self.sent = []

    def chains(self, step):
        for way in range(2):
            for part in range(2):
                length = self.steps if way == part else self.steps - 1
                if step >= self.steps - length:
                    yield way, part, step == self.steps - length

    def step(self, step):
        for way, part, first in self.chains(step):
            sign = 1 if way == 0 else -1
            mine = self.own(part, sign * (self.steps - step))
            if first:
                src = mine
            else:
                src = self.slots.at[way, part, step - 1]
                wait_bytes(src, self.recv_sems.at[way, part, step - 1])
                src[...] = (src[...].astype(F32) + mine[...].astype(F32)).astype(BF)
            copy = remote(
                src,
                self.slots.at[way, part, step],
                self.send_sems.at[way, part, step],
                self.recv_sems.at[way, part, step],
                self.neighbour(sign),
            )
            copy.start()
            self.sent.append(copy)

    def result(self, part):
        total = self.own(part, 0)[...].astype(F32)
        for way in range(2):
            slot = self.slots.at[way, part, self.steps - 1]
            wait_bytes(slot, self.recv_sems.at[way, part, self.steps - 1])
            total += slot[...].astype(F32)
        return total.astype(BF)

    def finish(self):
        for copy in self.sent:
            copy.wait_send()


def span(start, size):
    return pl.ds(pl.multiple_of(start, 16), size)


HALF_ROWS = BLK // 2
DELTAS = (4, 3, -3, 2, -2, 1, -1, 0)


def back_kernel(
    dq, dkv, tok, masks, query_grad, key_out, value_out,
    own, other, z1, home_src, raw, mbuf, tokq, tokt, preall, wa, wb, az, ra, ax, bx, rb, bz, fin, final,
    own_sem, mask_sem, ex_send, ex_recv, z1_send, z1_recv, home_send, home_recv, tok_send, tok_recv, dq_send, dq_recv,
    pre_send, pre_recv, pfw_send, pfw_recv, core_sem,
    az_send, az_recv, ax_send, ax_recv, bx_send, bx_recv, bz_send, bz_recv,
    fin_send, fin_recv, f2_send, f2_recv,
):
    X, Y, Z, C = here()
    head, low = Y // 2, lax.rem(Y, 2)
    unit_core = X // 2
    slot = lax.rem(X, 2)
    same = unit_core == C
    partner = device(X, Y, Z, 1 - C)
    beside = device(X, 2 * head + 1 - low, Z, C)
    seq = low * 2 + C

    load_own = pltpu.make_async_copy(dkv.at[pl.ds(C * 2, 2)], own, own_sem)
    load_own.start()
    load_mask = pltpu.make_async_copy(masks, mbuf, mask_sem)
    load_mask.start()

    def z_next(sign):
        return device(X, Y, around(Z + sign, NZ), C)

    def x_next(sign):
        return device(around(X + sign, NX), Y, Z, C)

    def y_next(by):
        return device(X, around(Y + by, NY), Z, C)

    ways = (1, 3, 2)
    i_mine = X + 4 * lax.rem(Z, 2)
    member = i_mine // 2
    target_a = (Y, 2 * head + member // 2, 4 * C + Z // 2, lax.rem(member, 2))
    target_b = (Y, 2 * (1 - head) + member // 2, 4 * C + Z // 2, lax.rem(member, 2))

    def is_me(place):
        x, y, z, core = place
        return jnp.logical_and(jnp.logical_and(x == X, y == Y), jnp.logical_and(z == Z, core == C))

    self_a, self_b = is_me(target_a), is_me(target_b)

    signal(partner)
    for xs in range(2):
        for cs in range(NC):
            @pl.when(jnp.logical_not(jnp.logical_and(2 * C + xs == X, C == cs)))
            def _(xs=xs, cs=cs):
                signal(device(2 * C + xs, Y, Z, cs))
    for sign in (1, -1):
        signal(z_next(sign))
        signal(x_next(sign))
    for cs in range(NC):
        signal(device(X, 2 * head + 1 - low, Z, cs))
    for by in ways:
        signal(y_next(by))
    signal(device(around(X + 2, NX), Y, Z, C))
    pl.semaphore_wait(pltpu.get_barrier_semaphore(), 15 - same.astype(jnp.int32))

    exchanges = {}
    for i, delta in enumerate(DELTAS):
        t = around(Z + delta, NZ)
        copy = remote(dkv.at[pl.ds((1 - C) * 2, 2), t], other.at[:, t], ex_send.at[i], ex_recv.at[i], partner)
        copy.start()
        exchanges[delta] = copy
    for xs in range(NX):
        cols = pl.ds(pl.multiple_of((slot * 8 + C * 4) * HD, GROUP_COLS), GROUP_COLS)
        is_self = jnp.logical_and(same, X == xs)
        send_or_copy(
            is_self, dq.at[xs], query_grad.at[0, :, cols], dq_send.at[xs], dq_recv, device(xs, Y, Z, unit_core)
        )
    for quarter in range(4):
        is_self = seq == quarter
        send_or_copy(
            is_self,
            tok.at[0, :, pl.ds(quarter * QUARTER, QUARTER)],
            tokq.at[seq],
            tok_send.at[quarter],
            tok_recv,
            device(X, 2 * head + quarter // 2, Z, quarter % 2),
        )

    load_own.wait()
    ready = set()

    def prepare(delta):
        if delta in ready:
            return
        ready.add(delta)
        t = around(Z + delta, NZ)
        exchanges[delta].wait_recv()
        for part in range(2):
            own[part, t] = (own[part, t].astype(F32) + other[part, t].astype(F32)).astype(BF)

    def own_part(half):
        def get(part, delta):
            prepare(4 if delta == -4 else delta)
            return own.at[part, around(Z + delta, NZ), pl.ds(half * HALF_ROWS, HALF_ROWS), :]

        return get

    rings = [
        Ring(NZ, Z, z_next, own_part(half), z1.at[half], z1_send.at[half], z1_recv.at[half]) for half in range(2)
    ]
    for step in range(NZ // 2):
        for ring in rings:
            ring.step(step)
    for half, ring in enumerate(rings):
        rows = pl.ds(half * HALF_ROWS, HALF_ROWS)
        for part in range(2):
            home_src[part, rows, :] = ring.result(part)
            xs = 2 * C + part
            is_self = jnp.logical_and(same, X == xs)
            send_or_copy(
                is_self,
                home_src.at[part, rows, :],
                raw.at[slot, rows, :],
                home_send.at[half, part],
                home_recv.at[half],
                device(xs, Y, Z, unit_core),
            )

    load_mask.wait()
    sends = []
    y_targets = (beside, y_next(around(2 * low - 1, NY)), y_next(2))
    y_places = ((head, 1 - low), (1 - head, 1 - low), (1 - head, low))

    def my_rows(half):
        return span(seq * BLK + half * HALF_ROWS, HALF_ROWS)

    for half in range(2):
        rows = pl.ds(half * HALF_ROWS, HALF_ROWS)
        wait_bytes(raw.at[:, rows, :], home_recv.at[half])
        for j in range(2):
            for what in range(2):
                mask = mbuf[what, 0, rows, j * HD : (j + 1) * HD] != 0
                piece = raw[j, rows, what * HD : (what + 1) * HD]
                first = (2 * j + what) * HD
                preall[head, my_rows(half), first : first + HD] = jnp.where(mask, piece, jnp.zeros_like(piece))
        mine = preall.at[head, my_rows(half), :]
        sends.append(remote(mine, mine, core_sem.at[half, 0], core_sem.at[half, 1], partner))
        sends[-1].start()
        for i in range(2):
            sends.append(remote(mine, mine, pre_send.at[half, i], pre_recv.at[half, i], y_targets[i]))
            sends[-1].start()
    for half in range(2):
        mine = preall.at[head, my_rows(half), :]
        sends.append(remote(mine, mine, pre_send.at[half, 2], pre_recv.at[half, 2], y_targets[2]))
        sends[-1].start()

    wait_bytes(tokq, tok_recv)
    for s in range(4):
        tokt[:, :, :, s * BLK : (s + 1) * BLK] = tokq[s].T.reshape(NZ, NX, 32, BLK)

    forwards = []

    def pass_on(i):
        place, lows = y_places[i]
        for half in range(2):
            piece = preall.at[place, span((lows * 2 + C) * BLK + half * HALF_ROWS, HALF_ROWS), :]
            wait_bytes(piece, pre_recv.at[half, i])
            copy = remote(piece, piece, pfw_send.at[half, i], pfw_recv.at[half, i], partner)
            copy.start()
            forwards.append(copy)
        return forwards[-2:]

    passed_on = [pass_on(0), pass_on(1)]
    for half in range(2):
        sends[half * 3].wait_recv()
    for copy in passed_on[0]:
        copy.wait_recv()

    made = set()

    def product(path, which, delta):
        if (path, which, delta) in made:
            return
        made.add((path, which, delta))
        cols = slice(path * KV_W, (path + 1) * KV_W)
        if path == 0:
            t = around(Z + delta, NZ)
            rows = tokt[t].reshape(128, 4 * BLK)
        else:
            t = around(X + delta, NX)
            rows = tokt[:, t].reshape(256, 4 * BLK)
        value = jnp.dot(rows, preall[around(head + which, 2), :, cols], preferred_element_type=F32).astype(BF)
        if path == 0:
            wa[which, t] = value.reshape(NX, 32, KV_W)
        else:
            wb[which, :, t] = value.reshape(NZ, 32, KV_W)

    def a_own(which):
        def get(part, delta):
            delta = 4 if delta == -4 else delta
            product(0, which, delta)
            return wa.at[which, around(Z + delta, NZ), pl.ds(part * 2, 2)]

        return get

    def b_own(which):
        def get(part, delta):
            delta = 2 if delta == -2 else delta
            product(1, which, delta)
            return wb.at[which, pl.ds(part * 4, 4), around(X + delta, NX)]

        return get

    a1 = [Ring(NZ, Z, z_next, a_own(s), az.at[s], az_send.at[s], az_recv.at[s]) for s in range(2)]
    b1 = [Ring(NX, X, x_next, b_own(s), bx.at[s], bx_send.at[s], bx_recv.at[s]) for s in range(2)]

    directs = []

    def direct(source, slots, send_sems, recv_sems, count, position, neighbour):
        deltas = sorted([d for d in range(1 - count // 2, count // 2 + 1) if d], key=lambda d: -abs(d))
        for delta in deltas:
            i = delta % count - 1
            src = source.at[around(position + delta, count)]
            copy = remote(src, slots.at[i], send_sems.at[i], recv_sems.at[i], neighbour(delta))
            copy.start()
            directs.append(copy)

    def collect(source, slots, recv_sems, count, position):
        total = source[position].astype(F32)
        for i in range(count - 1):
            wait_bytes(slots.at[i], recv_sems.at[i])
            total += slots[i].astype(F32)
        return total.astype(BF)

    def turn_a(which):
        for part in range(2):
            ra[which, part * 2 : (part + 1) * 2] = a1[which].result(part)
        direct(ra.at[which], ax.at[which], ax_send.at[which], ax_recv.at[which], NX, X, x_next)

    def turn_b(which):
        for part in range(2):
            rb[which, part * 4 : (part + 1) * 4] = b1[which].result(part)
        direct(rb.at[which], bz.at[which], bz_send.at[which], bz_recv.at[which], NZ, Z, z_next)

    def deliver(which, is_self, target):
        fin[which, :, KV_W:] = collect(rb.at[which], bz.at[which], bz_recv.at[which], NZ, Z)
        fin[which, :, :KV_W] = collect(ra.at[which], ax.at[which], ax_recv.at[which], NX, X)
        dst = final.at[span(i_mine * 32, 32), :]
        send_or_copy(is_self, fin.at[which], dst, fin_send.at[which], fin_recv, device(*target))

    a1[0].step(0)
    b1[0].step(0)
    passed_on.append(pass_on(2))
    a1[0].step(1)
    for copy in passed_on[1] + passed_on[2]:
        copy.wait_recv()
    a1[1].step(0)
    b1[1].step(0)
    b1[0].step(1)
    a1[0].step(2)
    a1[1].step(1)
    b1[1].step(1)
    turn_b(0)
    a1[0].step(3)
    a1[1].step(2)
    turn_a(0)
    turn_b(1)
    a1[1].step(3)
    deliver(0, self_a, target_a)
    turn_a(1)
    deliver(1, self_b, target_b)

    def sixty_four(member):
        return final.at[span(member * 64, 64), :]

    mine = sixty_four(seq)
    wait_bytes(mine, fin_recv)
    to_beside = remote(mine, mine, f2_send.at[0], f2_recv.at[0], beside)
    to_partner = remote(mine, mine, f2_send.at[1], f2_recv.at[1], partner)
    to_beside.start()
    to_partner.start()
    got = sixty_four((1 - low) * 2 + C)
    wait_bytes(got, f2_recv.at[0])
    passed = remote(got, got, f2_send.at[2], f2_recv.at[2], partner)
    passed.start()
    to_partner.wait_recv()
    passed.wait_recv()
    for j in range(2):
        for what, out in ((0, key_out), (1, value_out)):
            first = (2 * j + what) * HD
            out[:, j * HD : (j + 1) * HD] = final[:, first : first + HD].astype(F32) * 0.25

    wait_bytes(query_grad, dq_recv)
    for copy in exchanges.values():
        copy.wait_send()
    for xs in range(NX):
        wait_sent(jnp.logical_and(same, X == xs), dq.at[xs], dq_send.at[xs])
    for quarter in range(4):
        wait_sent(seq == quarter, tokq.at[0], tok_send.at[quarter])
    for half in range(2):
        for part in range(2):
            wait_sent(
                jnp.logical_and(same, X == 2 * C + part),
                raw.at[part, pl.ds(half * HALF_ROWS, HALF_ROWS), :],
                home_send.at[half, part],
            )
    for copy in sends + forwards + [to_beside, to_partner, passed]:
        copy.wait_send()
    for ring in rings + a1 + b1:
        ring.finish()
    for copy in directs:
        copy.wait_send()
    wait_sent(self_a, fin.at[0], fin_send.at[0])
    wait_sent(self_b, fin.at[1], fin_send.at[1])


def back(dq, dkv, tokens, clip_masks):
    wide = 2 * KV_W
    return pl.pallas_call(
        back_kernel,
        name="back",
        out_shape=(
            jax.ShapeDtypeStruct((1, BLK, 2048), BF),
            jax.ShapeDtypeStruct((256, KV_W), F32),
            jax.ShapeDtypeStruct((256, KV_W), F32),
        ),
        in_specs=[ANY_SPEC] * 4,
        out_specs=(ANY_SPEC, VMEM_SPEC, VMEM_SPEC),
        scratch_shapes=[
            pltpu.VMEM((2, NZ, BLK, KV_W), BF),
            pltpu.VMEM((2, NZ, BLK, KV_W), BF),
            pltpu.VMEM((2, 2, 2, 4, HALF_ROWS, KV_W), BF),
            pltpu.VMEM((2, BLK, KV_W), BF),
            pltpu.VMEM((2, BLK, KV_W), BF),
            pltpu.VMEM((2, 1, BLK, KV_W), jnp.int32),
            pltpu.VMEM((4, BLK, QUARTER), BF),
            pltpu.VMEM((NZ, NX, 32, 4 * BLK), BF),
            pltpu.VMEM((2, 4 * BLK, wide), BF),
            pltpu.VMEM((2, NZ, NX, 32, KV_W), BF),
            pltpu.VMEM((2, NZ, NX, 32, KV_W), BF),
            pltpu.VMEM((2, 2, 2, 4, 2, 32, KV_W), BF),
            pltpu.VMEM((2, NX, 32, KV_W), BF),
            pltpu.VMEM((2, NX - 1, 32, KV_W), BF),
            pltpu.VMEM((2, 2, 2, 2, 4, 32, KV_W), BF),
            pltpu.VMEM((2, NZ, 32, KV_W), BF),
            pltpu.VMEM((2, NZ - 1, 32, KV_W), BF),
            pltpu.VMEM((2, 32, wide), BF),
            pltpu.VMEM((256, wide), BF),
            DMA,
            DMA,
            DMA((8,)),
            DMA((8,)),
            DMA((2, 2, 2, 4)),
            DMA((2, 2, 2, 4)),
            DMA((2, 2)),
            DMA((2,)),
            DMA((4,)),
            DMA,
            DMA((4,)),
            DMA,
            DMA((2, 3)),
            DMA((2, 3)),
            DMA((2, 3)),
            DMA((2, 3)),
            DMA((2, 2)),
            DMA((2, 2, 2, 4)),
            DMA((2, 2, 2, 4)),
            DMA((2, NX - 1)),
            DMA((2, NX - 1)),
            DMA((2, 2, 2, 2)),
            DMA((2, 2, 2, 2)),
            DMA((2, NZ - 1)),
            DMA((2, NZ - 1)),
            DMA((2,)),
            DMA,
            DMA((3,)),
            DMA((3,)),
        ],
        compiler_params=pltpu.CompilerParams(
            collective_id=1, has_side_effects=True, vmem_limit_bytes=BACK_GRANT
        ),
        cost_estimate=pl.CostEstimate(flops=10**9, bytes_accessed=16 * 2**20, transcendentals=0),
    )(dq, dkv, tokens, clip_masks)


def on_device(
    tokens, queries, out_grad, key_weight, value_weight, noise_codes, clip_masks, block_order
):
    qx, dox, kv = front(tokens, queries, out_grad, key_weight, value_weight, noise_codes)
    dq, dkv = attention(block_order, qx, dox, kv)
    return back(dq, dkv, tokens, clip_masks)


def solution(mesh):
    placed = (
        P("dp", "ctx", "head"),
        P("dp", "ctx", "head"),
        P("dp", "ctx", "head"),
        P(None, "head"),
        P(None, "head"),
        P(None, "dp", "ctx", "head"),
        P(None, "dp", "ctx", "head"),
        P(),
    )
    return jax.shard_map(
        on_device,
        mesh=mesh,
        in_specs=placed,
        out_specs=(P("dp", "ctx", "head"), P("ctx", "head"), P("ctx", "head")),
        check_vma=False,
    )
```

```python
import functools
import math

import jax
import jax.numpy as jnp
from jax import lax
from jax.experimental import pallas as pl
from jax.experimental.pallas import tpu as pltpu
from jax.sharding import PartitionSpec as P

HD = 128
BLK = 128
NX, NY, NZ, NC = 4, 4, 8, 2
GROUP_COLS = 512
HALF_D = 4096
QUARTER = 1024
KV_W = 256
BLOCKS = 32
NOISE_STEP = 0.05
NOISE_MIDDLE = 7.5
SCALE = 1.0 / math.sqrt(HD)
SCALE_LOG2 = SCALE * math.log2(math.e)
FLOOR_SCORE = -1e30
BF = jnp.bfloat16
F32 = jnp.float32
MESH = pl.DeviceIdType.MESH
VMEM_GRANT = 62 * 2**20
ATTENTION_GRANT = 53 * 2**20
BACK_GRANT = 52 * 2**20
NT = (((1,), (1,)), ((), ()))
NN = (((1,), (0,)), ((), ()))
TN = (((0,), (0,)), ((), ()))


def here():
    ctx, head, dp = lax.axis_index("ctx"), lax.axis_index("head"), lax.axis_index("dp")
    return ctx // NZ, head * 2 + dp // 2, lax.rem(ctx, NZ), lax.rem(dp, 2)


def device(x, y, z, core):
    return {"ctx": x * NZ + z, "head": y // 2, "dp": lax.rem(y, 2) * 2 + core}


def around(value, count):
    return lax.rem(value + count, count)


def signal(target):
    pl.semaphore_signal(pltpu.get_barrier_semaphore(), inc=1, device_id=target, device_id_type=MESH)


def remote(src, dst, send_sem, recv_sem, target):
    return pltpu.make_async_remote_copy(
        src_ref=src, dst_ref=dst, send_sem=send_sem, recv_sem=recv_sem, device_id=target, device_id_type=MESH
    )


def wait_bytes(ref, sem):
    pltpu.make_async_copy(ref, ref, sem).wait()


def send_or_copy(is_self, src, dst, send_sem, recv_sem, target):
    @pl.when(is_self)
    def _():
        pltpu.make_async_copy(src, dst, recv_sem).start()

    @pl.when(jnp.logical_not(is_self))
    def _():
        remote(src, dst, send_sem, recv_sem, target).start()


def wait_sent(is_self, ref, send_sem):
    @pl.when(jnp.logical_not(is_self))
    def _():
        wait_bytes(ref, send_sem)


CHUNKS = ((0, 16, True), (16, 32, True), (48, 32, True), (80, 32, True), (112, 16, False))
IN_FLIGHT = 2
ROW_CHUNKS = len(CHUNKS)


def front_kernel(
    tok, q, do, kw, vw, codes_in, qx, dox, kv,
    codes, xbuf, wbuf, acc, kvst,
    codes_sem, w_sem, own_sem, tok_send, tok_recv, q_send, q_recv, kv_send, kv_send0, kv_recv, hop_send, fw_send, fw_recv,
):
    X, Y, Z, C = here()
    head = Y // 2
    unit_core = X // 2
    same = unit_core == C
    peer = device(X, around(Y + 2, NY), Z, C)
    partner = device(X, Y, Z, 1 - C)

    loads = [pltpu.make_async_copy(codes_in, codes, codes_sem)]
    for half in range(2):
        rows = pl.ds(half * HALF_D, HALF_D)
        loads.append(pltpu.make_async_copy(kw.at[rows, :], wbuf.at[half, :, pl.ds(0, KV_W)], w_sem.at[half, 0]))
        loads.append(pltpu.make_async_copy(vw.at[rows, :], wbuf.at[half, :, pl.ds(KV_W, KV_W)], w_sem.at[half, 1]))
    own_x = pltpu.make_async_copy(tok.at[0], xbuf.at[head], own_sem)
    own_x.start()
    for load in loads:
        load.start()

    signal(peer)
    signal(partner)
    for xs in range(NX):
        @pl.when(jnp.logical_not(jnp.logical_and(same, X == xs)))
        def _(xs=xs):
            signal(device(xs, Y, Z, unit_core))
    for delta in (1, -1, 2, -2):
        zs = around(Z + delta, NZ)
        signal(device(X, Y, zs, C))
        for part in range(2):
            signal(device(2 * C + part, Y, zs, unit_core))
    pl.semaphore_wait(pltpu.get_barrier_semaphore(), 18 - same.astype(jnp.int32))

    def token_copy(r):
        rows = pl.ds(CHUNKS[r][0], CHUNKS[r][1])
        return remote(tok.at[0, rows, :], xbuf.at[head, rows, :], tok_send.at[r], tok_recv.at[r], peer)

    for r in range(IN_FLIGHT):
        token_copy(r).start()
    for j in range(2):
        for c2 in range(NC):
            cols = pl.ds((j * 8 + c2 * 4) * HD, GROUP_COLS)
            target = device(2 * C + j, Y, Z, c2)
            is_self = jnp.logical_and(2 * C + j == X, C == c2)
            send_or_copy(is_self, q.at[0, :, cols], qx.at[X], q_send.at[0, j, c2], q_recv.at[0], target)
            send_or_copy(is_self, do.at[0, :, cols], dox.at[X], q_send.at[1, j, c2], q_recv.at[1], target)

    own_x.wait()
    for load in loads:
        load.wait()
    acc[...] = jnp.dot(xbuf[head], wbuf[head], preferred_element_type=F32)

    mine = X * NZ + Z

    def rows_of(r):
        return pl.ds(CHUNKS[r][0], CHUNKS[r][1])

    def blocks(r, count):
        return kv.at[pl.ds(C * 16, count), rows_of(r), :]

    def spread(r):
        rows = rows_of(r)
        deltas = (2, -2, 1, -1) if CHUNKS[r][2] else (4, 3, -3, 2, -2, 1, -1)
        for j in range(2):
            src = kvst.at[j, rows, :]
            dst = kv.at[mine, rows, :]
            for delta in deltas:
                kind = {2: 0, -2: 1}.get(delta, 2) if CHUNKS[r][2] else 2
                target = device(2 * C + j, Y, around(Z + delta, NZ), unit_core)
                remote(src, dst, kv_send.at[r, j], kv_recv.at[r, kind], target).start()
            is_self = jnp.logical_and(same, 2 * C + j == X)
            send_or_copy(is_self, src, dst, kv_send0.at[r, j], kv_recv.at[r, 2], device(2 * C + j, Y, Z, unit_core))

    def relay(r):
        rows = rows_of(r)
        for kind, sign in ((0, 1), (1, -1)):
            wait_bytes(blocks(r, 2), kv_recv.at[r, kind])
            source = around(Z - 2 * sign, NZ)
            for part in range(2):
                piece = kv.at[(2 * C + part) * NZ + source, rows, :]
                for far in (2, 1) if part == kind else (1,):
                    target = device(X, Y, around(Z + sign * far, NZ), C)
                    remote(piece, piece, hop_send.at[r, kind], kv_recv.at[r, 2], target).start()

    def forward(r):
        wait_bytes(blocks(r, 12 if CHUNKS[r][2] else 16), kv_recv.at[r, 2])
        whole = blocks(r, 16)
        remote(whole, whole, fw_send.at[r], fw_recv.at[r], partner).start()

    for r in range(ROW_CHUNKS):
        rows = rows_of(r)
        wait_bytes(xbuf.at[1 - head, rows, :], tok_recv.at[r])
        token_copy(r).wait_send()
        if r + IN_FLIGHT < ROW_CHUNKS:
            token_copy(r + IN_FLIGHT).start()
        both = acc[rows, :] + jnp.dot(xbuf[1 - head, rows, :], wbuf[1 - head], preferred_element_type=F32)
        for what in range(2):
            shift = NOISE_STEP * (codes[what, 0, rows, :].astype(F32) - NOISE_MIDDLE)
            value = (both[:, what * KV_W : (what + 1) * KV_W] + shift).astype(BF)
            for j in range(2):
                kvst[j, rows, what * HD : (what + 1) * HD] = value[:, j * HD : (j + 1) * HD]
        spread(r)
        if r >= 1 and CHUNKS[r - 1][2]:
            relay(r - 1)
        if r >= 2:
            forward(r - 2)
    forward(ROW_CHUNKS - 2)
    forward(ROW_CHUNKS - 1)

    for r in range(ROW_CHUNKS):
        rows = rows_of(r)
        wait_bytes(kv.at[pl.ds((1 - C) * 16, 16), rows, :], fw_recv.at[r])
        wait_bytes(blocks(r, 16), fw_send.at[r])
        for j in range(2):
            is_self = jnp.logical_and(same, 2 * C + j == X)
            wait_sent(is_self, kvst.at[j, rows, :], kv_send0.at[r, j])
            wait_bytes(blocks(r, 4 if CHUNKS[r][2] else 7), kv_send.at[r, j])
        if CHUNKS[r][2]:
            for kind in range(2):
                wait_bytes(blocks(r, 3), hop_send.at[r, kind])
    wait_bytes(qx, q_recv.at[0])
    wait_bytes(dox, q_recv.at[1])
    for j in range(2):
        for c2 in range(NC):
            is_self = jnp.logical_and(2 * C + j == X, C == c2)
            wait_sent(is_self, qx.at[0], q_send.at[0, j, c2])
            wait_sent(is_self, dox.at[0], q_send.at[1, j, c2])


ANY_SPEC = pl.BlockSpec(memory_space=pl.ANY)
VMEM_SPEC = pl.BlockSpec(memory_space=pltpu.VMEM)
DMA = pltpu.SemaphoreType.DMA


def front(tokens, queries, out_grad, key_weight, value_weight, noise_codes):
    return pl.pallas_call(
        front_kernel,
        name="front",
        out_shape=(
            jax.ShapeDtypeStruct((NX, BLK, GROUP_COLS), BF),
            jax.ShapeDtypeStruct((NX, BLK, GROUP_COLS), BF),
            jax.ShapeDtypeStruct((BLOCKS, BLK, KV_W), BF),
        ),
        in_specs=[ANY_SPEC] * 6,
        out_specs=(ANY_SPEC,) * 3,
        scratch_shapes=[
            pltpu.VMEM((2, 1, BLK, KV_W), jnp.int32),
            pltpu.VMEM((2, BLK, HALF_D), BF),
            pltpu.VMEM((2, HALF_D, 2 * KV_W), BF),
            pltpu.VMEM((BLK, 2 * KV_W), F32),
            pltpu.VMEM((2, BLK, KV_W), BF),
            DMA,
            DMA((2, 2)),
            DMA,
            DMA((ROW_CHUNKS,)),
            DMA((ROW_CHUNKS,)),
            DMA((2, 2, 2)),
            DMA((2,)),
            DMA((ROW_CHUNKS, 2)),
            DMA((ROW_CHUNKS, 2)),
            DMA((ROW_CHUNKS, 3)),
            DMA((ROW_CHUNKS, 2)),
            DMA((ROW_CHUNKS,)),
            DMA((ROW_CHUNKS,)),
        ],
        compiler_params=pltpu.CompilerParams(
            collective_id=0, has_side_effects=True, vmem_limit_bytes=VMEM_GRANT
        ),
        cost_estimate=pl.CostEstimate(flops=10**9, bytes_accessed=16 * 2**20, transcendentals=0),
    )(tokens, queries, out_grad, key_weight, value_weight, noise_codes)


KEYS = 256
LEVELS = (8, 4, 2, 1)
ROWS = 4 * BLK


def attention_kernel(
    order, q, do, kv, dq_out, dkv_out,
    kvb, qs, dos, stb, dpb, dk, dv, dqt, dkvb, block_at, kv_sem, q_sem, do_sem, out_sem,
):
    Z = lax.rem(lax.axis_index("ctx"), NZ)

    def at_place(block):
        return pl.ds(pl.multiple_of(order[block] * BLK, BLK), BLK)

    def load(block, carry):
        pltpu.make_async_copy(kv.at[block], kvb.at[at_place(block), :], kv_sem).start()
        block_at[order[block]] = block
        return carry

    for x in range(NX):
        for h in range(4):
            cols, rows = pl.ds(h * HD, HD), pl.ds(h * BLK, BLK)
            pltpu.make_async_copy(q.at[x, :, cols], qs.at[x, rows, :], q_sem).start()
            pltpu.make_async_copy(do.at[x, :, cols], dos.at[x, rows, :], do_sem).start()
    lax.fori_loop(0, BLOCKS, load, 0)

    def clear(i, carry):
        rows = pl.ds(pl.multiple_of(i * 256, 256), 256)
        dk[rows, :] = jnp.zeros((256, HD), F32)
        dv[rows, :] = jnp.zeros((256, HD), F32)
        return carry

    lax.fori_loop(0, 16, clear, 0)
    wait_bytes(qs, q_sem)
    wait_bytes(dos, do_sem)
    wait_bytes(kvb, kv_sem)

    def run(count, body, carry):
        done = 0
        for units in LEVELS:
            times = (count - done) // units
            base = done

            def step(i, state, units=units, base=base):
                start = pl.multiple_of((base + i * units) * KEYS, KEYS)
                return body(pl.ds(start, units * KEYS), units * KEYS, state)

            carry = lax.fori_loop(0, times, step, carry)
            done = base + times * units
        return carry

    def fold(array, size, how):
        return how(array.reshape(size // 8, 8, ROWS), axis=0)

    def tile(x, carry):
        place = order[x * NZ + Z]
        last = place // 2
        qx = qs[x]
        dx = dos[x]

        def score_step(rows, size, top):
            st = lax.dot_general(kvb[rows, :HD], qx, NT, preferred_element_type=F32)
            stb[rows, :] = st
            return jnp.maximum(top, fold(st, size, jnp.max))

        top = run(last, score_step, jnp.full((8, ROWS), FLOOR_SCORE, F32))
        rows = pl.ds(pl.multiple_of(last * KEYS, KEYS), KEYS)
        st = lax.dot_general(kvb[rows, :HD], qx, NT, preferred_element_type=F32)
        key_places = last * KEYS + lax.broadcasted_iota(jnp.int32, (KEYS, ROWS), 0)
        query_places = place * BLK + lax.rem(lax.broadcasted_iota(jnp.int32, (KEYS, ROWS), 1), BLK)
        st = jnp.where(key_places <= query_places, st, FLOOR_SCORE)
        stb[rows, :] = st
        top = jnp.maximum(top, fold(st, KEYS, jnp.max))
        top = jnp.max(top, axis=0, keepdims=True) * SCALE_LOG2

        def weigh_step(rows, size, state):
            total, weighted = state
            weights = jnp.exp2(stb[rows, :] * SCALE_LOG2 - top)
            dpt = lax.dot_general(kvb[rows, HD:], dx, NT, preferred_element_type=F32)
            dpb[rows, :] = dpt
            stb[rows, :] = weights
            return total + fold(weights, size, jnp.sum), weighted + fold(weights * dpt, size, jnp.sum)

        zero = jnp.zeros((8, ROWS), F32)
        total, weighted = run(last + 1, weigh_step, (zero, zero))
        inverse = 1.0 / jnp.sum(total, axis=0, keepdims=True)
        delta = jnp.sum(weighted, axis=0, keepdims=True) * inverse
        dqt[...] = jnp.zeros((HD, ROWS), F32)

        def grad_step(rows, size, state):
            probs = stb[rows, :] * inverse
            low = probs.astype(BF)
            grads = (probs * (dpb[rows, :] - delta)).astype(BF)
            dv[rows, :] += lax.dot_general(low, dx, NN, preferred_element_type=F32)
            dk[rows, :] += lax.dot_general(grads, qx, NN, preferred_element_type=F32)
            dqt[...] += lax.dot_general(kvb[rows, :HD], grads, TN, preferred_element_type=F32)
            return state

        run(last + 1, grad_step, 0)
        dq = dqt[...].T
        for h in range(4):
            dq_out[x, :, h * HD : (h + 1) * HD] = (dq[h * BLK : (h + 1) * BLK, :] * SCALE).astype(BF)
        return carry

    lax.fori_loop(0, NX, tile, 0)

    def finish(i, carry):
        rows = pl.ds(pl.multiple_of(i * 256, 256), 256)
        dkvb[rows, :HD] = (dk[rows, :] * SCALE).astype(BF)
        dkvb[rows, HD:] = dv[rows, :].astype(BF)
        for j in range(2):
            block = block_at[2 * i + j]
            src = dkvb.at[pl.ds(pl.multiple_of(i * 256 + j * BLK, BLK), BLK), :]
            pltpu.make_async_copy(src, dkv_out.at[block // NZ, lax.rem(block, NZ)], out_sem).start()
        return carry

    lax.fori_loop(0, 16, finish, 0)
    wait_bytes(dkvb, out_sem)


def attention(block_order, qx, dox, kv):
    tokens = BLOCKS * BLK
    return pl.pallas_call(
        attention_kernel,
        name="attention",
        out_shape=(
            jax.ShapeDtypeStruct((NX, BLK, GROUP_COLS), BF),
            jax.ShapeDtypeStruct((NX, NZ, BLK, KV_W), BF),
        ),
        in_specs=[pl.BlockSpec(memory_space=pltpu.SMEM)] + [ANY_SPEC] * 3,
        out_specs=(VMEM_SPEC, ANY_SPEC),
        scratch_shapes=[
            pltpu.VMEM((tokens, KV_W), BF),
            pltpu.VMEM((NX, ROWS, HD), BF),
            pltpu.VMEM((NX, ROWS, HD), BF),
            pltpu.VMEM((tokens, ROWS), F32),
            pltpu.VMEM((tokens, ROWS), F32),
            pltpu.VMEM((tokens, HD), F32),
            pltpu.VMEM((tokens, HD), F32),
            pltpu.VMEM((HD, ROWS), F32),
            pltpu.VMEM((tokens, KV_W), BF),
            pltpu.SMEM((BLOCKS,), jnp.int32),
            DMA,
            DMA,
            DMA,
            DMA,
        ],
        compiler_params=pltpu.CompilerParams(vmem_limit_bytes=ATTENTION_GRANT),
        cost_estimate=pl.CostEstimate(flops=10**10, bytes_accessed=8 * 2**20, transcendentals=10**7),
    )(block_order, qx, dox, kv)


class Ring:
    def __init__(self, count, position, neighbour, own, slots, send_sems, recv_sems):
        self.count, self.position, self.neighbour, self.own = count, position, neighbour, own
        self.slots, self.send_sems, self.recv_sems = slots, send_sems, recv_sems
        self.steps = count // 2
        self.sent = []

    def chains(self, step):
        for way in range(2):
            for part in range(2):
                length = self.steps if way == part else self.steps - 1
                if step >= self.steps - length:
                    yield way, part, step == self.steps - length

    def step(self, step):
        for way, part, first in self.chains(step):
            sign = 1 if way == 0 else -1
            mine = self.own(part, sign * (self.steps - step))
            if first:
                src = mine
            else:
                src = self.slots.at[way, part, step - 1]
                wait_bytes(src, self.recv_sems.at[way, part, step - 1])
                src[...] = (src[...].astype(F32) + mine[...].astype(F32)).astype(BF)
            copy = remote(
                src,
                self.slots.at[way, part, step],
                self.send_sems.at[way, part, step],
                self.recv_sems.at[way, part, step],
                self.neighbour(sign),
            )
            copy.start()
            self.sent.append(copy)

    def result(self, part):
        total = self.own(part, 0)[...].astype(F32)
        for way in range(2):
            slot = self.slots.at[way, part, self.steps - 1]
            wait_bytes(slot, self.recv_sems.at[way, part, self.steps - 1])
            total += slot[...].astype(F32)
        return total.astype(BF)

    def finish(self):
        for copy in self.sent:
            copy.wait_send()


def span(start, size):
    return pl.ds(pl.multiple_of(start, 16), size)


HALF_ROWS = BLK // 2
RINGS = 4
RING_ROWS = BLK // RINGS
DELTAS = (4, 3, -3, 2, -2, 1, -1, 0)


def back_kernel(
    dq, dkv, tok, masks, query_grad, key_out, value_out,
    own, other, z1, home_src, raw, mbuf, tokq, tokt, preall, wa, wb, az, ra, ax, bx, rb, bz, fin, final,
    own_sem, mask_sem, ex_send, ex_recv, z1_send, z1_recv, home_send, home_recv, tok_send, tok_recv, dq_send, dq_recv,
    pre_send, pre_recv, pfw_send, pfw_recv, core_sem,
    az_send, az_recv, ax_send, ax_recv, bx_send, bx_recv, bz_send, bz_recv,
    fin_send, fin_recv, f2_send, f2_recv,
):
    X, Y, Z, C = here()
    head, low = Y // 2, lax.rem(Y, 2)
    unit_core = X // 2
    slot = lax.rem(X, 2)
    same = unit_core == C
    partner = device(X, Y, Z, 1 - C)
    beside = device(X, 2 * head + 1 - low, Z, C)
    seq = low * 2 + C

    load_own = pltpu.make_async_copy(dkv.at[pl.ds(C * 2, 2)], own, own_sem)
    load_own.start()
    load_mask = pltpu.make_async_copy(masks, mbuf, mask_sem)
    load_mask.start()

    def z_next(sign):
        return device(X, Y, around(Z + sign, NZ), C)

    def x_next(sign):
        return device(around(X + sign, NX), Y, Z, C)

    def y_next(by):
        return device(X, around(Y + by, NY), Z, C)

    ways = (1, 3, 2)
    i_mine = X + 4 * lax.rem(Z, 2)
    targets = [
        [(Y, 2 * around(head + which, 2) + lows, 4 * C + Z // 2, lax.rem(Z, 2)) for lows in range(2)]
        for which in range(2)
    ]

    def is_me(place):
        x, y, z, core = place
        return jnp.logical_and(jnp.logical_and(x == X, y == Y), jnp.logical_and(z == Z, core == C))

    is_final = [[is_me(target) for target in pair] for pair in targets]

    signal(partner)
    for xs in range(2):
        for cs in range(NC):
            @pl.when(jnp.logical_not(jnp.logical_and(2 * C + xs == X, C == cs)))
            def _(xs=xs, cs=cs):
                signal(device(2 * C + xs, Y, Z, cs))
    for sign in (1, -1):
        signal(z_next(sign))
        signal(x_next(sign))
    for cs in range(NC):
        signal(device(X, 2 * head + 1 - low, Z, cs))
    for by in ways:
        signal(y_next(by))
    signal(device(around(X + 2, NX), Y, Z, C))
    pl.semaphore_wait(pltpu.get_barrier_semaphore(), 15 - same.astype(jnp.int32))

    exchanges = {}
    for i, delta in enumerate(DELTAS):
        t = around(Z + delta, NZ)
        copy = remote(dkv.at[pl.ds((1 - C) * 2, 2), t], other.at[:, t], ex_send.at[i], ex_recv.at[i], partner)
        copy.start()
        exchanges[delta] = copy
    for xs in range(NX):
        cols = pl.ds(pl.multiple_of((slot * 8 + C * 4) * HD, GROUP_COLS), GROUP_COLS)
        is_self = jnp.logical_and(same, X == xs)
        send_or_copy(
            is_self, dq.at[xs], query_grad.at[0, :, cols], dq_send.at[xs], dq_recv, device(xs, Y, Z, unit_core)
        )
    for quarter in range(4):
        is_self = seq == quarter
        send_or_copy(
            is_self,
            tok.at[0, :, pl.ds(quarter * QUARTER, QUARTER)],
            tokq.at[seq],
            tok_send.at[quarter],
            tok_recv,
            device(X, 2 * head + quarter // 2, Z, quarter % 2),
        )

    load_own.wait()
    ready = set()

    def prepare(delta):
        if delta in ready:
            return
        ready.add(delta)
        t = around(Z + delta, NZ)
        exchanges[delta].wait_recv()
        for part in range(2):
            own[part, t] = (own[part, t].astype(F32) + other[part, t].astype(F32)).astype(BF)

    def own_part(i):
        def get(part, delta):
            prepare(4 if delta == -4 else delta)
            return own.at[part, around(Z + delta, NZ), pl.ds(i * RING_ROWS, RING_ROWS), :]

        return get

    rings = [Ring(NZ, Z, z_next, own_part(i), z1.at[i], z1_send.at[i], z1_recv.at[i]) for i in range(RINGS)]
    for step in range(NZ // 2):
        for ring in rings:
            ring.step(step)
    for half in range(2):
        rows = pl.ds(half * HALF_ROWS, HALF_ROWS)
        for i in range(half * RINGS // 2, (half + 1) * RINGS // 2):
            for part in range(2):
                home_src[part, i * RING_ROWS : (i + 1) * RING_ROWS, :] = rings[i].result(part)
        for part in range(2):
            xs = 2 * C + part
            is_self = jnp.logical_and(same, X == xs)
            send_or_copy(
                is_self,
                home_src.at[part, rows, :],
                raw.at[slot, rows, :],
                home_send.at[half, part],
                home_recv.at[half],
                device(xs, Y, Z, unit_core),
            )

    load_mask.wait()
    sends = []
    y_targets = (beside, y_next(around(2 * low - 1, NY)), y_next(2))
    y_places = ((head, 1 - low), (1 - head, 1 - low), (1 - head, low))

    def my_rows(half):
        return span(seq * BLK + half * HALF_ROWS, HALF_ROWS)

    for half in range(2):
        rows = pl.ds(half * HALF_ROWS, HALF_ROWS)
        wait_bytes(raw.at[:, rows, :], home_recv.at[half])
        for j in range(2):
            for what in range(2):
                mask = mbuf[what, 0, rows, j * HD : (j + 1) * HD] != 0
                piece = raw[j, rows, what * HD : (what + 1) * HD]
                first = (2 * j + what) * HD
                preall[head, my_rows(half), first : first + HD] = jnp.where(mask, piece, jnp.zeros_like(piece))
        mine = preall.at[head, my_rows(half), :]
        sends.append(remote(mine, mine, core_sem.at[half, 0], core_sem.at[half, 1], partner))
        sends[-1].start()
        for i in range(2):
            sends.append(remote(mine, mine, pre_send.at[half, i], pre_recv.at[half, i], y_targets[i]))
            sends[-1].start()
    for half in range(2):
        mine = preall.at[head, my_rows(half), :]
        sends.append(remote(mine, mine, pre_send.at[half, 2], pre_recv.at[half, 2], y_targets[2]))
        sends[-1].start()

    wait_bytes(tokq, tok_recv)
    for s in range(4):
        tokt[:, :, :, s * BLK : (s + 1) * BLK] = tokq[s].T.reshape(NZ, NX, 32, BLK)

    forwards = []

    def pass_on(i):
        place, lows = y_places[i]
        for half in range(2):
            piece = preall.at[place, span((lows * 2 + C) * BLK + half * HALF_ROWS, HALF_ROWS), :]
            wait_bytes(piece, pre_recv.at[half, i])
            copy = remote(piece, piece, pfw_send.at[half, i], pfw_recv.at[half, i], partner)
            copy.start()
            forwards.append(copy)
        return forwards[-2:]

    passed_on = [pass_on(0), pass_on(1)]
    for half in range(2):
        sends[half * 3].wait_recv()
    for copy in passed_on[0]:
        copy.wait_recv()

    made = set()

    def product(path, which, delta):
        if (path, which, delta) in made:
            return
        made.add((path, which, delta))
        cols = slice(path * KV_W, (path + 1) * KV_W)
        if path == 0:
            t = around(Z + delta, NZ)
            rows = tokt[t].reshape(128, 4 * BLK)
        else:
            t = around(X + delta, NX)
            rows = tokt[:, t].reshape(256, 4 * BLK)
        value = jnp.dot(rows, preall[around(head + which, 2), :, cols], preferred_element_type=F32).astype(BF)
        if path == 0:
            wa[which, t] = value.reshape(NX, 32, KV_W)
        else:
            wb[which, :, t] = value.reshape(NZ, 32, KV_W)

    def a_own(which):
        def get(part, delta):
            delta = 4 if delta == -4 else delta
            product(0, which, delta)
            return wa.at[which, around(Z + delta, NZ), pl.ds(part * 2, 2)]

        return get

    def b_own(which):
        def get(part, delta):
            delta = 2 if delta == -2 else delta
            product(1, which, delta)
            return wb.at[which, pl.ds(part * 4, 4), around(X + delta, NX)]

        return get

    a1 = [Ring(NZ, Z, z_next, a_own(s), az.at[s], az_send.at[s], az_recv.at[s]) for s in range(2)]
    b1 = [Ring(NX, X, x_next, b_own(s), bx.at[s], bx_send.at[s], bx_recv.at[s]) for s in range(2)]

    directs = []

    def direct(source, slots, send_sems, recv_sems, count, position, neighbour):
        deltas = sorted([d for d in range(1 - count // 2, count // 2 + 1) if d], key=lambda d: -abs(d))
        for delta in deltas:
            i = delta % count - 1
            src = source.at[around(position + delta, count)]
            copy = remote(src, slots.at[i], send_sems.at[i], recv_sems.at[i], neighbour(delta))
            copy.start()
            directs.append(copy)

    def collect(source, slots, recv_sems, count, position):
        total = source[position].astype(F32)
        for i in range(count - 1):
            wait_bytes(slots.at[i], recv_sems.at[i])
            total += slots[i].astype(F32)
        return total.astype(BF)

    def turn_a(which):
        for part in range(2):
            ra[which, part * 2 : (part + 1) * 2] = a1[which].result(part)
        direct(ra.at[which], ax.at[which], ax_send.at[which], ax_recv.at[which], NX, X, x_next)

    def turn_b(which):
        for part in range(2):
            rb[which, part * 4 : (part + 1) * 4] = b1[which].result(part)
        direct(rb.at[which], bz.at[which], bz_send.at[which], bz_recv.at[which], NZ, Z, z_next)

    def deliver(which):
        fin[which, :, KV_W:] = collect(rb.at[which], bz.at[which], bz_recv.at[which], NZ, Z)
        fin[which, :, :KV_W] = collect(ra.at[which], ax.at[which], ax_recv.at[which], NX, X)
        dst = final.at[span(i_mine * 32, 32), :]
        for lows in range(2):
            send_or_copy(
                is_final[which][lows],
                fin.at[which],
                dst,
                fin_send.at[which, lows],
                fin_recv,
                device(*targets[which][lows]),
            )

    a1[0].step(0)
    b1[0].step(0)
    passed_on.append(pass_on(2))
    a1[0].step(1)
    for copy in passed_on[1] + passed_on[2]:
        copy.wait_recv()
    a1[1].step(0)
    b1[1].step(0)
    b1[0].step(1)
    a1[0].step(2)
    a1[1].step(1)
    b1[1].step(1)
    turn_b(0)
    a1[0].step(3)
    a1[1].step(2)
    turn_a(0)
    turn_b(1)
    a1[1].step(3)
    deliver(0)
    turn_a(1)
    deliver(1)

    mine = final.at[span(C * BLK, BLK), :]
    wait_bytes(mine, fin_recv)
    to_partner = remote(mine, mine, f2_send, f2_recv, partner)
    to_partner.start()
    to_partner.wait_recv()
    for j in range(2):
        for what, out in ((0, key_out), (1, value_out)):
            first = (2 * j + what) * HD
            out[:, j * HD : (j + 1) * HD] = final[:, first : first + HD].astype(F32) * 0.25

    wait_bytes(query_grad, dq_recv)
    for copy in exchanges.values():
        copy.wait_send()
    for xs in range(NX):
        wait_sent(jnp.logical_and(same, X == xs), dq.at[xs], dq_send.at[xs])
    for quarter in range(4):
        wait_sent(seq == quarter, tokq.at[0], tok_send.at[quarter])
    for half in range(2):
        for part in range(2):
            wait_sent(
                jnp.logical_and(same, X == 2 * C + part),
                raw.at[part, pl.ds(half * HALF_ROWS, HALF_ROWS), :],
                home_send.at[half, part],
            )
    for copy in sends + forwards + [to_partner]:
        copy.wait_send()
    for ring in rings + a1 + b1:
        ring.finish()
    for copy in directs:
        copy.wait_send()
    for which in range(2):
        for lows in range(2):
            wait_sent(is_final[which][lows], fin.at[which], fin_send.at[which, lows])


def back(dq, dkv, tokens, clip_masks):
    wide = 2 * KV_W
    return pl.pallas_call(
        back_kernel,
        name="back",
        out_shape=(
            jax.ShapeDtypeStruct((1, BLK, 2048), BF),
            jax.ShapeDtypeStruct((256, KV_W), F32),
            jax.ShapeDtypeStruct((256, KV_W), F32),
        ),
        in_specs=[ANY_SPEC] * 4,
        out_specs=(ANY_SPEC, VMEM_SPEC, VMEM_SPEC),
        scratch_shapes=[
            pltpu.VMEM((2, NZ, BLK, KV_W), BF),
            pltpu.VMEM((2, NZ, BLK, KV_W), BF),
            pltpu.VMEM((RINGS, 2, 2, 4, RING_ROWS, KV_W), BF),
            pltpu.VMEM((2, BLK, KV_W), BF),
            pltpu.VMEM((2, BLK, KV_W), BF),
            pltpu.VMEM((2, 1, BLK, KV_W), jnp.int32),
            pltpu.VMEM((4, BLK, QUARTER), BF),
            pltpu.VMEM((NZ, NX, 32, 4 * BLK), BF),
            pltpu.VMEM((2, 4 * BLK, wide), BF),
            pltpu.VMEM((2, NZ, NX, 32, KV_W), BF),
            pltpu.VMEM((2, NZ, NX, 32, KV_W), BF),
            pltpu.VMEM((2, 2, 2, 4, 2, 32, KV_W), BF),
            pltpu.VMEM((2, NX, 32, KV_W), BF),
            pltpu.VMEM((2, NX - 1, 32, KV_W), BF),
            pltpu.VMEM((2, 2, 2, 2, 4, 32, KV_W), BF),
            pltpu.VMEM((2, NZ, 32, KV_W), BF),
            pltpu.VMEM((2, NZ - 1, 32, KV_W), BF),
            pltpu.VMEM((2, 32, wide), BF),
            pltpu.VMEM((256, wide), BF),
            DMA,
            DMA,
            DMA((8,)),
            DMA((8,)),
            DMA((RINGS, 2, 2, 4)),
            DMA((RINGS, 2, 2, 4)),
            DMA((2, 2)),
            DMA((2,)),
            DMA((4,)),
            DMA,
            DMA((4,)),
            DMA,
            DMA((2, 3)),
            DMA((2, 3)),
            DMA((2, 3)),
            DMA((2, 3)),
            DMA((2, 2)),
            DMA((2, 2, 2, 4)),
            DMA((2, 2, 2, 4)),
            DMA((2, NX - 1)),
            DMA((2, NX - 1)),
            DMA((2, 2, 2, 2)),
            DMA((2, 2, 2, 2)),
            DMA((2, NZ - 1)),
            DMA((2, NZ - 1)),
            DMA((2, 2)),
            DMA,
            DMA,
            DMA,
        ],
        compiler_params=pltpu.CompilerParams(
            collective_id=1, has_side_effects=True, vmem_limit_bytes=BACK_GRANT
        ),
        cost_estimate=pl.CostEstimate(flops=10**9, bytes_accessed=16 * 2**20, transcendentals=0),
    )(dq, dkv, tokens, clip_masks)


def on_device(
    tokens, queries, out_grad, key_weight, value_weight, noise_codes, clip_masks, block_order
):
    qx, dox, kv = front(tokens, queries, out_grad, key_weight, value_weight, noise_codes)
    dq, dkv = attention(block_order, qx, dox, kv)
    return back(dq, dkv, tokens, clip_masks)


def solution(mesh):
    placed = (
        P("dp", "ctx", "head"),
        P("dp", "ctx", "head"),
        P("dp", "ctx", "head"),
        P(None, "head"),
        P(None, "head"),
        P(None, "dp", "ctx", "head"),
        P(None, "dp", "ctx", "head"),
        P(),
    )
    return jax.shard_map(
        on_device,
        mesh=mesh,
        in_specs=placed,
        out_specs=(P("dp", "ctx", "head"), P("ctx", "head"), P("ctx", "head")),
        check_vma=False,
    )
```

```python
import functools
import math

import jax
import jax.numpy as jnp
from jax import lax
from jax.experimental import pallas as pl
from jax.experimental.pallas import tpu as pltpu
from jax.sharding import PartitionSpec as P

HD = 128
BLK = 128
NX, NY, NZ, NC = 4, 4, 8, 2
GROUP_COLS = 512
HALF_D = 4096
QUARTER = 1024
KV_W = 256
BLOCKS = 32
NOISE_STEP = 0.05
NOISE_MIDDLE = 7.5
SCALE = 1.0 / math.sqrt(HD)
SCALE_LOG2 = SCALE * math.log2(math.e)
FLOOR_SCORE = -1e30
BF = jnp.bfloat16
F32 = jnp.float32
MESH = pl.DeviceIdType.MESH
VMEM_GRANT = 62 * 2**20
ATTENTION_GRANT = 53 * 2**20
BACK_GRANT = 52 * 2**20
NT = (((1,), (1,)), ((), ()))
NN = (((1,), (0,)), ((), ()))
TN = (((0,), (0,)), ((), ()))


def here():
    ctx, head, dp = lax.axis_index("ctx"), lax.axis_index("head"), lax.axis_index("dp")
    return ctx // NZ, head * 2 + dp // 2, lax.rem(ctx, NZ), lax.rem(dp, 2)


def device(x, y, z, core):
    return {"ctx": x * NZ + z, "head": y // 2, "dp": lax.rem(y, 2) * 2 + core}


def around(value, count):
    return lax.rem(value + count, count)


def signal(target):
    pl.semaphore_signal(pltpu.get_barrier_semaphore(), inc=1, device_id=target, device_id_type=MESH)


def remote(src, dst, send_sem, recv_sem, target):
    return pltpu.make_async_remote_copy(
        src_ref=src, dst_ref=dst, send_sem=send_sem, recv_sem=recv_sem, device_id=target, device_id_type=MESH
    )


def wait_bytes(ref, sem):
    pltpu.make_async_copy(ref, ref, sem).wait()


def send_or_copy(is_self, src, dst, send_sem, recv_sem, target):
    @pl.when(is_self)
    def _():
        pltpu.make_async_copy(src, dst, recv_sem).start()

    @pl.when(jnp.logical_not(is_self))
    def _():
        remote(src, dst, send_sem, recv_sem, target).start()


def wait_sent(is_self, ref, send_sem):
    @pl.when(jnp.logical_not(is_self))
    def _():
        wait_bytes(ref, send_sem)


CHUNKS = ((0, 16, True), (16, 32, True), (48, 32, True), (80, 32, True), (112, 16, False))
IN_FLIGHT = 2
ROW_CHUNKS = len(CHUNKS)


def front_kernel(
    tok, q, do, kw, vw, codes_in, qx, dox, kv,
    codes, xbuf, wbuf, acc, kvst,
    codes_sem, w_sem, own_sem, tok_send, tok_recv, q_send, q_recv, kv_send, kv_send0, kv_recv, hop_send, fw_send, fw_recv,
):
    X, Y, Z, C = here()
    head = Y // 2
    unit_core = X // 2
    same = unit_core == C
    peer = device(X, around(Y + 2, NY), Z, C)
    partner = device(X, Y, Z, 1 - C)

    signal(peer)
    signal(partner)
    for xs in range(NX):
        @pl.when(jnp.logical_not(jnp.logical_and(same, X == xs)))
        def _(xs=xs):
            signal(device(xs, Y, Z, unit_core))
    for delta in (1, -1, 2, -2):
        zs = around(Z + delta, NZ)
        signal(device(X, Y, zs, C))
        for part in range(2):
            signal(device(2 * C + part, Y, zs, unit_core))
    loads = [pltpu.make_async_copy(codes_in, codes, codes_sem)]
    for half in range(2):
        rows = pl.ds(half * HALF_D, HALF_D)
        loads.append(pltpu.make_async_copy(kw.at[rows, :], wbuf.at[half, :, pl.ds(0, KV_W)], w_sem.at[half, 0]))
        loads.append(pltpu.make_async_copy(vw.at[rows, :], wbuf.at[half, :, pl.ds(KV_W, KV_W)], w_sem.at[half, 1]))
    own_x = pltpu.make_async_copy(tok.at[0], xbuf.at[head], own_sem)
    own_x.start()
    for load in loads:
        load.start()

    pl.semaphore_wait(pltpu.get_barrier_semaphore(), 18 - same.astype(jnp.int32))

    def token_copy(r):
        rows = pl.ds(CHUNKS[r][0], CHUNKS[r][1])
        return remote(tok.at[0, rows, :], xbuf.at[head, rows, :], tok_send.at[r], tok_recv.at[r], peer)

    for r in range(IN_FLIGHT):
        token_copy(r).start()
    for j in range(2):
        for c2 in range(NC):
            cols = pl.ds((j * 8 + c2 * 4) * HD, GROUP_COLS)
            target = device(2 * C + j, Y, Z, c2)
            is_self = jnp.logical_and(2 * C + j == X, C == c2)
            send_or_copy(is_self, q.at[0, :, cols], qx.at[X], q_send.at[0, j, c2], q_recv.at[0], target)
            send_or_copy(is_self, do.at[0, :, cols], dox.at[X], q_send.at[1, j, c2], q_recv.at[1], target)

    own_x.wait()
    for load in loads:
        load.wait()
    acc[...] = jnp.dot(xbuf[head], wbuf[head], preferred_element_type=F32)

    mine = X * NZ + Z

    def rows_of(r):
        return pl.ds(CHUNKS[r][0], CHUNKS[r][1])

    def blocks(r, count):
        return kv.at[pl.ds(C * 16, count), rows_of(r), :]

    def spread(r):
        rows = rows_of(r)
        deltas = (2, -2, 1, -1) if CHUNKS[r][2] else (4, 3, -3, 2, -2, 1, -1)
        for j in range(2):
            src = kvst.at[j, rows, :]
            dst = kv.at[mine, rows, :]
            for delta in deltas:
                kind = {2: 0, -2: 1}.get(delta, 2) if CHUNKS[r][2] else 2
                target = device(2 * C + j, Y, around(Z + delta, NZ), unit_core)
                remote(src, dst, kv_send.at[r, j], kv_recv.at[r, kind], target).start()
            is_self = jnp.logical_and(same, 2 * C + j == X)
            send_or_copy(is_self, src, dst, kv_send0.at[r, j], kv_recv.at[r, 2], device(2 * C + j, Y, Z, unit_core))

    def relay(r):
        rows = rows_of(r)
        for kind, sign in ((0, 1), (1, -1)):
            wait_bytes(blocks(r, 2), kv_recv.at[r, kind])
            source = around(Z - 2 * sign, NZ)
            for part in range(2):
                piece = kv.at[(2 * C + part) * NZ + source, rows, :]
                for far in (2, 1) if part == kind else (1,):
                    target = device(X, Y, around(Z + sign * far, NZ), C)
                    remote(piece, piece, hop_send.at[r, kind], kv_recv.at[r, 2], target).start()

    def forward(r):
        wait_bytes(blocks(r, 12 if CHUNKS[r][2] else 16), kv_recv.at[r, 2])
        whole = blocks(r, 16)
        remote(whole, whole, fw_send.at[r], fw_recv.at[r], partner).start()

    for r in range(ROW_CHUNKS):
        rows = rows_of(r)
        wait_bytes(xbuf.at[1 - head, rows, :], tok_recv.at[r])
        token_copy(r).wait_send()
        if r + IN_FLIGHT < ROW_CHUNKS:
            token_copy(r + IN_FLIGHT).start()
        both = acc[rows, :] + jnp.dot(xbuf[1 - head, rows, :], wbuf[1 - head], preferred_element_type=F32)
        for what in range(2):
            shift = NOISE_STEP * (codes[what, 0, rows, :].astype(F32) - NOISE_MIDDLE)
            value = (both[:, what * KV_W : (what + 1) * KV_W] + shift).astype(BF)
            for j in range(2):
                kvst[j, rows, what * HD : (what + 1) * HD] = value[:, j * HD : (j + 1) * HD]
        spread(r)
        if r >= 1 and CHUNKS[r - 1][2]:
            relay(r - 1)
        if r >= 2:
            forward(r - 2)
    forward(ROW_CHUNKS - 2)
    forward(ROW_CHUNKS - 1)

    for r in range(ROW_CHUNKS):
        rows = rows_of(r)
        wait_bytes(kv.at[pl.ds((1 - C) * 16, 16), rows, :], fw_recv.at[r])
        wait_bytes(blocks(r, 16), fw_send.at[r])
        for j in range(2):
            is_self = jnp.logical_and(same, 2 * C + j == X)
            wait_sent(is_self, kvst.at[j, rows, :], kv_send0.at[r, j])
            wait_bytes(blocks(r, 4 if CHUNKS[r][2] else 7), kv_send.at[r, j])
        if CHUNKS[r][2]:
            for kind in range(2):
                wait_bytes(blocks(r, 3), hop_send.at[r, kind])
    wait_bytes(qx, q_recv.at[0])
    wait_bytes(dox, q_recv.at[1])
    for j in range(2):
        for c2 in range(NC):
            is_self = jnp.logical_and(2 * C + j == X, C == c2)
            wait_sent(is_self, qx.at[0], q_send.at[0, j, c2])
            wait_sent(is_self, dox.at[0], q_send.at[1, j, c2])


ANY_SPEC = pl.BlockSpec(memory_space=pl.ANY)
VMEM_SPEC = pl.BlockSpec(memory_space=pltpu.VMEM)
DMA = pltpu.SemaphoreType.DMA


def front(tokens, queries, out_grad, key_weight, value_weight, noise_codes):
    return pl.pallas_call(
        front_kernel,
        name="front",
        out_shape=(
            jax.ShapeDtypeStruct((NX, BLK, GROUP_COLS), BF),
            jax.ShapeDtypeStruct((NX, BLK, GROUP_COLS), BF),
            jax.ShapeDtypeStruct((BLOCKS, BLK, KV_W), BF),
        ),
        in_specs=[ANY_SPEC] * 6,
        out_specs=(ANY_SPEC,) * 3,
        scratch_shapes=[
            pltpu.VMEM((2, 1, BLK, KV_W), jnp.int32),
            pltpu.VMEM((2, BLK, HALF_D), BF),
            pltpu.VMEM((2, HALF_D, 2 * KV_W), BF),
            pltpu.VMEM((BLK, 2 * KV_W), F32),
            pltpu.VMEM((2, BLK, KV_W), BF),
            DMA,
            DMA((2, 2)),
            DMA,
            DMA((ROW_CHUNKS,)),
            DMA((ROW_CHUNKS,)),
            DMA((2, 2, 2)),
            DMA((2,)),
            DMA((ROW_CHUNKS, 2)),
            DMA((ROW_CHUNKS, 2)),
            DMA((ROW_CHUNKS, 3)),
            DMA((ROW_CHUNKS, 2)),
            DMA((ROW_CHUNKS,)),
            DMA((ROW_CHUNKS,)),
        ],
        compiler_params=pltpu.CompilerParams(
            collective_id=0, has_side_effects=True, vmem_limit_bytes=VMEM_GRANT
        ),
        cost_estimate=pl.CostEstimate(flops=10**9, bytes_accessed=16 * 2**20, transcendentals=0),
    )(tokens, queries, out_grad, key_weight, value_weight, noise_codes)


KEYS = 256
LEVELS = (8, 4, 2, 1)
ROWS = 4 * BLK


def attention_kernel(
    order, q, do, kv, dq_out, dkv_out,
    kvb, qs, dos, stb, dpb, dk, dv, dqt, dkvb, block_at, kv_sem, q_sem, do_sem, out_sem,
):
    Z = lax.rem(lax.axis_index("ctx"), NZ)

    def at_place(block):
        return pl.ds(pl.multiple_of(order[block] * BLK, BLK), BLK)

    def load(block, carry):
        pltpu.make_async_copy(kv.at[block], kvb.at[at_place(block), :], kv_sem).start()
        block_at[order[block]] = block
        return carry

    for x in range(NX):
        for h in range(4):
            cols, rows = pl.ds(h * HD, HD), pl.ds(h * BLK, BLK)
            pltpu.make_async_copy(q.at[x, :, cols], qs.at[x, rows, :], q_sem).start()
            pltpu.make_async_copy(do.at[x, :, cols], dos.at[x, rows, :], do_sem).start()
    lax.fori_loop(0, BLOCKS, load, 0)

    def clear(i, carry):
        rows = pl.ds(pl.multiple_of(i * 256, 256), 256)
        dk[rows, :] = jnp.zeros((256, HD), F32)
        dv[rows, :] = jnp.zeros((256, HD), F32)
        return carry

    lax.fori_loop(0, 16, clear, 0)
    wait_bytes(qs, q_sem)
    wait_bytes(dos, do_sem)
    wait_bytes(kvb, kv_sem)

    def run(count, body, carry):
        done = 0
        for units in LEVELS:
            times = (count - done) // units
            base = done

            def step(i, state, units=units, base=base):
                start = pl.multiple_of((base + i * units) * KEYS, KEYS)
                return body(pl.ds(start, units * KEYS), units * KEYS, state)

            carry = lax.fori_loop(0, times, step, carry)
            done = base + times * units
        return carry

    def fold(array, size, how):
        return how(array.reshape(size // 8, 8, ROWS), axis=0)

    def tile(x, carry):
        place = order[x * NZ + Z]
        last = place // 2
        qx = qs[x]
        dx = dos[x]

        def score_step(rows, size, top):
            st = lax.dot_general(kvb[rows, :HD], qx, NT, preferred_element_type=F32)
            stb[rows, :] = st
            return jnp.maximum(top, fold(st, size, jnp.max))

        top = run(last, score_step, jnp.full((8, ROWS), FLOOR_SCORE, F32))
        rows = pl.ds(pl.multiple_of(last * KEYS, KEYS), KEYS)
        st = lax.dot_general(kvb[rows, :HD], qx, NT, preferred_element_type=F32)
        key_places = last * KEYS + lax.broadcasted_iota(jnp.int32, (KEYS, ROWS), 0)
        query_places = place * BLK + lax.rem(lax.broadcasted_iota(jnp.int32, (KEYS, ROWS), 1), BLK)
        st = jnp.where(key_places <= query_places, st, FLOOR_SCORE)
        stb[rows, :] = st
        top = jnp.maximum(top, fold(st, KEYS, jnp.max))
        top = jnp.max(top, axis=0, keepdims=True) * SCALE_LOG2

        def weigh_step(rows, size, state):
            total, weighted = state
            weights = jnp.exp2(stb[rows, :] * SCALE_LOG2 - top)
            dpt = lax.dot_general(kvb[rows, HD:], dx, NT, preferred_element_type=F32)
            dpb[rows, :] = dpt
            stb[rows, :] = weights
            return total + fold(weights, size, jnp.sum), weighted + fold(weights * dpt, size, jnp.sum)

        zero = jnp.zeros((8, ROWS), F32)
        total, weighted = run(last + 1, weigh_step, (zero, zero))
        inverse = 1.0 / jnp.sum(total, axis=0, keepdims=True)
        delta = jnp.sum(weighted, axis=0, keepdims=True) * inverse
        dqt[...] = jnp.zeros((HD, ROWS), F32)

        def grad_step(rows, size, state):
            probs = stb[rows, :] * inverse
            low = probs.astype(BF)
            grads = (probs * (dpb[rows, :] - delta)).astype(BF)
            dv[rows, :] += lax.dot_general(low, dx, NN, preferred_element_type=F32)
            dk[rows, :] += lax.dot_general(grads, qx, NN, preferred_element_type=F32)
            dqt[...] += lax.dot_general(kvb[rows, :HD], grads, TN, preferred_element_type=F32)
            return state

        run(last + 1, grad_step, 0)
        dq = dqt[...].T
        for h in range(4):
            dq_out[x, :, h * HD : (h + 1) * HD] = (dq[h * BLK : (h + 1) * BLK, :] * SCALE).astype(BF)
        return carry

    lax.fori_loop(0, NX, tile, 0)

    def finish(i, carry):
        rows = pl.ds(pl.multiple_of(i * 256, 256), 256)
        dkvb[rows, :HD] = (dk[rows, :] * SCALE).astype(BF)
        dkvb[rows, HD:] = dv[rows, :].astype(BF)
        for j in range(2):
            block = block_at[2 * i + j]
            src = dkvb.at[pl.ds(pl.multiple_of(i * 256 + j * BLK, BLK), BLK), :]
            pltpu.make_async_copy(src, dkv_out.at[block // NZ, lax.rem(block, NZ)], out_sem).start()
        return carry

    lax.fori_loop(0, 16, finish, 0)
    wait_bytes(dkvb, out_sem)


def attention(block_order, qx, dox, kv):
    tokens = BLOCKS * BLK
    return pl.pallas_call(
        attention_kernel,
        name="attention",
        out_shape=(
            jax.ShapeDtypeStruct((NX, BLK, GROUP_COLS), BF),
            jax.ShapeDtypeStruct((NX, NZ, BLK, KV_W), BF),
        ),
        in_specs=[pl.BlockSpec(memory_space=pltpu.SMEM)] + [ANY_SPEC] * 3,
        out_specs=(VMEM_SPEC, ANY_SPEC),
        scratch_shapes=[
            pltpu.VMEM((tokens, KV_W), BF),
            pltpu.VMEM((NX, ROWS, HD), BF),
            pltpu.VMEM((NX, ROWS, HD), BF),
            pltpu.VMEM((tokens, ROWS), F32),
            pltpu.VMEM((tokens, ROWS), F32),
            pltpu.VMEM((tokens, HD), F32),
            pltpu.VMEM((tokens, HD), F32),
            pltpu.VMEM((HD, ROWS), F32),
            pltpu.VMEM((tokens, KV_W), BF),
            pltpu.SMEM((BLOCKS,), jnp.int32),
            DMA,
            DMA,
            DMA,
            DMA,
        ],
        compiler_params=pltpu.CompilerParams(vmem_limit_bytes=ATTENTION_GRANT),
        cost_estimate=pl.CostEstimate(flops=10**10, bytes_accessed=8 * 2**20, transcendentals=10**7),
    )(block_order, qx, dox, kv)


class Ring:
    def __init__(self, count, position, neighbour, own, slots, send_sems, recv_sems):
        self.count, self.position, self.neighbour, self.own = count, position, neighbour, own
        self.slots, self.send_sems, self.recv_sems = slots, send_sems, recv_sems
        self.steps = count // 2
        self.sent = []

    def chains(self, step):
        for way in range(2):
            for part in range(2):
                length = self.steps if way == part else self.steps - 1
                if step >= self.steps - length:
                    yield way, part, step == self.steps - length

    def step(self, step):
        for way, part, first in self.chains(step):
            sign = 1 if way == 0 else -1
            mine = self.own(part, sign * (self.steps - step))
            if first:
                src = mine
            else:
                src = self.slots.at[way, part, step - 1]
                wait_bytes(src, self.recv_sems.at[way, part, step - 1])
                src[...] = (src[...].astype(F32) + mine[...].astype(F32)).astype(BF)
            copy = remote(
                src,
                self.slots.at[way, part, step],
                self.send_sems.at[way, part, step],
                self.recv_sems.at[way, part, step],
                self.neighbour(sign),
            )
            copy.start()
            self.sent.append(copy)

    def result(self, part):
        total = self.own(part, 0)[...].astype(F32)
        for way in range(2):
            slot = self.slots.at[way, part, self.steps - 1]
            wait_bytes(slot, self.recv_sems.at[way, part, self.steps - 1])
            total += slot[...].astype(F32)
        return total.astype(BF)

    def finish(self):
        for copy in self.sent:
            copy.wait_send()


def span(start, size):
    return pl.ds(pl.multiple_of(start, 16), size)


HALF_ROWS = BLK // 2
RINGS = 4
RING_ROWS = BLK // RINGS
DELTAS = (4, 3, -3, 2, -2, 1, -1, 0)


def back_kernel(
    dq, dkv, tok, masks, query_grad, key_out, value_out,
    own, other, z1, home_src, raw, mbuf, tokq, tokt, preall, wa, wb, az, ra, ax, bx, rb, bz, fin, final,
    own_sem, mask_sem, ex_send, ex_recv, z1_send, z1_recv, home_send, home_recv, tok_send, tok_recv, dq_send, dq_recv,
    pre_send, pre_recv, pfw_send, pfw_recv, core_sem,
    az_send, az_recv, ax_send, ax_recv, bx_send, bx_recv, bz_send, bz_recv,
    fin_send, fin_recv, f2_send, f2_recv,
):
    X, Y, Z, C = here()
    head, low = Y // 2, lax.rem(Y, 2)
    unit_core = X // 2
    slot = lax.rem(X, 2)
    same = unit_core == C
    partner = device(X, Y, Z, 1 - C)
    beside = device(X, 2 * head + 1 - low, Z, C)
    seq = low * 2 + C

    def z_next(sign):
        return device(X, Y, around(Z + sign, NZ), C)

    def x_next(sign):
        return device(around(X + sign, NX), Y, Z, C)

    def y_next(by):
        return device(X, around(Y + by, NY), Z, C)

    ways = (1, 3, 2)
    i_mine = X + 4 * lax.rem(Z, 2)
    targets = [
        [(Y, 2 * around(head + which, 2) + lows, 4 * C + Z // 2, lax.rem(Z, 2)) for lows in range(2)]
        for which in range(2)
    ]

    def is_me(place):
        x, y, z, core = place
        return jnp.logical_and(jnp.logical_and(x == X, y == Y), jnp.logical_and(z == Z, core == C))

    is_final = [[is_me(target) for target in pair] for pair in targets]

    signal(partner)
    for xs in range(2):
        for cs in range(NC):
            @pl.when(jnp.logical_not(jnp.logical_and(2 * C + xs == X, C == cs)))
            def _(xs=xs, cs=cs):
                signal(device(2 * C + xs, Y, Z, cs))
    for sign in (1, -1):
        signal(z_next(sign))
        signal(x_next(sign))
    for cs in range(NC):
        signal(device(X, 2 * head + 1 - low, Z, cs))
    for by in ways:
        signal(y_next(by))
    signal(device(around(X + 2, NX), Y, Z, C))
    load_own = pltpu.make_async_copy(dkv.at[pl.ds(C * 2, 2)], own, own_sem)
    load_own.start()
    load_mask = pltpu.make_async_copy(masks, mbuf, mask_sem)
    load_mask.start()
    pl.semaphore_wait(pltpu.get_barrier_semaphore(), 15 - same.astype(jnp.int32))

    exchanges = {}
    for i, delta in enumerate(DELTAS):
        t = around(Z + delta, NZ)
        copy = remote(dkv.at[pl.ds((1 - C) * 2, 2), t], other.at[:, t], ex_send.at[i], ex_recv.at[i], partner)
        copy.start()
        exchanges[delta] = copy
    for xs in range(NX):
        cols = pl.ds(pl.multiple_of((slot * 8 + C * 4) * HD, GROUP_COLS), GROUP_COLS)
        is_self = jnp.logical_and(same, X == xs)
        send_or_copy(
            is_self, dq.at[xs], query_grad.at[0, :, cols], dq_send.at[xs], dq_recv, device(xs, Y, Z, unit_core)
        )
    for quarter in range(4):
        is_self = seq == quarter
        send_or_copy(
            is_self,
            tok.at[0, :, pl.ds(quarter * QUARTER, QUARTER)],
            tokq.at[seq],
            tok_send.at[quarter],
            tok_recv,
            device(X, 2 * head + quarter // 2, Z, quarter % 2),
        )

    load_own.wait()
    ready = set()

    def prepare(delta):
        if delta in ready:
            return
        ready.add(delta)
        t = around(Z + delta, NZ)
        exchanges[delta].wait_recv()
        for part in range(2):
            own[part, t] = (own[part, t].astype(F32) + other[part, t].astype(F32)).astype(BF)

    def own_part(i):
        def get(part, delta):
            prepare(4 if delta == -4 else delta)
            return own.at[part, around(Z + delta, NZ), pl.ds(i * RING_ROWS, RING_ROWS), :]

        return get

    rings = [Ring(NZ, Z, z_next, own_part(i), z1.at[i], z1_send.at[i], z1_recv.at[i]) for i in range(RINGS)]
    for step in range(NZ // 2):
        for ring in rings:
            ring.step(step)
    for half in range(2):
        rows = pl.ds(half * HALF_ROWS, HALF_ROWS)
        for i in range(half * RINGS // 2, (half + 1) * RINGS // 2):
            for part in range(2):
                home_src[part, i * RING_ROWS : (i + 1) * RING_ROWS, :] = rings[i].result(part)
        for part in range(2):
            xs = 2 * C + part
            is_self = jnp.logical_and(same, X == xs)
            send_or_copy(
                is_self,
                home_src.at[part, rows, :],
                raw.at[slot, rows, :],
                home_send.at[half, part],
                home_recv.at[half],
                device(xs, Y, Z, unit_core),
            )

    load_mask.wait()
    sends = []
    y_targets = (beside, y_next(around(2 * low - 1, NY)), y_next(2))
    y_places = ((head, 1 - low), (1 - head, 1 - low), (1 - head, low))

    def my_rows(half):
        return span(seq * BLK + half * HALF_ROWS, HALF_ROWS)

    for half in range(2):
        rows = pl.ds(half * HALF_ROWS, HALF_ROWS)
        wait_bytes(raw.at[:, rows, :], home_recv.at[half])
        for j in range(2):
            for what in range(2):
                mask = mbuf[what, 0, rows, j * HD : (j + 1) * HD] != 0
                piece = raw[j, rows, what * HD : (what + 1) * HD]
                first = (2 * j + what) * HD
                preall[head, my_rows(half), first : first + HD] = jnp.where(mask, piece, jnp.zeros_like(piece))
        mine = preall.at[head, my_rows(half), :]
        sends.append(remote(mine, mine, core_sem.at[half, 0], core_sem.at[half, 1], partner))
        sends[-1].start()
        for i in range(2):
            sends.append(remote(mine, mine, pre_send.at[half, i], pre_recv.at[half, i], y_targets[i]))
            sends[-1].start()
    for half in range(2):
        mine = preall.at[head, my_rows(half), :]
        sends.append(remote(mine, mine, pre_send.at[half, 2], pre_recv.at[half, 2], y_targets[2]))
        sends[-1].start()

    wait_bytes(tokq, tok_recv)
    for s in range(4):
        tokt[:, :, :, s * BLK : (s + 1) * BLK] = tokq[s].T.reshape(NZ, NX, 32, BLK)

    forwards = []

    def pass_on(i):
        place, lows = y_places[i]
        for half in range(2):
            piece = preall.at[place, span((lows * 2 + C) * BLK + half * HALF_ROWS, HALF_ROWS), :]
            wait_bytes(piece, pre_recv.at[half, i])
            copy = remote(piece, piece, pfw_send.at[half, i], pfw_recv.at[half, i], partner)
            copy.start()
            forwards.append(copy)
        return forwards[-2:]

    passed_on = [pass_on(0), pass_on(1)]
    for half in range(2):
        sends[half * 3].wait_recv()
    for copy in passed_on[0]:
        copy.wait_recv()

    made = set()

    def product(path, which, delta):
        if (path, which, delta) in made:
            return
        made.add((path, which, delta))
        cols = slice(path * KV_W, (path + 1) * KV_W)
        if path == 0:
            t = around(Z + delta, NZ)
            rows = tokt[t].reshape(128, 4 * BLK)
        else:
            t = around(X + delta, NX)
            rows = tokt[:, t].reshape(256, 4 * BLK)
        value = jnp.dot(rows, preall[around(head + which, 2), :, cols], preferred_element_type=F32).astype(BF)
        if path == 0:
            wa[which, t] = value.reshape(NX, 32, KV_W)
        else:
            wb[which, :, t] = value.reshape(NZ, 32, KV_W)

    def a_own(which):
        def get(part, delta):
            delta = 4 if delta == -4 else delta
            product(0, which, delta)
            return wa.at[which, around(Z + delta, NZ), pl.ds(part * 2, 2)]

        return get

    def b_own(which):
        def get(part, delta):
            delta = 2 if delta == -2 else delta
            product(1, which, delta)
            return wb.at[which, pl.ds(part * 4, 4), around(X + delta, NX)]

        return get

    a1 = [Ring(NZ, Z, z_next, a_own(s), az.at[s], az_send.at[s], az_recv.at[s]) for s in range(2)]
    b1 = [Ring(NX, X, x_next, b_own(s), bx.at[s], bx_send.at[s], bx_recv.at[s]) for s in range(2)]

    directs = []

    def direct(source, slots, send_sems, recv_sems, count, position, neighbour):
        deltas = sorted([d for d in range(1 - count // 2, count // 2 + 1) if d], key=lambda d: -abs(d))
        for delta in deltas:
            i = delta % count - 1
            src = source.at[around(position + delta, count)]
            copy = remote(src, slots.at[i], send_sems.at[i], recv_sems.at[i], neighbour(delta))
            copy.start()
            directs.append(copy)

    def collect(source, slots, recv_sems, count, position):
        total = source[position].astype(F32)
        for i in range(count - 1):
            wait_bytes(slots.at[i], recv_sems.at[i])
            total += slots[i].astype(F32)
        return total.astype(BF)

    def turn_a(which):
        for part in range(2):
            ra[which, part * 2 : (part + 1) * 2] = a1[which].result(part)
        direct(ra.at[which], ax.at[which], ax_send.at[which], ax_recv.at[which], NX, X, x_next)

    def turn_b(which):
        for part in range(2):
            rb[which, part * 4 : (part + 1) * 4] = b1[which].result(part)
        direct(rb.at[which], bz.at[which], bz_send.at[which], bz_recv.at[which], NZ, Z, z_next)

    def deliver(which):
        fin[which, :, KV_W:] = collect(rb.at[which], bz.at[which], bz_recv.at[which], NZ, Z)
        fin[which, :, :KV_W] = collect(ra.at[which], ax.at[which], ax_recv.at[which], NX, X)
        dst = final.at[span(i_mine * 32, 32), :]
        for lows in range(2):
            send_or_copy(
                is_final[which][lows],
                fin.at[which],
                dst,
                fin_send.at[which, lows],
                fin_recv,
                device(*targets[which][lows]),
            )

    a1[0].step(0)
    passed_on.append(pass_on(2))
    a1[0].step(1)
    for copy in passed_on[1] + passed_on[2]:
        copy.wait_recv()
    a1[1].step(0)
    b1[0].step(0)
    b1[1].step(0)
    a1[0].step(2)
    a1[1].step(1)
    b1[0].step(1)
    a1[0].step(3)
    a1[1].step(2)
    b1[1].step(1)
    turn_b(0)
    turn_a(0)
    a1[1].step(3)
    turn_b(1)
    turn_a(1)
    deliver(0)
    deliver(1)

    mine = final.at[span(C * BLK, BLK), :]
    wait_bytes(mine, fin_recv)
    to_partner = remote(mine, mine, f2_send, f2_recv, partner)
    to_partner.start()
    to_partner.wait_recv()
    for j in range(2):
        for what, out in ((0, key_out), (1, value_out)):
            first = (2 * j + what) * HD
            out[:, j * HD : (j + 1) * HD] = final[:, first : first + HD].astype(F32) * 0.25

    wait_bytes(query_grad, dq_recv)
    for copy in exchanges.values():
        copy.wait_send()
    for xs in range(NX):
        wait_sent(jnp.logical_and(same, X == xs), dq.at[xs], dq_send.at[xs])
    for quarter in range(4):
        wait_sent(seq == quarter, tokq.at[0], tok_send.at[quarter])
    for half in range(2):
        for part in range(2):
            wait_sent(
                jnp.logical_and(same, X == 2 * C + part),
                raw.at[part, pl.ds(half * HALF_ROWS, HALF_ROWS), :],
                home_send.at[half, part],
            )
    for copy in sends + forwards + [to_partner]:
        copy.wait_send()
    for ring in rings + a1 + b1:
        ring.finish()
    for copy in directs:
        copy.wait_send()
    for which in range(2):
        for lows in range(2):
            wait_sent(is_final[which][lows], fin.at[which], fin_send.at[which, lows])


def back(dq, dkv, tokens, clip_masks):
    wide = 2 * KV_W
    return pl.pallas_call(
        back_kernel,
        name="back",
        out_shape=(
            jax.ShapeDtypeStruct((1, BLK, 2048), BF),
            jax.ShapeDtypeStruct((256, KV_W), F32),
            jax.ShapeDtypeStruct((256, KV_W), F32),
        ),
        in_specs=[ANY_SPEC] * 4,
        out_specs=(ANY_SPEC, VMEM_SPEC, VMEM_SPEC),
        scratch_shapes=[
            pltpu.VMEM((2, NZ, BLK, KV_W), BF),
            pltpu.VMEM((2, NZ, BLK, KV_W), BF),
            pltpu.VMEM((RINGS, 2, 2, 4, RING_ROWS, KV_W), BF),
            pltpu.VMEM((2, BLK, KV_W), BF),
            pltpu.VMEM((2, BLK, KV_W), BF),
            pltpu.VMEM((2, 1, BLK, KV_W), jnp.int32),
            pltpu.VMEM((4, BLK, QUARTER), BF),
            pltpu.VMEM((NZ, NX, 32, 4 * BLK), BF),
            pltpu.VMEM((2, 4 * BLK, wide), BF),
            pltpu.VMEM((2, NZ, NX, 32, KV_W), BF),
            pltpu.VMEM((2, NZ, NX, 32, KV_W), BF),
            pltpu.VMEM((2, 2, 2, 4, 2, 32, KV_W), BF),
            pltpu.VMEM((2, NX, 32, KV_W), BF),
            pltpu.VMEM((2, NX - 1, 32, KV_W), BF),
            pltpu.VMEM((2, 2, 2, 2, 4, 32, KV_W), BF),
            pltpu.VMEM((2, NZ, 32, KV_W), BF),
            pltpu.VMEM((2, NZ - 1, 32, KV_W), BF),
            pltpu.VMEM((2, 32, wide), BF),
            pltpu.VMEM((256, wide), BF),
            DMA,
            DMA,
            DMA((8,)),
            DMA((8,)),
            DMA((RINGS, 2, 2, 4)),
            DMA((RINGS, 2, 2, 4)),
            DMA((2, 2)),
            DMA((2,)),
            DMA((4,)),
            DMA,
            DMA((4,)),
            DMA,
            DMA((2, 3)),
            DMA((2, 3)),
            DMA((2, 3)),
            DMA((2, 3)),
            DMA((2, 2)),
            DMA((2, 2, 2, 4)),
            DMA((2, 2, 2, 4)),
            DMA((2, NX - 1)),
            DMA((2, NX - 1)),
            DMA((2, 2, 2, 2)),
            DMA((2, 2, 2, 2)),
            DMA((2, NZ - 1)),
            DMA((2, NZ - 1)),
            DMA((2, 2)),
            DMA,
            DMA,
            DMA,
        ],
        compiler_params=pltpu.CompilerParams(
            collective_id=1, has_side_effects=True, vmem_limit_bytes=BACK_GRANT
        ),
        cost_estimate=pl.CostEstimate(flops=10**9, bytes_accessed=16 * 2**20, transcendentals=0),
    )(dq, dkv, tokens, clip_masks)


def on_device(
    tokens, queries, out_grad, key_weight, value_weight, noise_codes, clip_masks, block_order
):
    qx, dox, kv = front(tokens, queries, out_grad, key_weight, value_weight, noise_codes)
    dq, dkv = attention(block_order, qx, dox, kv)
    return back(dq, dkv, tokens, clip_masks)


def solution(mesh):
    placed = (
        P("dp", "ctx", "head"),
        P("dp", "ctx", "head"),
        P("dp", "ctx", "head"),
        P(None, "head"),
        P(None, "head"),
        P(None, "dp", "ctx", "head"),
        P(None, "dp", "ctx", "head"),
        P(),
    )
    return jax.shard_map(
        on_device,
        mesh=mesh,
        in_specs=placed,
        out_specs=(P("dp", "ctx", "head"), P("ctx", "head"), P("ctx", "head")),
        check_vma=False,
    )
```

```python
import functools
import math

import jax
import jax.numpy as jnp
from jax import lax
from jax.experimental import pallas as pl
from jax.experimental.pallas import tpu as pltpu
from jax.sharding import PartitionSpec as P

HD = 128
BLK = 128
NX, NY, NZ, NC = 4, 4, 8, 2
GROUP_COLS = 512
HALF_D = 4096
QUARTER = 1024
KV_W = 256
BLOCKS = 32
NOISE_STEP = 0.05
NOISE_MIDDLE = 7.5
SCALE = 1.0 / math.sqrt(HD)
SCALE_LOG2 = SCALE * math.log2(math.e)
FLOOR_SCORE = -1e30
BF = jnp.bfloat16
F32 = jnp.float32
MESH = pl.DeviceIdType.MESH
VMEM_GRANT = 62 * 2**20
ATTENTION_GRANT = 53 * 2**20
BACK_GRANT = 52 * 2**20
NT = (((1,), (1,)), ((), ()))
NN = (((1,), (0,)), ((), ()))
TN = (((0,), (0,)), ((), ()))


def here():
    ctx, head, dp = lax.axis_index("ctx"), lax.axis_index("head"), lax.axis_index("dp")
    return ctx // NZ, head * 2 + dp // 2, lax.rem(ctx, NZ), lax.rem(dp, 2)


def device(x, y, z, core):
    return {"ctx": x * NZ + z, "head": y // 2, "dp": lax.rem(y, 2) * 2 + core}


def around(value, count):
    return lax.rem(value + count, count)


def signal(target):
    pl.semaphore_signal(pltpu.get_barrier_semaphore(), inc=1, device_id=target, device_id_type=MESH)


def remote(src, dst, send_sem, recv_sem, target):
    return pltpu.make_async_remote_copy(
        src_ref=src, dst_ref=dst, send_sem=send_sem, recv_sem=recv_sem, device_id=target, device_id_type=MESH
    )


def wait_bytes(ref, sem):
    pltpu.make_async_copy(ref, ref, sem).wait()


def send_or_copy(is_self, src, dst, send_sem, recv_sem, target):
    @pl.when(is_self)
    def _():
        pltpu.make_async_copy(src, dst, recv_sem).start()

    @pl.when(jnp.logical_not(is_self))
    def _():
        remote(src, dst, send_sem, recv_sem, target).start()


def wait_sent(is_self, ref, send_sem):
    @pl.when(jnp.logical_not(is_self))
    def _():
        wait_bytes(ref, send_sem)


CHUNKS = ((0, 16, True), (16, 32, True), (48, 32, True), (80, 32, True), (112, 16, False))
IN_FLIGHT = 2
ROW_CHUNKS = len(CHUNKS)


def front_kernel(
    tok, q, do, kw, vw, codes_in, qx, dox, kv,
    codes, xbuf, wbuf, acc, kvst,
    codes_sem, w_sem, own_sem, tok_send, tok_recv, q_send, q_recv, kv_send, kv_send0, kv_recv, hop_send, fw_send, fw_recv,
):
    X, Y, Z, C = here()
    head = Y // 2
    unit_core = X // 2
    same = unit_core == C
    peer = device(X, around(Y + 2, NY), Z, C)
    partner = device(X, Y, Z, 1 - C)

    signal(peer)
    signal(partner)
    for xs in range(NX):
        @pl.when(jnp.logical_not(jnp.logical_and(same, X == xs)))
        def _(xs=xs):
            signal(device(xs, Y, Z, unit_core))
    for delta in (1, -1, 2, -2):
        zs = around(Z + delta, NZ)
        signal(device(X, Y, zs, C))
        for part in range(2):
            signal(device(2 * C + part, Y, zs, unit_core))
    loads = [pltpu.make_async_copy(codes_in, codes, codes_sem)]
    for half in range(2):
        rows = pl.ds(half * HALF_D, HALF_D)
        loads.append(pltpu.make_async_copy(kw.at[rows, :], wbuf.at[half, :, pl.ds(0, KV_W)], w_sem.at[half, 0]))
        loads.append(pltpu.make_async_copy(vw.at[rows, :], wbuf.at[half, :, pl.ds(KV_W, KV_W)], w_sem.at[half, 1]))
    own_x = pltpu.make_async_copy(tok.at[0], xbuf.at[head], own_sem)
    own_x.start()
    for load in loads:
        load.start()

    pl.semaphore_wait(pltpu.get_barrier_semaphore(), 18 - same.astype(jnp.int32))

    def token_copy(r):
        rows = pl.ds(CHUNKS[r][0], CHUNKS[r][1])
        return remote(tok.at[0, rows, :], xbuf.at[head, rows, :], tok_send.at[r], tok_recv.at[r], peer)

    for r in range(IN_FLIGHT):
        token_copy(r).start()
    for j in range(2):
        for c2 in range(NC):
            cols = pl.ds((j * 8 + c2 * 4) * HD, GROUP_COLS)
            target = device(2 * C + j, Y, Z, c2)
            is_self = jnp.logical_and(2 * C + j == X, C == c2)
            send_or_copy(is_self, q.at[0, :, cols], qx.at[X], q_send.at[0, j, c2], q_recv.at[0], target)
            send_or_copy(is_self, do.at[0, :, cols], dox.at[X], q_send.at[1, j, c2], q_recv.at[1], target)

    own_x.wait()
    for load in loads:
        load.wait()
    acc[...] = jnp.dot(xbuf[head], wbuf[head], preferred_element_type=F32)

    mine = X * NZ + Z

    def rows_of(r):
        return pl.ds(CHUNKS[r][0], CHUNKS[r][1])

    def blocks(r, count):
        return kv.at[pl.ds(C * 16, count), rows_of(r), :]

    def spread(r):
        rows = rows_of(r)
        deltas = (2, -2, 1, -1) if CHUNKS[r][2] else (4, 3, -3, 2, -2, 1, -1)
        for j in range(2):
            src = kvst.at[j, rows, :]
            dst = kv.at[mine, rows, :]
            for delta in deltas:
                kind = {2: 0, -2: 1}.get(delta, 2) if CHUNKS[r][2] else 2
                target = device(2 * C + j, Y, around(Z + delta, NZ), unit_core)
                remote(src, dst, kv_send.at[r, j], kv_recv.at[r, kind], target).start()
            is_self = jnp.logical_and(same, 2 * C + j == X)
            send_or_copy(is_self, src, dst, kv_send0.at[r, j], kv_recv.at[r, 2], device(2 * C + j, Y, Z, unit_core))

    def relay(r):
        rows = rows_of(r)
        for kind, sign in ((0, 1), (1, -1)):
            wait_bytes(blocks(r, 2), kv_recv.at[r, kind])
            source = around(Z - 2 * sign, NZ)
            for part in range(2):
                piece = kv.at[(2 * C + part) * NZ + source, rows, :]
                for far in (2, 1) if part == kind else (1,):
                    target = device(X, Y, around(Z + sign * far, NZ), C)
                    remote(piece, piece, hop_send.at[r, kind], kv_recv.at[r, 2], target).start()

    def forward(r):
        wait_bytes(blocks(r, 12 if CHUNKS[r][2] else 16), kv_recv.at[r, 2])
        whole = blocks(r, 16)
        remote(whole, whole, fw_send.at[r], fw_recv.at[r], partner).start()

    for r in range(ROW_CHUNKS):
        rows = rows_of(r)
        wait_bytes(xbuf.at[1 - head, rows, :], tok_recv.at[r])
        token_copy(r).wait_send()
        if r + IN_FLIGHT < ROW_CHUNKS:
            token_copy(r + IN_FLIGHT).start()
        both = acc[rows, :] + jnp.dot(xbuf[1 - head, rows, :], wbuf[1 - head], preferred_element_type=F32)
        for what in range(2):
            shift = NOISE_STEP * (codes[what, 0, rows, :].astype(F32) - NOISE_MIDDLE)
            value = (both[:, what * KV_W : (what + 1) * KV_W] + shift).astype(BF)
            for j in range(2):
                kvst[j, rows, what * HD : (what + 1) * HD] = value[:, j * HD : (j + 1) * HD]
        spread(r)
        if r >= 1 and CHUNKS[r - 1][2]:
            relay(r - 1)
        if r >= 2:
            forward(r - 2)
    forward(ROW_CHUNKS - 2)
    forward(ROW_CHUNKS - 1)

    for r in range(ROW_CHUNKS):
        rows = rows_of(r)
        wait_bytes(kv.at[pl.ds((1 - C) * 16, 16), rows, :], fw_recv.at[r])
        wait_bytes(blocks(r, 16), fw_send.at[r])
        for j in range(2):
            is_self = jnp.logical_and(same, 2 * C + j == X)
            wait_sent(is_self, kvst.at[j, rows, :], kv_send0.at[r, j])
            wait_bytes(blocks(r, 4 if CHUNKS[r][2] else 7), kv_send.at[r, j])
        if CHUNKS[r][2]:
            for kind in range(2):
                wait_bytes(blocks(r, 3), hop_send.at[r, kind])
    wait_bytes(qx, q_recv.at[0])
    wait_bytes(dox, q_recv.at[1])
    for j in range(2):
        for c2 in range(NC):
            is_self = jnp.logical_and(2 * C + j == X, C == c2)
            wait_sent(is_self, qx.at[0], q_send.at[0, j, c2])
            wait_sent(is_self, dox.at[0], q_send.at[1, j, c2])


ANY_SPEC = pl.BlockSpec(memory_space=pl.ANY)
VMEM_SPEC = pl.BlockSpec(memory_space=pltpu.VMEM)
DMA = pltpu.SemaphoreType.DMA


def front(tokens, queries, out_grad, key_weight, value_weight, noise_codes):
    return pl.pallas_call(
        front_kernel,
        name="front",
        out_shape=(
            jax.ShapeDtypeStruct((NX, BLK, GROUP_COLS), BF),
            jax.ShapeDtypeStruct((NX, BLK, GROUP_COLS), BF),
            jax.ShapeDtypeStruct((BLOCKS, BLK, KV_W), BF),
        ),
        in_specs=[ANY_SPEC] * 6,
        out_specs=(ANY_SPEC,) * 3,
        scratch_shapes=[
            pltpu.VMEM((2, 1, BLK, KV_W), jnp.int32),
            pltpu.VMEM((2, BLK, HALF_D), BF),
            pltpu.VMEM((2, HALF_D, 2 * KV_W), BF),
            pltpu.VMEM((BLK, 2 * KV_W), F32),
            pltpu.VMEM((2, BLK, KV_W), BF),
            DMA,
            DMA((2, 2)),
            DMA,
            DMA((ROW_CHUNKS,)),
            DMA((ROW_CHUNKS,)),
            DMA((2, 2, 2)),
            DMA((2,)),
            DMA((ROW_CHUNKS, 2)),
            DMA((ROW_CHUNKS, 2)),
            DMA((ROW_CHUNKS, 3)),
            DMA((ROW_CHUNKS, 2)),
            DMA((ROW_CHUNKS,)),
            DMA((ROW_CHUNKS,)),
        ],
        compiler_params=pltpu.CompilerParams(
            collective_id=0, has_side_effects=True, vmem_limit_bytes=VMEM_GRANT
        ),
        cost_estimate=pl.CostEstimate(flops=10**9, bytes_accessed=16 * 2**20, transcendentals=0),
    )(tokens, queries, out_grad, key_weight, value_weight, noise_codes)


KEYS = 256
LEVELS = (8, 4, 2, 1)
ROWS = 4 * BLK


def attention_kernel(
    order, q, do, kv, dq_out, dkv_out,
    kvb, qs, dos, stb, dpb, dk, dv, dqt, dkvb, block_at, kv_sem, q_sem, do_sem, out_sem,
):
    Z = lax.rem(lax.axis_index("ctx"), NZ)

    def at_place(block):
        return pl.ds(pl.multiple_of(order[block] * BLK, BLK), BLK)

    def load(block, carry):
        pltpu.make_async_copy(kv.at[block], kvb.at[at_place(block), :], kv_sem).start()
        block_at[order[block]] = block
        return carry

    for x in range(NX):
        for h in range(4):
            cols, rows = pl.ds(h * HD, HD), pl.ds(h * BLK, BLK)
            pltpu.make_async_copy(q.at[x, :, cols], qs.at[x, rows, :], q_sem).start()
            pltpu.make_async_copy(do.at[x, :, cols], dos.at[x, rows, :], do_sem).start()
    lax.fori_loop(0, BLOCKS, load, 0)

    def clear(i, carry):
        rows = pl.ds(pl.multiple_of(i * 256, 256), 256)
        dk[rows, :] = jnp.zeros((256, HD), F32)
        dv[rows, :] = jnp.zeros((256, HD), F32)
        return carry

    lax.fori_loop(0, 16, clear, 0)
    wait_bytes(qs, q_sem)
    wait_bytes(dos, do_sem)
    wait_bytes(kvb, kv_sem)

    def run(count, body, carry):
        done = 0
        for units in LEVELS:
            times = (count - done) // units
            base = done

            def step(i, state, units=units, base=base):
                start = pl.multiple_of((base + i * units) * KEYS, KEYS)
                return body(pl.ds(start, units * KEYS), units * KEYS, state)

            carry = lax.fori_loop(0, times, step, carry)
            done = base + times * units
        return carry

    def fold(array, size, how):
        return how(array.reshape(size // 8, 8, ROWS), axis=0)

    def tile(x, carry):
        place = order[x * NZ + Z]
        last = place // 2
        qx = qs[x]
        dx = dos[x]

        def score_step(rows, size, top):
            st = lax.dot_general(kvb[rows, :HD], qx, NT, preferred_element_type=F32)
            stb[rows, :] = st
            return jnp.maximum(top, fold(st, size, jnp.max))

        top = run(last, score_step, jnp.full((8, ROWS), FLOOR_SCORE, F32))
        rows = pl.ds(pl.multiple_of(last * KEYS, KEYS), KEYS)
        st = lax.dot_general(kvb[rows, :HD], qx, NT, preferred_element_type=F32)
        key_places = last * KEYS + lax.broadcasted_iota(jnp.int32, (KEYS, ROWS), 0)
        query_places = place * BLK + lax.rem(lax.broadcasted_iota(jnp.int32, (KEYS, ROWS), 1), BLK)
        st = jnp.where(key_places <= query_places, st, FLOOR_SCORE)
        stb[rows, :] = st
        top = jnp.maximum(top, fold(st, KEYS, jnp.max))
        top = jnp.max(top, axis=0, keepdims=True) * SCALE_LOG2

        def weigh_step(rows, size, state):
            total, weighted = state
            weights = jnp.exp2(stb[rows, :] * SCALE_LOG2 - top)
            dpt = lax.dot_general(kvb[rows, HD:], dx, NT, preferred_element_type=F32)
            dpb[rows, :] = dpt
            stb[rows, :] = weights
            return total + fold(weights, size, jnp.sum), weighted + fold(weights * dpt, size, jnp.sum)

        zero = jnp.zeros((8, ROWS), F32)
        total, weighted = run(last + 1, weigh_step, (zero, zero))
        inverse = 1.0 / jnp.sum(total, axis=0, keepdims=True)
        delta = jnp.sum(weighted, axis=0, keepdims=True) * inverse
        dqt[...] = jnp.zeros((HD, ROWS), F32)

        def grad_step(rows, size, state):
            probs = stb[rows, :] * inverse
            low = probs.astype(BF)
            grads = (probs * (dpb[rows, :] - delta)).astype(BF)
            dv[rows, :] += lax.dot_general(low, dx, NN, preferred_element_type=F32)
            dk[rows, :] += lax.dot_general(grads, qx, NN, preferred_element_type=F32)
            dqt[...] += lax.dot_general(kvb[rows, :HD], grads, TN, preferred_element_type=F32)
            return state

        run(last + 1, grad_step, 0)
        dq = dqt[...].T
        for h in range(4):
            dq_out[x, :, h * HD : (h + 1) * HD] = (dq[h * BLK : (h + 1) * BLK, :] * SCALE).astype(BF)
        return carry

    lax.fori_loop(0, NX, tile, 0)

    def finish(i, carry):
        rows = pl.ds(pl.multiple_of(i * 256, 256), 256)
        dkvb[rows, :HD] = (dk[rows, :] * SCALE).astype(BF)
        dkvb[rows, HD:] = dv[rows, :].astype(BF)
        for j in range(2):
            block = block_at[2 * i + j]
            src = dkvb.at[pl.ds(pl.multiple_of(i * 256 + j * BLK, BLK), BLK), :]
            pltpu.make_async_copy(src, dkv_out.at[block // NZ, lax.rem(block, NZ)], out_sem).start()
        return carry

    lax.fori_loop(0, 16, finish, 0)
    wait_bytes(dkvb, out_sem)


def attention(block_order, qx, dox, kv):
    tokens = BLOCKS * BLK
    return pl.pallas_call(
        attention_kernel,
        name="attention",
        out_shape=(
            jax.ShapeDtypeStruct((NX, BLK, GROUP_COLS), BF),
            jax.ShapeDtypeStruct((NX, NZ, BLK, KV_W), BF),
        ),
        in_specs=[pl.BlockSpec(memory_space=pltpu.SMEM)] + [ANY_SPEC] * 3,
        out_specs=(VMEM_SPEC, ANY_SPEC),
        scratch_shapes=[
            pltpu.VMEM((tokens, KV_W), BF),
            pltpu.VMEM((NX, ROWS, HD), BF),
            pltpu.VMEM((NX, ROWS, HD), BF),
            pltpu.VMEM((tokens, ROWS), F32),
            pltpu.VMEM((tokens, ROWS), F32),
            pltpu.VMEM((tokens, HD), F32),
            pltpu.VMEM((tokens, HD), F32),
            pltpu.VMEM((HD, ROWS), F32),
            pltpu.VMEM((tokens, KV_W), BF),
            pltpu.SMEM((BLOCKS,), jnp.int32),
            DMA,
            DMA,
            DMA,
            DMA,
        ],
        compiler_params=pltpu.CompilerParams(vmem_limit_bytes=ATTENTION_GRANT),
        cost_estimate=pl.CostEstimate(flops=10**10, bytes_accessed=8 * 2**20, transcendentals=10**7),
    )(block_order, qx, dox, kv)


class Ring:
    def __init__(self, count, position, neighbour, own, slots, send_sems, recv_sems):
        self.count, self.position, self.neighbour, self.own = count, position, neighbour, own
        self.slots, self.send_sems, self.recv_sems = slots, send_sems, recv_sems
        self.steps = count // 2
        self.sent = []

    def chains(self, step):
        for way in range(2):
            for part in range(2):
                length = self.steps if way == part else self.steps - 1
                if step >= self.steps - length:
                    yield way, part, step == self.steps - length

    def step(self, step):
        for way, part, first in self.chains(step):
            sign = 1 if way == 0 else -1
            mine = self.own(part, sign * (self.steps - step))
            if first:
                src = mine
            else:
                src = self.slots.at[way, part, step - 1]
                wait_bytes(src, self.recv_sems.at[way, part, step - 1])
                src[...] = (src[...].astype(F32) + mine[...].astype(F32)).astype(BF)
            copy = remote(
                src,
                self.slots.at[way, part, step],
                self.send_sems.at[way, part, step],
                self.recv_sems.at[way, part, step],
                self.neighbour(sign),
            )
            copy.start()
            self.sent.append(copy)

    def result(self, part):
        total = self.own(part, 0)[...].astype(F32)
        for way in range(2):
            slot = self.slots.at[way, part, self.steps - 1]
            wait_bytes(slot, self.recv_sems.at[way, part, self.steps - 1])
            total += slot[...].astype(F32)
        return total.astype(BF)

    def finish(self):
        for copy in self.sent:
            copy.wait_send()


def span(start, size):
    return pl.ds(pl.multiple_of(start, 16), size)


HALF_ROWS = BLK // 2
RINGS = 4
RING_ROWS = BLK // RINGS
DELTAS = (4, 3, -3, 2, -2, 1, -1, 0)


def back_kernel(
    dq, dkv, tok, masks, query_grad, key_out, value_out,
    own, other, z1, home_src, raw, mbuf, tokq, tokt, preall, wa, wb, az, ra, ax, bx, rb, bz, fin, final,
    own_sem, mask_sem, ex_send, ex_recv, z1_send, z1_recv, home_send, home_recv, tok_send, tok_recv, dq_send, dq_recv,
    pre_send, pre_recv, pfw_send, pfw_recv, core_sem,
    az_send, az_recv, ax_send, ax_recv, bx_send, bx_recv, bz_send, bz_recv,
    fin_send, fin_recv, f2_send, f2_recv,
):
    X, Y, Z, C = here()
    head, low = Y // 2, lax.rem(Y, 2)
    unit_core = X // 2
    slot = lax.rem(X, 2)
    same = unit_core == C
    partner = device(X, Y, Z, 1 - C)
    beside = device(X, 2 * head + 1 - low, Z, C)
    seq = low * 2 + C

    def z_next(sign):
        return device(X, Y, around(Z + sign, NZ), C)

    def x_next(sign):
        return device(around(X + sign, NX), Y, Z, C)

    def y_next(by):
        return device(X, around(Y + by, NY), Z, C)

    ways = (1, 3, 2)
    i_mine = X + 4 * lax.rem(Z, 2)
    targets = [
        [(Y, 2 * around(head + which, 2) + lows, 4 * C + Z // 2, lax.rem(Z, 2)) for lows in range(2)]
        for which in range(2)
    ]

    def is_me(place):
        x, y, z, core = place
        return jnp.logical_and(jnp.logical_and(x == X, y == Y), jnp.logical_and(z == Z, core == C))

    is_final = [[is_me(target) for target in pair] for pair in targets]

    signal(partner)
    for xs in range(2):
        for cs in range(NC):
            @pl.when(jnp.logical_not(jnp.logical_and(2 * C + xs == X, C == cs)))
            def _(xs=xs, cs=cs):
                signal(device(2 * C + xs, Y, Z, cs))
    for sign in (1, -1):
        signal(z_next(sign))
        signal(x_next(sign))
    for cs in range(NC):
        signal(device(X, 2 * head + 1 - low, Z, cs))
    for by in ways:
        signal(y_next(by))
    signal(device(around(X + 2, NX), Y, Z, C))
    load_own = pltpu.make_async_copy(dkv.at[pl.ds(C * 2, 2)], own, own_sem)
    load_own.start()
    load_mask = pltpu.make_async_copy(masks, mbuf, mask_sem)
    load_mask.start()
    pl.semaphore_wait(pltpu.get_barrier_semaphore(), 15 - same.astype(jnp.int32))

    exchanges = {}
    for i, delta in enumerate(DELTAS):
        t = around(Z + delta, NZ)
        copy = remote(dkv.at[pl.ds((1 - C) * 2, 2), t], other.at[:, t], ex_send.at[i], ex_recv.at[i], partner)
        copy.start()
        exchanges[delta] = copy
    for xs in range(NX):
        cols = pl.ds(pl.multiple_of((slot * 8 + C * 4) * HD, GROUP_COLS), GROUP_COLS)
        is_self = jnp.logical_and(same, X == xs)
        send_or_copy(
            is_self, dq.at[xs], query_grad.at[0, :, cols], dq_send.at[xs], dq_recv, device(xs, Y, Z, unit_core)
        )
    for quarter in range(4):
        is_self = seq == quarter
        send_or_copy(
            is_self,
            tok.at[0, :, pl.ds(quarter * QUARTER, QUARTER)],
            tokq.at[seq],
            tok_send.at[quarter],
            tok_recv,
            device(X, 2 * head + quarter // 2, Z, quarter % 2),
        )

    load_own.wait()
    ready = set()

    def prepare(delta):
        if delta in ready:
            return
        ready.add(delta)
        t = around(Z + delta, NZ)
        exchanges[delta].wait_recv()
        for part in range(2):
            own[part, t] = (own[part, t].astype(F32) + other[part, t].astype(F32)).astype(BF)

    def own_part(i):
        def get(part, delta):
            prepare(4 if delta == -4 else delta)
            return own.at[part, around(Z + delta, NZ), pl.ds(i * RING_ROWS, RING_ROWS), :]

        return get

    rings = [Ring(NZ, Z, z_next, own_part(i), z1.at[i], z1_send.at[i], z1_recv.at[i]) for i in range(RINGS)]
    for step in range(NZ // 2):
        for ring in rings:
            ring.step(step)
    for half in range(2):
        rows = pl.ds(half * HALF_ROWS, HALF_ROWS)
        for i in range(half * RINGS // 2, (half + 1) * RINGS // 2):
            for part in range(2):
                home_src[part, i * RING_ROWS : (i + 1) * RING_ROWS, :] = rings[i].result(part)
        for part in range(2):
            xs = 2 * C + part
            is_self = jnp.logical_and(same, X == xs)
            send_or_copy(
                is_self,
                home_src.at[part, rows, :],
                raw.at[slot, rows, :],
                home_send.at[half, part],
                home_recv.at[half],
                device(xs, Y, Z, unit_core),
            )

    load_mask.wait()
    sends = []
    y_targets = (beside, y_next(around(2 * low - 1, NY)), y_next(2))
    y_places = ((head, 1 - low), (1 - head, 1 - low), (1 - head, low))

    def my_rows(half):
        return span(seq * BLK + half * HALF_ROWS, HALF_ROWS)

    for half in range(2):
        rows = pl.ds(half * HALF_ROWS, HALF_ROWS)
        wait_bytes(raw.at[:, rows, :], home_recv.at[half])
        for j in range(2):
            for what in range(2):
                mask = mbuf[what, 0, rows, j * HD : (j + 1) * HD] != 0
                piece = raw[j, rows, what * HD : (what + 1) * HD]
                first = (2 * j + what) * HD
                preall[head, my_rows(half), first : first + HD] = jnp.where(mask, piece, jnp.zeros_like(piece))
        mine = preall.at[head, my_rows(half), :]
        sends.append(remote(mine, mine, core_sem.at[half, 0], core_sem.at[half, 1], partner))
        sends[-1].start()
        for i in range(2):
            sends.append(remote(mine, mine, pre_send.at[half, i], pre_recv.at[half, i], y_targets[i]))
            sends[-1].start()
    for half in range(2):
        mine = preall.at[head, my_rows(half), :]
        sends.append(remote(mine, mine, pre_send.at[half, 2], pre_recv.at[half, 2], y_targets[2]))
        sends[-1].start()

    wait_bytes(tokq, tok_recv)
    for s in range(4):
        tokt[:, :, :, s * BLK : (s + 1) * BLK] = tokq[s].T.reshape(NZ, NX, 32, BLK)

    forwards = []

    def pass_on(i):
        place, lows = y_places[i]
        for half in range(2):
            piece = preall.at[place, span((lows * 2 + C) * BLK + half * HALF_ROWS, HALF_ROWS), :]
            wait_bytes(piece, pre_recv.at[half, i])
            copy = remote(piece, piece, pfw_send.at[half, i], pfw_recv.at[half, i], partner)
            copy.start()
            forwards.append(copy)
        return forwards[-2:]

    passed_on = [pass_on(0)]
    for half in range(2):
        sends[half * 3].wait_recv()
    for copy in passed_on[0]:
        copy.wait_recv()

    made = set()

    def product(path, which, delta):
        if (path, which, delta) in made:
            return
        made.add((path, which, delta))
        cols = slice(path * KV_W, (path + 1) * KV_W)
        if path == 0:
            t = around(Z + delta, NZ)
            rows = tokt[t].reshape(128, 4 * BLK)
        else:
            t = around(X + delta, NX)
            rows = tokt[:, t].reshape(256, 4 * BLK)
        value = jnp.dot(rows, preall[around(head + which, 2), :, cols], preferred_element_type=F32).astype(BF)
        if path == 0:
            wa[which, t] = value.reshape(NX, 32, KV_W)
        else:
            wb[which, :, t] = value.reshape(NZ, 32, KV_W)

    def a_own(which):
        def get(part, delta):
            delta = 4 if delta == -4 else delta
            product(0, which, delta)
            return wa.at[which, around(Z + delta, NZ), pl.ds(part * 2, 2)]

        return get

    def b_own(which):
        def get(part, delta):
            delta = 2 if delta == -2 else delta
            product(1, which, delta)
            return wb.at[which, pl.ds(part * 4, 4), around(X + delta, NX)]

        return get

    a1 = [Ring(NZ, Z, z_next, a_own(s), az.at[s], az_send.at[s], az_recv.at[s]) for s in range(2)]
    b1 = [Ring(NX, X, x_next, b_own(s), bx.at[s], bx_send.at[s], bx_recv.at[s]) for s in range(2)]

    directs = []

    def direct(source, slots, send_sems, recv_sems, count, position, neighbour):
        deltas = sorted([d for d in range(1 - count // 2, count // 2 + 1) if d], key=lambda d: -abs(d))
        for delta in deltas:
            i = delta % count - 1
            src = source.at[around(position + delta, count)]
            copy = remote(src, slots.at[i], send_sems.at[i], recv_sems.at[i], neighbour(delta))
            copy.start()
            directs.append(copy)

    def collect(source, slots, recv_sems, count, position):
        total = source[position].astype(F32)
        for i in range(count - 1):
            wait_bytes(slots.at[i], recv_sems.at[i])
            total += slots[i].astype(F32)
        return total.astype(BF)

    def turn_a(which):
        for part in range(2):
            ra[which, part * 2 : (part + 1) * 2] = a1[which].result(part)
        direct(ra.at[which], ax.at[which], ax_send.at[which], ax_recv.at[which], NX, X, x_next)

    def turn_b(which):
        for part in range(2):
            rb[which, part * 4 : (part + 1) * 4] = b1[which].result(part)
        direct(rb.at[which], bz.at[which], bz_send.at[which], bz_recv.at[which], NZ, Z, z_next)

    def deliver(which):
        fin[which, :, KV_W:] = collect(rb.at[which], bz.at[which], bz_recv.at[which], NZ, Z)
        fin[which, :, :KV_W] = collect(ra.at[which], ax.at[which], ax_recv.at[which], NX, X)
        dst = final.at[span(i_mine * 32, 32), :]
        for lows in range(2):
            send_or_copy(
                is_final[which][lows],
                fin.at[which],
                dst,
                fin_send.at[which, lows],
                fin_recv,
                device(*targets[which][lows]),
            )

    a1[0].step(0)
    passed_on.append(pass_on(1))
    passed_on.append(pass_on(2))
    a1[0].step(1)
    for copy in passed_on[1] + passed_on[2]:
        copy.wait_recv()
    a1[1].step(0)
    b1[0].step(0)
    b1[1].step(0)
    a1[0].step(2)
    a1[1].step(1)
    b1[0].step(1)
    a1[0].step(3)
    a1[1].step(2)
    b1[1].step(1)
    turn_b(0)
    turn_a(0)
    a1[1].step(3)
    turn_b(1)
    turn_a(1)
    deliver(0)
    deliver(1)

    mine = final.at[span(C * BLK, BLK), :]
    wait_bytes(mine, fin_recv)
    to_partner = remote(mine, mine, f2_send, f2_recv, partner)
    to_partner.start()
    to_partner.wait_recv()
    for j in range(2):
        for what, out in ((0, key_out), (1, value_out)):
            first = (2 * j + what) * HD
            out[:, j * HD : (j + 1) * HD] = final[:, first : first + HD].astype(F32) * 0.25

    wait_bytes(query_grad, dq_recv)
    for copy in exchanges.values():
        copy.wait_send()
    for xs in range(NX):
        wait_sent(jnp.logical_and(same, X == xs), dq.at[xs], dq_send.at[xs])
    for quarter in range(4):
        wait_sent(seq == quarter, tokq.at[0], tok_send.at[quarter])
    for half in range(2):
        for part in range(2):
            wait_sent(
                jnp.logical_and(same, X == 2 * C + part),
                raw.at[part, pl.ds(half * HALF_ROWS, HALF_ROWS), :],
                home_send.at[half, part],
            )
    for copy in sends + forwards + [to_partner]:
        copy.wait_send()
    for ring in rings + a1 + b1:
        ring.finish()
    for copy in directs:
        copy.wait_send()
    for which in range(2):
        for lows in range(2):
            wait_sent(is_final[which][lows], fin.at[which], fin_send.at[which, lows])


def back(dq, dkv, tokens, clip_masks):
    wide = 2 * KV_W
    return pl.pallas_call(
        back_kernel,
        name="back",
        out_shape=(
            jax.ShapeDtypeStruct((1, BLK, 2048), BF),
            jax.ShapeDtypeStruct((256, KV_W), F32),
            jax.ShapeDtypeStruct((256, KV_W), F32),
        ),
        in_specs=[ANY_SPEC] * 4,
        out_specs=(ANY_SPEC, VMEM_SPEC, VMEM_SPEC),
        scratch_shapes=[
            pltpu.VMEM((2, NZ, BLK, KV_W), BF),
            pltpu.VMEM((2, NZ, BLK, KV_W), BF),
            pltpu.VMEM((RINGS, 2, 2, 4, RING_ROWS, KV_W), BF),
            pltpu.VMEM((2, BLK, KV_W), BF),
            pltpu.VMEM((2, BLK, KV_W), BF),
            pltpu.VMEM((2, 1, BLK, KV_W), jnp.int32),
            pltpu.VMEM((4, BLK, QUARTER), BF),
            pltpu.VMEM((NZ, NX, 32, 4 * BLK), BF),
            pltpu.VMEM((2, 4 * BLK, wide), BF),
            pltpu.VMEM((2, NZ, NX, 32, KV_W), BF),
            pltpu.VMEM((2, NZ, NX, 32, KV_W), BF),
            pltpu.VMEM((2, 2, 2, 4, 2, 32, KV_W), BF),
            pltpu.VMEM((2, NX, 32, KV_W), BF),
            pltpu.VMEM((2, NX - 1, 32, KV_W), BF),
            pltpu.VMEM((2, 2, 2, 2, 4, 32, KV_W), BF),
            pltpu.VMEM((2, NZ, 32, KV_W), BF),
            pltpu.VMEM((2, NZ - 1, 32, KV_W), BF),
            pltpu.VMEM((2, 32, wide), BF),
            pltpu.VMEM((256, wide), BF),
            DMA,
            DMA,
            DMA((8,)),
            DMA((8,)),
            DMA((RINGS, 2, 2, 4)),
            DMA((RINGS, 2, 2, 4)),
            DMA((2, 2)),
            DMA((2,)),
            DMA((4,)),
            DMA,
            DMA((4,)),
            DMA,
            DMA((2, 3)),
            DMA((2, 3)),
            DMA((2, 3)),
            DMA((2, 3)),
            DMA((2, 2)),
            DMA((2, 2, 2, 4)),
            DMA((2, 2, 2, 4)),
            DMA((2, NX - 1)),
            DMA((2, NX - 1)),
            DMA((2, 2, 2, 2)),
            DMA((2, 2, 2, 2)),
            DMA((2, NZ - 1)),
            DMA((2, NZ - 1)),
            DMA((2, 2)),
            DMA,
            DMA,
            DMA,
        ],
        compiler_params=pltpu.CompilerParams(
            collective_id=1, has_side_effects=True, vmem_limit_bytes=BACK_GRANT
        ),
        cost_estimate=pl.CostEstimate(flops=10**9, bytes_accessed=16 * 2**20, transcendentals=0),
    )(dq, dkv, tokens, clip_masks)


def on_device(
    tokens, queries, out_grad, key_weight, value_weight, noise_codes, clip_masks, block_order
):
    qx, dox, kv = front(tokens, queries, out_grad, key_weight, value_weight, noise_codes)
    dq, dkv = attention(block_order, qx, dox, kv)
    return back(dq, dkv, tokens, clip_masks)


def solution(mesh):
    placed = (
        P("dp", "ctx", "head"),
        P("dp", "ctx", "head"),
        P("dp", "ctx", "head"),
        P(None, "head"),
        P(None, "head"),
        P(None, "dp", "ctx", "head"),
        P(None, "dp", "ctx", "head"),
        P(),
    )
    return jax.shard_map(
        on_device,
        mesh=mesh,
        in_specs=placed,
        out_specs=(P("dp", "ctx", "head"), P("ctx", "head"), P("ctx", "head")),
        check_vma=False,
    )
```

```python
import functools
import math

import jax
import jax.numpy as jnp
from jax import lax
from jax.experimental import pallas as pl
from jax.experimental.pallas import tpu as pltpu
from jax.sharding import PartitionSpec as P

HD = 128
BLK = 128
NX, NY, NZ, NC = 4, 4, 8, 2
GROUP_COLS = 512
HALF_D = 4096
QUARTER = 1024
KV_W = 256
BLOCKS = 32
NOISE_STEP = 0.05
NOISE_MIDDLE = 7.5
SCALE = 1.0 / math.sqrt(HD)
SCALE_LOG2 = SCALE * math.log2(math.e)
FLOOR_SCORE = -1e30
BF = jnp.bfloat16
F32 = jnp.float32
MESH = pl.DeviceIdType.MESH
VMEM_GRANT = 62 * 2**20
ATTENTION_GRANT = 53 * 2**20
BACK_GRANT = 52 * 2**20
NT = (((1,), (1,)), ((), ()))
NN = (((1,), (0,)), ((), ()))
TN = (((0,), (0,)), ((), ()))


def here():
    ctx, head, dp = lax.axis_index("ctx"), lax.axis_index("head"), lax.axis_index("dp")
    return ctx // NZ, head * 2 + dp // 2, lax.rem(ctx, NZ), lax.rem(dp, 2)


def device(x, y, z, core):
    return {"ctx": x * NZ + z, "head": y // 2, "dp": lax.rem(y, 2) * 2 + core}


def around(value, count):
    return lax.rem(value + count, count)


def signal(target):
    pl.semaphore_signal(pltpu.get_barrier_semaphore(), inc=1, device_id=target, device_id_type=MESH)


def remote(src, dst, send_sem, recv_sem, target):
    return pltpu.make_async_remote_copy(
        src_ref=src, dst_ref=dst, send_sem=send_sem, recv_sem=recv_sem, device_id=target, device_id_type=MESH
    )


def wait_bytes(ref, sem):
    pltpu.make_async_copy(ref, ref, sem).wait()


def send_or_copy(is_self, src, dst, send_sem, recv_sem, target):
    @pl.when(is_self)
    def _():
        pltpu.make_async_copy(src, dst, recv_sem).start()

    @pl.when(jnp.logical_not(is_self))
    def _():
        remote(src, dst, send_sem, recv_sem, target).start()


def wait_sent(is_self, ref, send_sem):
    @pl.when(jnp.logical_not(is_self))
    def _():
        wait_bytes(ref, send_sem)


CHUNKS = ((0, 16, True), (16, 32, True), (48, 32, True), (80, 32, True), (112, 16, False))
IN_FLIGHT = 2
ROW_CHUNKS = len(CHUNKS)


def front_kernel(
    tok, q, do, kw, vw, codes_in, qx, dox, kv,
    codes, xbuf, wbuf, acc, kvst,
    codes_sem, w_sem, own_sem, tok_send, tok_recv, q_send, q_recv, kv_send, kv_send0, kv_recv, hop_send, fw_send, fw_recv,
):
    X, Y, Z, C = here()
    head = Y // 2
    unit_core = X // 2
    same = unit_core == C
    peer = device(X, around(Y + 2, NY), Z, C)
    partner = device(X, Y, Z, 1 - C)

    signal(peer)
    signal(partner)
    for xs in range(NX):
        @pl.when(jnp.logical_not(jnp.logical_and(same, X == xs)))
        def _(xs=xs):
            signal(device(xs, Y, Z, unit_core))
    for delta in (1, -1, 2, -2):
        zs = around(Z + delta, NZ)
        signal(device(X, Y, zs, C))
        for part in range(2):
            signal(device(2 * C + part, Y, zs, unit_core))
    loads = [pltpu.make_async_copy(codes_in, codes, codes_sem)]
    for half in range(2):
        rows = pl.ds(half * HALF_D, HALF_D)
        loads.append(pltpu.make_async_copy(kw.at[rows, :], wbuf.at[half, :, pl.ds(0, KV_W)], w_sem.at[half, 0]))
        loads.append(pltpu.make_async_copy(vw.at[rows, :], wbuf.at[half, :, pl.ds(KV_W, KV_W)], w_sem.at[half, 1]))
    own_x = pltpu.make_async_copy(tok.at[0], xbuf.at[head], own_sem)
    own_x.start()
    for load in loads:
        load.start()

    pl.semaphore_wait(pltpu.get_barrier_semaphore(), 18 - same.astype(jnp.int32))

    def token_copy(r):
        rows = pl.ds(CHUNKS[r][0], CHUNKS[r][1])
        return remote(tok.at[0, rows, :], xbuf.at[head, rows, :], tok_send.at[r], tok_recv.at[r], peer)

    for r in range(IN_FLIGHT):
        token_copy(r).start()
    for j in range(2):
        for c2 in range(NC):
            cols = pl.ds((j * 8 + c2 * 4) * HD, GROUP_COLS)
            target = device(2 * C + j, Y, Z, c2)
            is_self = jnp.logical_and(2 * C + j == X, C == c2)
            send_or_copy(is_self, q.at[0, :, cols], qx.at[X], q_send.at[0, j, c2], q_recv.at[0], target)
            send_or_copy(is_self, do.at[0, :, cols], dox.at[X], q_send.at[1, j, c2], q_recv.at[1], target)

    own_x.wait()
    for load in loads:
        load.wait()
    acc[...] = jnp.dot(xbuf[head], wbuf[head], preferred_element_type=F32)

    mine = X * NZ + Z

    def rows_of(r):
        return pl.ds(CHUNKS[r][0], CHUNKS[r][1])

    def blocks(r, count):
        return kv.at[pl.ds(C * 16, count), rows_of(r), :]

    def spread(r):
        rows = rows_of(r)
        deltas = (2, -2, 1, -1) if CHUNKS[r][2] else (4, 3, -3, 2, -2, 1, -1)
        for j in range(2):
            src = kvst.at[j, rows, :]
            dst = kv.at[mine, rows, :]
            for delta in deltas:
                kind = {2: 0, -2: 1}.get(delta, 2) if CHUNKS[r][2] else 2
                target = device(2 * C + j, Y, around(Z + delta, NZ), unit_core)
                remote(src, dst, kv_send.at[r, j], kv_recv.at[r, kind], target).start()
            is_self = jnp.logical_and(same, 2 * C + j == X)
            send_or_copy(is_self, src, dst, kv_send0.at[r, j], kv_recv.at[r, 2], device(2 * C + j, Y, Z, unit_core))

    def relay(r):
        rows = rows_of(r)
        for kind, sign in ((0, 1), (1, -1)):
            wait_bytes(blocks(r, 2), kv_recv.at[r, kind])
            source = around(Z - 2 * sign, NZ)
            for part in range(2):
                piece = kv.at[(2 * C + part) * NZ + source, rows, :]
                for far in (2, 1) if part == kind else (1,):
                    target = device(X, Y, around(Z + sign * far, NZ), C)
                    remote(piece, piece, hop_send.at[r, kind], kv_recv.at[r, 2], target).start()

    def forward(r):
        wait_bytes(blocks(r, 12 if CHUNKS[r][2] else 16), kv_recv.at[r, 2])
        whole = blocks(r, 16)
        remote(whole, whole, fw_send.at[r], fw_recv.at[r], partner).start()

    for r in range(ROW_CHUNKS):
        rows = rows_of(r)
        wait_bytes(xbuf.at[1 - head, rows, :], tok_recv.at[r])
        token_copy(r).wait_send()
        if r + IN_FLIGHT < ROW_CHUNKS:
            token_copy(r + IN_FLIGHT).start()
        both = acc[rows, :] + jnp.dot(xbuf[1 - head, rows, :], wbuf[1 - head], preferred_element_type=F32)
        for what in range(2):
            shift = NOISE_STEP * (codes[what, 0, rows, :].astype(F32) - NOISE_MIDDLE)
            value = (both[:, what * KV_W : (what + 1) * KV_W] + shift).astype(BF)
            for j in range(2):
                kvst[j, rows, what * HD : (what + 1) * HD] = value[:, j * HD : (j + 1) * HD]
        spread(r)
        if r >= 1 and CHUNKS[r - 1][2]:
            relay(r - 1)
        if r >= 2:
            forward(r - 2)
    forward(ROW_CHUNKS - 2)
    forward(ROW_CHUNKS - 1)

    for r in range(ROW_CHUNKS):
        rows = rows_of(r)
        wait_bytes(kv.at[pl.ds((1 - C) * 16, 16), rows, :], fw_recv.at[r])
        wait_bytes(blocks(r, 16), fw_send.at[r])
        for j in range(2):
            is_self = jnp.logical_and(same, 2 * C + j == X)
            wait_sent(is_self, kvst.at[j, rows, :], kv_send0.at[r, j])
            wait_bytes(blocks(r, 4 if CHUNKS[r][2] else 7), kv_send.at[r, j])
        if CHUNKS[r][2]:
            for kind in range(2):
                wait_bytes(blocks(r, 3), hop_send.at[r, kind])
    wait_bytes(qx, q_recv.at[0])
    wait_bytes(dox, q_recv.at[1])
    for j in range(2):
        for c2 in range(NC):
            is_self = jnp.logical_and(2 * C + j == X, C == c2)
            wait_sent(is_self, qx.at[0], q_send.at[0, j, c2])
            wait_sent(is_self, dox.at[0], q_send.at[1, j, c2])


ANY_SPEC = pl.BlockSpec(memory_space=pl.ANY)
VMEM_SPEC = pl.BlockSpec(memory_space=pltpu.VMEM)
DMA = pltpu.SemaphoreType.DMA


def front(tokens, queries, out_grad, key_weight, value_weight, noise_codes):
    return pl.pallas_call(
        front_kernel,
        name="front",
        out_shape=(
            jax.ShapeDtypeStruct((NX, BLK, GROUP_COLS), BF),
            jax.ShapeDtypeStruct((NX, BLK, GROUP_COLS), BF),
            jax.ShapeDtypeStruct((BLOCKS, BLK, KV_W), BF),
        ),
        in_specs=[ANY_SPEC] * 6,
        out_specs=(ANY_SPEC,) * 3,
        scratch_shapes=[
            pltpu.VMEM((2, 1, BLK, KV_W), jnp.int32),
            pltpu.VMEM((2, BLK, HALF_D), BF),
            pltpu.VMEM((2, HALF_D, 2 * KV_W), BF),
            pltpu.VMEM((BLK, 2 * KV_W), F32),
            pltpu.VMEM((2, BLK, KV_W), BF),
            DMA,
            DMA((2, 2)),
            DMA,
            DMA((ROW_CHUNKS,)),
            DMA((ROW_CHUNKS,)),
            DMA((2, 2, 2)),
            DMA((2,)),
            DMA((ROW_CHUNKS, 2)),
            DMA((ROW_CHUNKS, 2)),
            DMA((ROW_CHUNKS, 3)),
            DMA((ROW_CHUNKS, 2)),
            DMA((ROW_CHUNKS,)),
            DMA((ROW_CHUNKS,)),
        ],
        compiler_params=pltpu.CompilerParams(
            collective_id=0, has_side_effects=True, vmem_limit_bytes=VMEM_GRANT
        ),
        cost_estimate=pl.CostEstimate(flops=10**9, bytes_accessed=16 * 2**20, transcendentals=0),
    )(tokens, queries, out_grad, key_weight, value_weight, noise_codes)


KEYS = 256
LEVELS = (8, 4, 2, 1)
ROWS = 4 * BLK


def attention_kernel(
    order, q, do, kv, dq_out, dkv_out,
    kvb, qs, dos, stb, dpb, dk, dv, dqt, dkvb, block_at, kv_sem, q_sem, do_sem, out_sem,
):
    Z = lax.rem(lax.axis_index("ctx"), NZ)

    def at_place(block):
        return pl.ds(pl.multiple_of(order[block] * BLK, BLK), BLK)

    def load(block, carry):
        pltpu.make_async_copy(kv.at[block], kvb.at[at_place(block), :], kv_sem).start()
        block_at[order[block]] = block
        return carry

    for x in range(NX):
        for h in range(4):
            cols, rows = pl.ds(h * HD, HD), pl.ds(h * BLK, BLK)
            pltpu.make_async_copy(q.at[x, :, cols], qs.at[x, rows, :], q_sem).start()
            pltpu.make_async_copy(do.at[x, :, cols], dos.at[x, rows, :], do_sem).start()
    lax.fori_loop(0, BLOCKS, load, 0)

    def clear(i, carry):
        rows = pl.ds(pl.multiple_of(i * 256, 256), 256)
        dk[rows, :] = jnp.zeros((256, HD), F32)
        dv[rows, :] = jnp.zeros((256, HD), F32)
        return carry

    lax.fori_loop(0, 16, clear, 0)
    wait_bytes(qs, q_sem)
    wait_bytes(dos, do_sem)
    wait_bytes(kvb, kv_sem)

    def run(count, body, carry):
        done = 0
        for units in LEVELS:
            times = (count - done) // units
            base = done

            def step(i, state, units=units, base=base):
                start = pl.multiple_of((base + i * units) * KEYS, KEYS)
                return body(pl.ds(start, units * KEYS), units * KEYS, state)

            carry = lax.fori_loop(0, times, step, carry)
            done = base + times * units
        return carry

    def fold(array, size, how):
        return how(array.reshape(size // 8, 8, ROWS), axis=0)

    def tile(x, carry):
        place = order[x * NZ + Z]
        last = place // 2
        qx = qs[x]
        dx = dos[x]

        def score_step(rows, size, top):
            st = lax.dot_general(kvb[rows, :HD], qx, NT, preferred_element_type=F32)
            stb[rows, :] = st
            return jnp.maximum(top, fold(st, size, jnp.max))

        top = run(last, score_step, jnp.full((8, ROWS), FLOOR_SCORE, F32))
        rows = pl.ds(pl.multiple_of(last * KEYS, KEYS), KEYS)
        st = lax.dot_general(kvb[rows, :HD], qx, NT, preferred_element_type=F32)
        key_places = last * KEYS + lax.broadcasted_iota(jnp.int32, (KEYS, ROWS), 0)
        query_places = place * BLK + lax.rem(lax.broadcasted_iota(jnp.int32, (KEYS, ROWS), 1), BLK)
        st = jnp.where(key_places <= query_places, st, FLOOR_SCORE)
        stb[rows, :] = st
        top = jnp.maximum(top, fold(st, KEYS, jnp.max))
        top = jnp.max(top, axis=0, keepdims=True) * SCALE_LOG2

        def weigh_step(rows, size, state):
            total, weighted = state
            weights = jnp.exp2(stb[rows, :] * SCALE_LOG2 - top)
            dpt = lax.dot_general(kvb[rows, HD:], dx, NT, preferred_element_type=F32)
            dpb[rows, :] = dpt
            stb[rows, :] = weights
            return total + fold(weights, size, jnp.sum), weighted + fold(weights * dpt, size, jnp.sum)

        zero = jnp.zeros((8, ROWS), F32)
        total, weighted = run(last + 1, weigh_step, (zero, zero))
        inverse = 1.0 / jnp.sum(total, axis=0, keepdims=True)
        delta = jnp.sum(weighted, axis=0, keepdims=True) * inverse
        dqt[...] = jnp.zeros((HD, ROWS), F32)

        def grad_step(rows, size, state):
            probs = stb[rows, :] * inverse
            low = probs.astype(BF)
            grads = (probs * (dpb[rows, :] - delta)).astype(BF)
            dv[rows, :] += lax.dot_general(low, dx, NN, preferred_element_type=F32)
            dk[rows, :] += lax.dot_general(grads, qx, NN, preferred_element_type=F32)
            dqt[...] += lax.dot_general(kvb[rows, :HD], grads, TN, preferred_element_type=F32)
            return state

        run(last + 1, grad_step, 0)
        dq = dqt[...].T
        for h in range(4):
            dq_out[x, :, h * HD : (h + 1) * HD] = (dq[h * BLK : (h + 1) * BLK, :] * SCALE).astype(BF)
        return carry

    lax.fori_loop(0, NX, tile, 0)

    def finish(i, carry):
        rows = pl.ds(pl.multiple_of(i * 256, 256), 256)
        dkvb[rows, :HD] = (dk[rows, :] * SCALE).astype(BF)
        dkvb[rows, HD:] = dv[rows, :].astype(BF)
        for j in range(2):
            block = block_at[2 * i + j]
            src = dkvb.at[pl.ds(pl.multiple_of(i * 256 + j * BLK, BLK), BLK), :]
            pltpu.make_async_copy(src, dkv_out.at[block // NZ, lax.rem(block, NZ)], out_sem).start()
        return carry

    lax.fori_loop(0, 16, finish, 0)
    wait_bytes(dkvb, out_sem)


def attention(block_order, qx, dox, kv):
    tokens = BLOCKS * BLK
    return pl.pallas_call(
        attention_kernel,
        name="attention",
        out_shape=(
            jax.ShapeDtypeStruct((NX, BLK, GROUP_COLS), BF),
            jax.ShapeDtypeStruct((NX, NZ, BLK, KV_W), BF),
        ),
        in_specs=[pl.BlockSpec(memory_space=pltpu.SMEM)] + [ANY_SPEC] * 3,
        out_specs=(VMEM_SPEC, ANY_SPEC),
        scratch_shapes=[
            pltpu.VMEM((tokens, KV_W), BF),
            pltpu.VMEM((NX, ROWS, HD), BF),
            pltpu.VMEM((NX, ROWS, HD), BF),
            pltpu.VMEM((tokens, ROWS), F32),
            pltpu.VMEM((tokens, ROWS), F32),
            pltpu.VMEM((tokens, HD), F32),
            pltpu.VMEM((tokens, HD), F32),
            pltpu.VMEM((HD, ROWS), F32),
            pltpu.VMEM((tokens, KV_W), BF),
            pltpu.SMEM((BLOCKS,), jnp.int32),
            DMA,
            DMA,
            DMA,
            DMA,
        ],
        compiler_params=pltpu.CompilerParams(vmem_limit_bytes=ATTENTION_GRANT),
        cost_estimate=pl.CostEstimate(flops=10**10, bytes_accessed=8 * 2**20, transcendentals=10**7),
    )(block_order, qx, dox, kv)


class Ring:
    def __init__(self, count, position, neighbour, own, slots, send_sems, recv_sems):
        self.count, self.position, self.neighbour, self.own = count, position, neighbour, own
        self.slots, self.send_sems, self.recv_sems = slots, send_sems, recv_sems
        self.steps = count // 2
        self.sent = []

    def chains(self, step):
        for way in range(2):
            for part in range(2):
                length = self.steps if way == part else self.steps - 1
                if step >= self.steps - length:
                    yield way, part, step == self.steps - length

    def step(self, step):
        for way, part, first in self.chains(step):
            sign = 1 if way == 0 else -1
            mine = self.own(part, sign * (self.steps - step))
            if first:
                src = mine
            else:
                src = self.slots.at[way, part, step - 1]
                wait_bytes(src, self.recv_sems.at[way, part, step - 1])
                src[...] = (src[...].astype(F32) + mine[...].astype(F32)).astype(BF)
            copy = remote(
                src,
                self.slots.at[way, part, step],
                self.send_sems.at[way, part, step],
                self.recv_sems.at[way, part, step],
                self.neighbour(sign),
            )
            copy.start()
            self.sent.append(copy)

    def result(self, part):
        total = self.own(part, 0)[...].astype(F32)
        for way in range(2):
            slot = self.slots.at[way, part, self.steps - 1]
            wait_bytes(slot, self.recv_sems.at[way, part, self.steps - 1])
            total += slot[...].astype(F32)
        return total.astype(BF)

    def finish(self):
        for copy in self.sent:
            copy.wait_send()


def span(start, size):
    return pl.ds(pl.multiple_of(start, 16), size)


HALF_ROWS = BLK // 2
RINGS = 4
RING_ROWS = BLK // RINGS
DELTAS = (4, 3, -3, 2, -2, 1, -1, 0)


def back_kernel(
    dq, dkv, tok, masks, query_grad, key_out, value_out,
    own, other, z1, home_src, raw, mbuf, tokq, tokt, preall, wa, wb, az, ra, ax, bx, rb, bz, fin, final,
    own_sem, mask_sem, ex_send, ex_recv, z1_send, z1_recv, home_send, home_recv, tok_send, tok_recv, dq_send, dq_recv,
    pre_send, pre_recv, pfw_send, pfw_recv, core_sem,
    az_send, az_recv, ax_send, ax_recv, bx_send, bx_recv, bz_send, bz_recv,
    fin_send, fin_recv, f2_send, f2_recv,
):
    X, Y, Z, C = here()
    head, low = Y // 2, lax.rem(Y, 2)
    unit_core = X // 2
    slot = lax.rem(X, 2)
    same = unit_core == C
    partner = device(X, Y, Z, 1 - C)
    beside = device(X, 2 * head + 1 - low, Z, C)
    seq = low * 2 + C

    def z_next(sign):
        return device(X, Y, around(Z + sign, NZ), C)

    def x_next(sign):
        return device(around(X + sign, NX), Y, Z, C)

    def y_next(by):
        return device(X, around(Y + by, NY), Z, C)

    ways = (1, 3, 2)
    i_mine = X + 4 * lax.rem(Z, 2)
    targets = [
        [(Y, 2 * around(head + which, 2) + lows, 4 * C + Z // 2, lax.rem(Z, 2)) for lows in range(2)]
        for which in range(2)
    ]

    def is_me(place):
        x, y, z, core = place
        return jnp.logical_and(jnp.logical_and(x == X, y == Y), jnp.logical_and(z == Z, core == C))

    is_final = [[is_me(target) for target in pair] for pair in targets]

    signal(partner)
    for xs in range(2):
        for cs in range(NC):
            @pl.when(jnp.logical_not(jnp.logical_and(2 * C + xs == X, C == cs)))
            def _(xs=xs, cs=cs):
                signal(device(2 * C + xs, Y, Z, cs))
    for sign in (1, -1):
        signal(z_next(sign))
        signal(x_next(sign))
    for cs in range(NC):
        signal(device(X, 2 * head + 1 - low, Z, cs))
    for by in ways:
        signal(y_next(by))
    signal(device(around(X + 2, NX), Y, Z, C))
    load_own = pltpu.make_async_copy(dkv.at[pl.ds(C * 2, 2)], own, own_sem)
    load_own.start()
    load_mask = pltpu.make_async_copy(masks, mbuf, mask_sem)
    load_mask.start()
    pl.semaphore_wait(pltpu.get_barrier_semaphore(), 15 - same.astype(jnp.int32))

    exchanges = {}
    for i, delta in enumerate(DELTAS):
        t = around(Z + delta, NZ)
        copy = remote(dkv.at[pl.ds((1 - C) * 2, 2), t], other.at[:, t], ex_send.at[i], ex_recv.at[i], partner)
        copy.start()
        exchanges[delta] = copy
    for xs in range(NX):
        cols = pl.ds(pl.multiple_of((slot * 8 + C * 4) * HD, GROUP_COLS), GROUP_COLS)
        is_self = jnp.logical_and(same, X == xs)
        send_or_copy(
            is_self, dq.at[xs], query_grad.at[0, :, cols], dq_send.at[xs], dq_recv, device(xs, Y, Z, unit_core)
        )
    for quarter in range(4):
        is_self = seq == quarter
        send_or_copy(
            is_self,
            tok.at[0, :, pl.ds(quarter * QUARTER, QUARTER)],
            tokq.at[seq],
            tok_send.at[quarter],
            tok_recv,
            device(X, 2 * head + quarter // 2, Z, quarter % 2),
        )

    load_own.wait()
    ready = set()

    def prepare(delta):
        if delta in ready:
            return
        ready.add(delta)
        t = around(Z + delta, NZ)
        exchanges[delta].wait_recv()
        for part in range(2):
            own[part, t] = (own[part, t].astype(F32) + other[part, t].astype(F32)).astype(BF)

    def own_part(i):
        def get(part, delta):
            prepare(4 if delta == -4 else delta)
            return own.at[part, around(Z + delta, NZ), pl.ds(i * RING_ROWS, RING_ROWS), :]

        return get

    rings = [Ring(NZ, Z, z_next, own_part(i), z1.at[i], z1_send.at[i], z1_recv.at[i]) for i in range(RINGS)]
    for step in range(NZ // 2):
        for ring in rings:
            ring.step(step)
    for half in range(2):
        rows = pl.ds(half * HALF_ROWS, HALF_ROWS)
        for i in range(half * RINGS // 2, (half + 1) * RINGS // 2):
            for part in range(2):
                home_src[part, i * RING_ROWS : (i + 1) * RING_ROWS, :] = rings[i].result(part)
        for part in range(2):
            xs = 2 * C + part
            is_self = jnp.logical_and(same, X == xs)
            send_or_copy(
                is_self,
                home_src.at[part, rows, :],
                raw.at[slot, rows, :],
                home_send.at[half, part],
                home_recv.at[half],
                device(xs, Y, Z, unit_core),
            )

    load_mask.wait()
    sends = []
    y_targets = (beside, y_next(around(2 * low - 1, NY)), y_next(2))
    y_places = ((head, 1 - low), (1 - head, 1 - low), (1 - head, low))

    def my_rows(half):
        return span(seq * BLK + half * HALF_ROWS, HALF_ROWS)

    for half in range(2):
        rows = pl.ds(half * HALF_ROWS, HALF_ROWS)
        wait_bytes(raw.at[:, rows, :], home_recv.at[half])
        for j in range(2):
            for what in range(2):
                mask = mbuf[what, 0, rows, j * HD : (j + 1) * HD] != 0
                piece = raw[j, rows, what * HD : (what + 1) * HD]
                first = (2 * j + what) * HD
                preall[head, my_rows(half), first : first + HD] = jnp.where(mask, piece, jnp.zeros_like(piece))
        mine = preall.at[head, my_rows(half), :]
        sends.append(remote(mine, mine, core_sem.at[half, 0], core_sem.at[half, 1], partner))
        sends[-1].start()
        for i in range(2):
            sends.append(remote(mine, mine, pre_send.at[half, i], pre_recv.at[half, i], y_targets[i]))
            sends[-1].start()
    for half in range(2):
        mine = preall.at[head, my_rows(half), :]
        sends.append(remote(mine, mine, pre_send.at[half, 2], pre_recv.at[half, 2], y_targets[2]))
        sends[-1].start()

    wait_bytes(tokq, tok_recv)
    for s in range(4):
        tokt[:, :, :, s * BLK : (s + 1) * BLK] = tokq[s].T.reshape(NZ, NX, 32, BLK)

    forwards = []

    def pass_on(i):
        place, lows = y_places[i]
        for half in range(2):
            piece = preall.at[place, span((lows * 2 + C) * BLK + half * HALF_ROWS, HALF_ROWS), :]
            wait_bytes(piece, pre_recv.at[half, i])
            copy = remote(piece, piece, pfw_send.at[half, i], pfw_recv.at[half, i], partner)
            copy.start()
            forwards.append(copy)
        return forwards[-2:]

    passed_on = [pass_on(0)]
    for half in range(2):
        sends[half * 3].wait_recv()
    for copy in passed_on[0]:
        copy.wait_recv()

    made = set()

    def product(path, which, delta):
        if (path, which, delta) in made:
            return
        made.add((path, which, delta))
        cols = slice(path * KV_W, (path + 1) * KV_W)
        if path == 0:
            t = around(Z + delta, NZ)
            rows = tokt[t].reshape(128, 4 * BLK)
        else:
            t = around(X + delta, NX)
            rows = tokt[:, t].reshape(256, 4 * BLK)
        value = jnp.dot(rows, preall[around(head + which, 2), :, cols], preferred_element_type=F32).astype(BF)
        if path == 0:
            wa[which, t] = value.reshape(NX, 32, KV_W)
        else:
            wb[which, :, t] = value.reshape(NZ, 32, KV_W)

    def a_own(which):
        def get(part, delta):
            delta = 4 if delta == -4 else delta
            product(0, which, delta)
            return wa.at[which, around(Z + delta, NZ), pl.ds(part * 2, 2)]

        return get

    def b_own(which):
        def get(part, delta):
            delta = 2 if delta == -2 else delta
            product(1, which, delta)
            return wb.at[which, pl.ds(part * 4, 4), around(X + delta, NX)]

        return get

    a1 = [Ring(NZ, Z, z_next, a_own(s), az.at[s], az_send.at[s], az_recv.at[s]) for s in range(2)]
    b1 = [Ring(NX, X, x_next, b_own(s), bx.at[s], bx_send.at[s], bx_recv.at[s]) for s in range(2)]

    directs = []

    def direct(source, slots, send_sems, recv_sems, count, position, neighbour):
        deltas = sorted([d for d in range(1 - count // 2, count // 2 + 1) if d], key=lambda d: -abs(d))
        for delta in deltas:
            i = delta % count - 1
            src = source.at[around(position + delta, count)]
            copy = remote(src, slots.at[i], send_sems.at[i], recv_sems.at[i], neighbour(delta))
            copy.start()
            directs.append(copy)

    def collect(source, slots, recv_sems, count, position):
        total = source[position].astype(F32)
        for i in range(count - 1):
            wait_bytes(slots.at[i], recv_sems.at[i])
            total += slots[i].astype(F32)
        return total.astype(BF)

    def turn_a(which):
        for part in range(2):
            ra[which, part * 2 : (part + 1) * 2] = a1[which].result(part)
        direct(ra.at[which], ax.at[which], ax_send.at[which], ax_recv.at[which], NX, X, x_next)

    def turn_b(which):
        for part in range(2):
            rb[which, part * 4 : (part + 1) * 4] = b1[which].result(part)
        direct(rb.at[which], bz.at[which], bz_send.at[which], bz_recv.at[which], NZ, Z, z_next)

    def deliver(which):
        fin[which, :, KV_W:] = collect(rb.at[which], bz.at[which], bz_recv.at[which], NZ, Z)
        fin[which, :, :KV_W] = collect(ra.at[which], ax.at[which], ax_recv.at[which], NX, X)
        dst = final.at[span(i_mine * 32, 32), :]
        for lows in range(2):
            send_or_copy(
                is_final[which][lows],
                fin.at[which],
                dst,
                fin_send.at[which, lows],
                fin_recv,
                device(*targets[which][lows]),
            )

    a1[0].step(0)
    passed_on.append(pass_on(1))
    passed_on.append(pass_on(2))
    b1[0].step(0)
    a1[0].step(1)
    for copy in passed_on[1] + passed_on[2]:
        copy.wait_recv()
    a1[1].step(0)
    b1[1].step(0)
    a1[0].step(2)
    b1[0].step(1)
    a1[1].step(1)
    a1[0].step(3)
    a1[1].step(2)
    b1[1].step(1)
    turn_b(0)
    turn_a(0)
    a1[1].step(3)
    turn_b(1)
    turn_a(1)
    deliver(0)
    deliver(1)

    mine = final.at[span(C * BLK, BLK), :]
    wait_bytes(mine, fin_recv)
    to_partner = remote(mine, mine, f2_send, f2_recv, partner)
    to_partner.start()
    to_partner.wait_recv()
    for j in range(2):
        for what, out in ((0, key_out), (1, value_out)):
            first = (2 * j + what) * HD
            out[:, j * HD : (j + 1) * HD] = final[:, first : first + HD].astype(F32) * 0.25

    wait_bytes(query_grad, dq_recv)
    for copy in exchanges.values():
        copy.wait_send()
    for xs in range(NX):
        wait_sent(jnp.logical_and(same, X == xs), dq.at[xs], dq_send.at[xs])
    for quarter in range(4):
        wait_sent(seq == quarter, tokq.at[0], tok_send.at[quarter])
    for half in range(2):
        for part in range(2):
            wait_sent(
                jnp.logical_and(same, X == 2 * C + part),
                raw.at[part, pl.ds(half * HALF_ROWS, HALF_ROWS), :],
                home_send.at[half, part],
            )
    for copy in sends + forwards + [to_partner]:
        copy.wait_send()
    for ring in rings + a1 + b1:
        ring.finish()
    for copy in directs:
        copy.wait_send()
    for which in range(2):
        for lows in range(2):
            wait_sent(is_final[which][lows], fin.at[which], fin_send.at[which, lows])


def back(dq, dkv, tokens, clip_masks):
    wide = 2 * KV_W
    return pl.pallas_call(
        back_kernel,
        name="back",
        out_shape=(
            jax.ShapeDtypeStruct((1, BLK, 2048), BF),
            jax.ShapeDtypeStruct((256, KV_W), F32),
            jax.ShapeDtypeStruct((256, KV_W), F32),
        ),
        in_specs=[ANY_SPEC] * 4,
        out_specs=(ANY_SPEC, VMEM_SPEC, VMEM_SPEC),
        scratch_shapes=[
            pltpu.VMEM((2, NZ, BLK, KV_W), BF),
            pltpu.VMEM((2, NZ, BLK, KV_W), BF),
            pltpu.VMEM((RINGS, 2, 2, 4, RING_ROWS, KV_W), BF),
            pltpu.VMEM((2, BLK, KV_W), BF),
            pltpu.VMEM((2, BLK, KV_W), BF),
            pltpu.VMEM((2, 1, BLK, KV_W), jnp.int32),
            pltpu.VMEM((4, BLK, QUARTER), BF),
            pltpu.VMEM((NZ, NX, 32, 4 * BLK), BF),
            pltpu.VMEM((2, 4 * BLK, wide), BF),
            pltpu.VMEM((2, NZ, NX, 32, KV_W), BF),
            pltpu.VMEM((2, NZ, NX, 32, KV_W), BF),
            pltpu.VMEM((2, 2, 2, 4, 2, 32, KV_W), BF),
            pltpu.VMEM((2, NX, 32, KV_W), BF),
            pltpu.VMEM((2, NX - 1, 32, KV_W), BF),
            pltpu.VMEM((2, 2, 2, 2, 4, 32, KV_W), BF),
            pltpu.VMEM((2, NZ, 32, KV_W), BF),
            pltpu.VMEM((2, NZ - 1, 32, KV_W), BF),
            pltpu.VMEM((2, 32, wide), BF),
            pltpu.VMEM((256, wide), BF),
            DMA,
            DMA,
            DMA((8,)),
            DMA((8,)),
            DMA((RINGS, 2, 2, 4)),
            DMA((RINGS, 2, 2, 4)),
            DMA((2, 2)),
            DMA((2,)),
            DMA((4,)),
            DMA,
            DMA((4,)),
            DMA,
            DMA((2, 3)),
            DMA((2, 3)),
            DMA((2, 3)),
            DMA((2, 3)),
            DMA((2, 2)),
            DMA((2, 2, 2, 4)),
            DMA((2, 2, 2, 4)),
            DMA((2, NX - 1)),
            DMA((2, NX - 1)),
            DMA((2, 2, 2, 2)),
            DMA((2, 2, 2, 2)),
            DMA((2, NZ - 1)),
            DMA((2, NZ - 1)),
            DMA((2, 2)),
            DMA,
            DMA,
            DMA,
        ],
        compiler_params=pltpu.CompilerParams(
            collective_id=1, has_side_effects=True, vmem_limit_bytes=BACK_GRANT
        ),
        cost_estimate=pl.CostEstimate(flops=10**9, bytes_accessed=16 * 2**20, transcendentals=0),
    )(dq, dkv, tokens, clip_masks)


def on_device(
    tokens, queries, out_grad, key_weight, value_weight, noise_codes, clip_masks, block_order
):
    qx, dox, kv = front(tokens, queries, out_grad, key_weight, value_weight, noise_codes)
    dq, dkv = attention(block_order, qx, dox, kv)
    return back(dq, dkv, tokens, clip_masks)


def solution(mesh):
    placed = (
        P("dp", "ctx", "head"),
        P("dp", "ctx", "head"),
        P("dp", "ctx", "head"),
        P(None, "head"),
        P(None, "head"),
        P(None, "dp", "ctx", "head"),
        P(None, "dp", "ctx", "head"),
        P(),
    )
    return jax.shard_map(
        on_device,
        mesh=mesh,
        in_specs=placed,
        out_specs=(P("dp", "ctx", "head"), P("ctx", "head"), P("ctx", "head")),
        check_vma=False,
    )
```
